128 devices in a mesh: replica: 8 (over z_lo, x), mp: 16 (over z_hi, y, core).
Axes of the slice: x: 4, y: 4, z: 4 (z_hi: 2, z_lo: 2; z = z_hi * 2 + z_lo), core: 2. Of those that a mesh axis runs over, the one named last changes fastest.
Arguments:
- indices: int32 [256, 8, 16384], P('mp', None, 'replica'), may hold values from 0 to 511
- lengths: int32 [256, 16384], P('mp', 'replica'), may hold values from 1 to 8
- tables: bfloat16 [256, 512, 256], P('mp'), may hold values from -0.59765625 to 0.59765625
- proj: bfloat16 [256, 16], replicated, may hold values from -0.375 to 0.375
- w_hidden: bfloat16 [4096, 64], replicated, may hold values from -0.75 to 0.75
- w_out: bfloat16 [4096], replicated, may hold values from -0.09375 to 0.09375
- d_logit: float32 [16384], P(('replica', 'mp')), may hold values from -0.375 to 0.375
Outputs:
- logits: float32 [16384], P(('replica', 'mp'))
- table_grad: float32 [256, 512, 256], P('mp')
- hidden_grad: float32 [4096, 64], P(('replica', 'mp'))
- out_grad: float32 [4096], P(('replica', 'mp'))
- proj_grad: float32 [256, 16], P(('replica', 'mp'))
The draws below stay inside these ranges and needn't reach their ends.
All inputs are finite; a program needn't handle non-finite values.
Results may differ from the reference program's by a relative error of at most 0.035.
Values may be sent and summed in bfloat16 or wider, within the bound.
A program may use at most 192 MiB of HBM per device.

```python
import math
import jax
import jax.numpy as jnp
import numpy as np
from jax import lax

F = 256
E = 256
HID = 4096
K1 = 8
K2 = 8
FEAT = 64
BAG = 8
R = 512
B_DEV = 128
BATCH = 16384
N_REPLICA = 8
N_MP = 16


def plant(values, key, low, high):
    longest = values.shape.index(max(values.shape))
    spots = []
    for shift in (0, 1):
        where = [jax.random.randint(jax.random.fold_in(key, axis), (), 0, length) for axis, length in enumerate(values.shape)]
        where[longest] = (where[longest] + shift) % values.shape[longest]
        spots.append(tuple(where))
    return values.at[spots[0]].set(low).at[spots[1]].set(high)


def steps_of(own_key, extent, shards, low, high):
    def one(position, parts):
        heights = jax.random.uniform(jax.random.fold_in(jax.random.fold_in(own_key, 6), position), (parts,), jnp.float32, low / len(shards), high / len(shards))
        return jnp.repeat(jnp.exp(heights), extent[position] // parts).reshape((-1,) + (1,) * (len(extent) - position - 1))

    loudness = one(*shards[0])
    for cut in shards[1:]:
        loudness = loudness * one(*cut)
    return loudness


def cumulative_ranks(count, lean):
    loads = [(1 << 20) // math.isqrt(rank ** lean) + 1 for rank in range(1, count + 1)]
    scale = 1 + sum(loads) // (1 << 30)
    return np.cumsum(np.array([max(1, weight // scale) for weight in loads]))


def ranked(stream_key, dims, number_of, skew):
    grid = cumulative_ranks(number_of, skew)
    lot = jax.random.randint(jax.random.fold_in(stream_key, 1), dims, 0, int(grid[number_of - 1]))
    rank = jnp.searchsorted(jnp.asarray(grid, jnp.int32), lot, side="right")
    return jax.random.permutation(jax.random.fold_in(stream_key, 2), number_of)[rank].astype(jnp.int32)


def noise(own_key, extent, scale, bound, cuts=(), held_as=jnp.bfloat16):
    factor_of = steps_of(own_key, extent, cuts, -0.22, 0.18) if cuts else 1.0
    result = jax.random.normal(own_key, extent, jnp.float32) * scale * factor_of
    return jnp.minimum(jnp.maximum(result, -bound), bound).astype(held_as)


def setup_inputs(seed: int = 0) -> dict:
    streams_of = jax.random.split(jax.random.key(seed), 8)
    return {
        "indices": plant(ranked(streams_of[0], (F, BAG, BATCH), R, 2), jax.random.fold_in(streams_of[0], 3), 0, R - 1).astype(jnp.int32),
        "lengths": plant(jax.random.randint(streams_of[1], (F, BATCH), 1, BAG + 1), jax.random.fold_in(streams_of[1], 1), 1, BAG).astype(jnp.int32),
        "tables": noise(streams_of[2], (F, R, E), 0.1, 0.59765625, ((0, 16),)),
        "proj": noise(streams_of[3], (F, K1 + K2), F ** -0.5, 0.375),
        "w_hidden": noise(streams_of[4], (HID, FEAT), FEAT ** -0.5, 0.75),
        "w_out": noise(streams_of[5], (HID,), HID ** -0.5, 0.09375),
        "d_logit": noise(streams_of[6], (BATCH,), 0.0625, 0.375, ((0, 128),), jnp.float32),
    }


def pick_rows(table_one, index_one):
    return table_one[index_one]


def add_rows(grad_one, index_one, term_one):
    return grad_one.at[index_one.reshape(-1)].add(term_one.reshape(-1, term_one.shape[-1]))


def reference(indices, lengths, tables, proj, w_hidden, w_out, d_logit):
    highest = lax.Precision.HIGHEST
    proj_wide = proj.astype(jnp.float32)
    slot_ids = jnp.arange(BAG, dtype=jnp.int32)

    def one_block(state_in, block_id):
        out_acc, hid_acc, proj_acc, group_sum = state_in
        first_row = (block_id * B_DEV).astype(jnp.int32)
        row_index = lax.dynamic_slice_in_dim(indices, first_row, B_DEV, 2)
        bag_lengths = lax.dynamic_slice_in_dim(lengths, first_row, B_DEV, 1)
        cotangent = lax.dynamic_slice_in_dim(d_logit, first_row, B_DEV, 0)
        live_slots = (slot_ids[None, :, None] < bag_lengths[:, None, :]).astype(jnp.float32)
        looked_up = jax.vmap(pick_rows)(tables, row_index).astype(jnp.float32)
        pooled = jnp.sum(looked_up * live_slots[..., None], axis=1).astype(jnp.bfloat16)
        pooled_wide = pooled.astype(jnp.float32)
        factors = jnp.einsum("fk,fne->kne", proj_wide, pooled_wide, precision=highest)
        inter = jnp.einsum("ine,jne->ijn", factors[:K1], factors[K1:], precision=highest)
        features = inter.reshape(K1 * K2, B_DEV).astype(jnp.bfloat16)
        pre_act = jnp.dot(w_hidden, features, preferred_element_type=jnp.float32)
        hidden = jax.nn.silu(pre_act).astype(jnp.bfloat16)
        logit_block = jnp.dot(w_out, hidden, preferred_element_type=jnp.float32)
        out_acc = out_acc + jnp.dot(hidden.astype(jnp.float32), cotangent, precision=highest)
        sigmoid_v = jax.nn.sigmoid(pre_act)
        d_hidden = (w_out.astype(jnp.float32)[:, None] * cotangent[None, :] * sigmoid_v * (1.0 + pre_act * (1.0 - sigmoid_v))).astype(jnp.bfloat16)
        hid_acc = hid_acc + lax.dot_general(d_hidden, features, (((1,), (1,)), ((), ())), preferred_element_type=jnp.float32)
        d_inter = lax.dot_general(w_hidden, d_hidden, (((0,), (0,)), ((), ())), preferred_element_type=jnp.float32).reshape(K1, K2, B_DEV)
        d_left = jnp.einsum("ijn,jne->ine", d_inter, factors[K1:], precision=highest)
        d_right = jnp.einsum("ijn,ine->jne", d_inter, factors[:K1], precision=highest)
        d_factors = jnp.concatenate([d_left, d_right], axis=0).astype(jnp.bfloat16)
        d_wide = d_factors.astype(jnp.float32)
        proj_acc = proj_acc + jnp.einsum("fne,kne->fk", pooled_wide, d_wide, precision=highest)
        d_pooled = jnp.einsum("fk,kne->fne", proj_wide, d_wide, precision=highest).astype(jnp.bfloat16)
        term_all = live_slots[..., None] * d_pooled.astype(jnp.float32)[:, None, :, :]
        group_sum = jax.vmap(add_rows)(group_sum, row_index, term_all)
        return (out_acc, hid_acc, proj_acc, group_sum), logit_block

    def one_group(state_in, group_id):
        out_acc, hid_acc, proj_acc, table_total = state_in
        group_zero = jnp.zeros((F, R, E), jnp.float32)
        block_ids = group_id * N_MP + jnp.arange(N_MP, dtype=jnp.int32)
        (out_acc, hid_acc, proj_acc, group_sum), logit_rows = lax.scan(one_block, (out_acc, hid_acc, proj_acc, group_zero), block_ids)
        rounded = lax.optimization_barrier(group_sum.astype(jnp.bfloat16))
        table_total = table_total + rounded.astype(jnp.float32)
        return (out_acc, hid_acc, proj_acc, table_total), logit_rows

    start_state = (jnp.zeros((HID,), jnp.float32), jnp.zeros((HID, K1 * K2), jnp.float32), jnp.zeros((F, K1 + K2), jnp.float32), jnp.zeros((F, R, E), jnp.float32))
    (out_grad, hidden_grad, proj_grad, table_grad), logit_all = lax.scan(one_group, start_state, jnp.arange(N_REPLICA, dtype=jnp.int32))
    logits = logit_all.reshape(BATCH)
    return (logits, table_grad, hidden_grad, out_grad, proj_grad)
```

```python
import functools

import jax
import jax.numpy as jnp
from jax import lax
from jax.experimental import pallas as pl
from jax.experimental.pallas import tpu as pltpu
from jax.sharding import PartitionSpec as P

MESH = pl.DeviceIdType.MESH
K1 = 8
K2 = 8
KK = K1 + K2
SUB = 16
HI = 64
BITS = 4
VMEM = 60 * 1024 * 1024
F32 = jnp.float32
BF16 = jnp.bfloat16


def peers():
    me = lax.axis_index("mp")
    core = lax.rem(me, 2)
    y = lax.rem(lax.div(me, 2), 4)
    z = lax.div(me, 8)
    other = me + 1 - 2 * core
    right = z * 8 + lax.rem(y + 1, 4) * 2 + core
    left = z * 8 + lax.rem(y + 3, 4) * 2 + core
    across = (1 - z) * 8 + y * 2 + core
    return me, core, y, z, other, right, left, across


def barrier(devices):
    sem = pltpu.get_barrier_semaphore()
    for d in devices:
        pl.semaphore_signal(sem, inc=1, device_id={"mp": d}, device_id_type=MESH)
    pl.semaphore_wait(sem, len(devices))


def remote(src, dst, send, recv, device):
    return pltpu.make_async_remote_copy(
        src_ref=src, dst_ref=dst, send_sem=send, recv_sem=recv, device_id={"mp": device}, device_id_type=MESH
    )


def digits(words):
    return jnp.concatenate(
        [(lax.shift_right_logical(words, BITS * d) & 15).astype(F32).astype(BF16) for d in range(8)], axis=0
    )


def fwd_kernel(
    idx, lens, tab_t, kron, words_out, pooled_out, fac_out,
    sbuf, rcore, rhalf, rfull, rz, wbuf, pbuf,
    core_s, core_r, half_s, half_r, full_s, full_r, z_s, z_r, w_sem, p_sem,
):
    me, core, y, z, other, right, left, across = peers()
    barrier((other, right, left, across))
    n_f = idx.shape[0]
    emb = tab_t.shape[1]

    def zo_of(t):
        return jnp.where(t < 2, t, jnp.where(t < 6, lax.div(t - 2, 2), t - 6))

    def chunk_of(t):
        dy = jnp.where(t < 2, 2, jnp.where(t < 6, 1 + 2 * lax.rem(t, 2), 0))
        zo = zo_of(t)
        zt = lax.rem(z + 1 + zo, 2)
        return zt * 4 + lax.rem(y + dy, 4)

    def p_copy(t):
        slot = lax.rem(t, 2)
        return pltpu.make_async_copy(pbuf.at[slot], pooled_out.at[chunk_of(t)], p_sem.at[slot])

    def w_copy(t):
        return pltpu.make_async_copy(wbuf.at[t], words_out.at[chunk_of(t)], w_sem.at[t])

    def core_copy(t):
        return remote(sbuf.at[t, 1 - core], rcore.at[t], core_s.at[t], core_r.at[t], other)

    def half_copy(t, zo, d):
        return remote(
            sbuf.at[t, core, pl.ds(d * K1, K1)], rhalf.at[zo, d], half_s.at[zo, d], half_r.at[zo, d], (right, left)[d]
        )

    def full_copy(t, zo, d):
        return remote(sbuf.at[t, core], rfull.at[zo, d], full_s.at[zo, d], full_r.at[zo, d], (right, left)[d])

    def z_copy():
        return remote(sbuf.at[6, core], rz, z_s, z_r, across)

    def compute(t):
        q = chunk_of(t)
        slot = lax.rem(t, 2)
        where = pl.ds(pl.multiple_of(q * 256, 256), 256)

        @pl.when(t >= 2)
        def _():
            p_copy(t - 2).wait()

        def field(f, carry):
            ids = idx[f, :, where]
            live = lens[pl.ds(f, 1), where]
            lane_slot = lax.broadcasted_iota(jnp.int32, ids.shape, 0)
            hi = ids & (HI - 1)
            val = jnp.where(lane_slot < live, jnp.left_shift(1, BITS * lax.shift_right_logical(ids, 6)), 0)
            rows = lax.broadcasted_iota(jnp.int32, (HI, 256), 0)
            words = jnp.zeros((HI, 256), jnp.int32)
            for s in range(8):
                words = words + jnp.where(hi[s : s + 1, :] == rows, val[s : s + 1, :], 0)
            wbuf[t, f] = words
            pooled = jnp.dot(tab_t[f], digits(words), preferred_element_type=F32)
            pbuf[slot, f] = pooled.astype(BF16)
            return carry

        lax.fori_loop(0, n_f, field, 0)
        p_copy(t).start()
        w_copy(t).start()

        def block(eb, carry):
            rows = pl.ds(pl.multiple_of(eb * SUB, SUB), SUB)
            x = pbuf[slot, :, rows, :].reshape(n_f * SUB, 256)
            part = jnp.dot(kron[...], x, preferred_element_type=F32).astype(BF16).reshape(KK, SUB, 256)
            sbuf[t, 0, :, rows, :] = part[:, :, :128]
            sbuf[t, 1, :, rows, :] = part[:, :, 128:]
            return carry

        lax.fori_loop(0, emb // SUB, block, 0)
        core_copy(t).start()

    def add(t, pairs, out=None):
        def one(k, carry, refs):
            total = sbuf[t, core, k].astype(F32)
            for r, first in refs:
                total = total + r[k - first].astype(F32)
            if out is None:
                sbuf[t, core, k] = total.astype(BF16)
            else:
                out[k] = total
            return carry

        lax.fori_loop(0, K1, functools.partial(one, refs=[(r, a) for r, a, b in pairs if a < K1]), 0)
        lax.fori_loop(K1, KK, functools.partial(one, refs=[(r, a) for r, a, b in pairs if b > K1]), 0)

    def pass_on(t):
        core_copy(t).wait_recv()
        mine = (rcore.at[t], 0, KK)

        @pl.when(t < 2)
        def _():
            add(t, [mine])
            half_copy(t, zo_of(t), 0).start()
            half_copy(t, zo_of(t), 1).start()

        for d in range(2):

            @pl.when(jnp.logical_or(t == 2 + d, t == 4 + d))
            def _():
                zo = zo_of(t)
                half_copy(zo, zo, d).wait_recv()
                add(t, [mine, (rhalf.at[zo, d], d * K1, d * K1 + K1)])
                full_copy(t, zo, d).start()

        @pl.when(t == 6)
        def _():
            for d in range(2):
                full_copy(2 + d, 0, d).wait_recv()
            add(t, [mine, (rfull.at[0, 0], 0, KK), (rfull.at[0, 1], 0, KK)])
            z_copy().start()

    def step(t, carry):
        compute(t)

        @pl.when(t >= 1)
        def _():
            pass_on(t - 1)

        return carry

    lax.fori_loop(0, 8, step, 0)
    core_copy(7).wait_recv()
    for d in range(2):
        full_copy(4 + d, 1, d).wait_recv()
    z_copy().wait_recv()
    add(
        7, [(rcore.at[7], 0, KK), (rfull.at[1, 0], 0, KK), (rfull.at[1, 1], 0, KK), (rz, 0, KK)], fac_out
    )

    for t in range(8):
        core_copy(t).wait_send()
        w_copy(t).wait()
    for zo in range(2):
        for d in range(2):
            half_copy(zo, zo, d).wait_send()
            full_copy(2 + 2 * zo + d, zo, d).wait_send()
    z_copy().wait_send()
    p_copy(6).wait()
    p_copy(7).wait()


def forward(indices, lengths, tab_t, kron):
    n_f, emb, _ = tab_t.shape
    dma = pltpu.SemaphoreType.DMA
    vmem = pl.BlockSpec(memory_space=pltpu.VMEM)
    hbm = pl.BlockSpec(memory_space=pl.ANY)
    return pl.pallas_call(
        fwd_kernel,
        out_shape=(
            jax.ShapeDtypeStruct((8, n_f, HI, 256), jnp.int32),
            jax.ShapeDtypeStruct((8, n_f, emb, 256), BF16),
            jax.ShapeDtypeStruct((KK, emb, 128), F32),
        ),
        in_specs=[vmem] * 4,
        out_specs=(hbm, hbm, vmem),
        scratch_shapes=[
            pltpu.VMEM((8, 2, KK, emb, 128), BF16),
            pltpu.VMEM((8, KK, emb, 128), BF16),
            pltpu.VMEM((2, 2, K1, emb, 128), BF16),
            pltpu.VMEM((2, 2, KK, emb, 128), BF16),
            pltpu.VMEM((KK, emb, 128), BF16),
            pltpu.VMEM((8, n_f, HI, 256), jnp.int32),
            pltpu.VMEM((2, n_f, emb, 256), BF16),
            dma((8,)), dma((8,)), dma((2, 2)), dma((2, 2)), dma((2, 2)), dma((2, 2)), dma, dma, dma((8,)), dma((2,)),
        ],
        compiler_params=pltpu.CompilerParams(collective_id=0, has_side_effects=True, vmem_limit_bytes=VMEM),
        cost_estimate=pl.CostEstimate(flops=15 * 10**9, bytes_accessed=40 * 10**6, transcendentals=0),
    )(indices, lengths, tab_t, kron)


def nt(a, b):
    return lax.dot_general(a, b, (((1,), (1,)), ((), ())), preferred_element_type=F32)


def dense_kernel(fac, wh, wh_t, wo_col, wo_row, dl, logits, outp, hidp, dfac, inter):
    hid, _ = wh.shape
    emb = fac.shape[1]
    step = 512

    def left(i, carry):
        a = fac[i]
        for j in range(K2):
            inter[pl.ds(i * K2 + j, 1), :] = jnp.sum(a * fac[K1 + j], axis=0, keepdims=True)
        return carry

    lax.fori_loop(0, K1, left, 0)
    feat = inter[...].astype(BF16)
    row = dl[...]
    d0 = row.astype(BF16)
    r1 = row - d0.astype(F32)
    d1 = r1.astype(BF16)
    d2 = (r1 - d1.astype(F32)).astype(BF16)
    sub = lax.broadcasted_iota(jnp.int32, (8, row.shape[1]), 0)
    d_rows = jnp.where(
        sub == 0, d0.astype(F32), jnp.where(sub == 1, d1.astype(F32), jnp.where(sub == 2, d2.astype(F32), 0.0))
    ).astype(BF16)
    wo8 = wo_row[...]

    def top(c, carry):
        logit_acc, d_inter = carry
        at = pl.ds(pl.multiple_of(c * step, step), step)
        v = jnp.dot(wh[at, :], feat, preferred_element_type=F32)
        s = jax.nn.sigmoid(v)
        hidden = (v * s).astype(BF16)
        logit_acc = logit_acc + jnp.dot(wo_row[:, at], hidden, preferred_element_type=F32)
        outp[:, at] = nt(d_rows, hidden)
        d_hidden = (wo_col[at, :].astype(F32) * row * s * (1.0 + v * (1.0 - s))).astype(BF16)
        hidp[at, :] = nt(d_hidden, feat)
        d_inter = d_inter + jnp.dot(wh_t[:, at], d_hidden, preferred_element_type=F32)
        return logit_acc, d_inter

    del wo8
    n = row.shape[1]
    logit_acc, d_inter = lax.fori_loop(
        0, hid // step, top, (jnp.zeros((8, n), F32), jnp.zeros((K1 * K2, n), F32))
    )
    logits[...] = logit_acc[0:1]
    inter[...] = d_inter

    def back(eb, carry):
        rows = pl.ds(pl.multiple_of(eb * SUB, SUB), SUB)
        right = [fac[K1 + j, rows, :] for j in range(K2)]
        d_right = [jnp.zeros((SUB, n), F32) for _ in range(K2)]
        for i in range(K1):
            a = fac[i, rows, :]
            d_left = jnp.zeros((SUB, n), F32)
            for j in range(K2):
                g = inter[pl.ds(i * K2 + j, 1), :]
                d_left = d_left + g * right[j]
                d_right[j] = d_right[j] + g * a
            dfac[i, rows, :] = d_left.astype(BF16)
        for j in range(K2):
            dfac[K1 + j, rows, :] = d_right[j].astype(BF16)
        return carry

    lax.fori_loop(0, emb // SUB, back, 0)


def dense(fac, w_hidden, w_out, d_logit):
    hid, feat = w_hidden.shape
    n = d_logit.shape[0]
    wo_row = jnp.broadcast_to(w_out[None, :], (8, hid))
    return pl.pallas_call(
        dense_kernel,
        out_shape=(
            jax.ShapeDtypeStruct((1, n), F32),
            jax.ShapeDtypeStruct((8, hid), F32),
            jax.ShapeDtypeStruct((hid, feat), F32),
            jax.ShapeDtypeStruct(fac.shape, BF16),
        ),
        scratch_shapes=[pltpu.VMEM((feat, n), F32)],
        compiler_params=pltpu.CompilerParams(vmem_limit_bytes=VMEM),
        cost_estimate=pl.CostEstimate(flops=10**9, bytes_accessed=10**7, transcendentals=10**6),
    )(fac, w_hidden, w_hidden.T, w_out[:, None], wo_row, d_logit[None, :])


def bwd_kernel(
    dfac, words, pooled, kron_t, tg_out, pg_out,
    gbuf, acc, dpool, wbuf, pbuf,
    own_sem, w_sem, p_sem, core_s, core_r, ici_s, ici_r, half_s, half_r,
):
    me, core, y, z, other, right, left, across = peers()
    barrier((other, right, left, across))
    n_f = wbuf.shape[1]
    emb = dfac.shape[1]
    places = ((0, 0), (0, 3), (0, 1), (1, 0), (1, 3), (1, 1), (0, 2), (1, 2))

    def chip(n):
        dz, dy = places[n]
        return lax.rem(z + dz, 2) * 4 + lax.rem(y + dy, 4)

    def block(n):
        return chip(n) * 2 + core

    def to_core(n):
        return remote(gbuf.at[block(n)], gbuf.at[block(n)], core_s.at[n], core_r.at[n], other)

    def from_core(n):
        j = chip(n) * 2 + 1 - core
        return remote(gbuf.at[j], gbuf.at[j], core_s.at[n], core_r.at[n], other)

    def whole(n, m, device):
        j = block(n)
        return remote(gbuf.at[j], gbuf.at[j], ici_s.at[m], ici_r.at[m], device)

    def arrived(m):
        j = block(m)
        remote(gbuf.at[j], gbuf.at[j], ici_s.at[m], ici_r.at[m], right).wait_recv()

    def half(n, m, d):
        j = block(n)
        part = pl.ds(d * K1, K1)
        i = (m - 6, d)
        return remote(gbuf.at[j, part], gbuf.at[j, part], half_s.at[i], half_r.at[i], (right, left)[d])

    def half_arrived(m, d):
        j = block(m)
        part = pl.ds(d * K1, K1)
        i = (m - 6, d)
        remote(gbuf.at[j, part], gbuf.at[j, part], half_s.at[i], half_r.at[i], right).wait_recv()

    def w_copy(n):
        return pltpu.make_async_copy(words.at[chip(n)], wbuf.at[n % 2], w_sem.at[n % 2])

    def p_copy(n):
        return pltpu.make_async_copy(pooled.at[chip(n)], pbuf.at[n % 2], p_sem.at[n % 2])

    w_copy(0).start()
    p_copy(0).start()
    own = pltpu.make_async_copy(dfac, gbuf.at[me], own_sem)
    own.start()
    own.wait()
    sends = [whole(0, 1, right), whole(0, 2, left), whole(0, 3, across), to_core(0)]
    for s in sends:
        s.start()

    pg_out[...] = jnp.zeros_like(pg_out)

    def work(n, first):
        w_copy(n).wait()
        p_copy(n).wait()
        if n + 1 < 8:
            w_copy(n + 1).start()
            p_copy(n + 1).start()
        slot = n % 2
        base = chip(n) * 2

        def spread(eb, carry):
            rows = pl.ds(pl.multiple_of(eb * SUB, SUB), SUB)
            g = jnp.concatenate(
                [gbuf[base, :, rows, :].reshape(KK * SUB, 128), gbuf[base + 1, :, rows, :].reshape(KK * SUB, 128)],
                axis=1,
            )
            d = jnp.dot(kron_t[...], g, preferred_element_type=F32).astype(BF16)
            dpool[:, rows, :] = d.reshape(n_f, SUB, 256)
            x = pbuf[slot, :, rows, :].reshape(n_f * SUB, 256)
            pg_out[...] += nt(x, g)
            return carry

        lax.fori_loop(0, emb // SUB, spread, 0)

        def field(f, carry):
            part = nt(digits(wbuf[slot, f]), dpool[f])
            if first:
                acc[f] = part
            elif n == 7:
                tg_out[f] = (acc[f] + part).astype(BF16)
            else:
                acc[f] += part
            return carry

        lax.fori_loop(0, n_f, field, 0)

    def go(copy):
        copy.start()
        sends.append(copy)

    from_core(0).wait_recv()
    work(0, True)
    arrived(1)
    go(half(1, 6, 0))
    go(to_core(1))
    arrived(2)
    go(half(2, 6, 1))
    go(to_core(2))
    arrived(3)
    go(whole(3, 4, right))
    go(whole(3, 5, left))
    go(to_core(3))
    from_core(1).wait_recv()
    work(1, False)
    from_core(2).wait_recv()
    work(2, False)
    for d in range(2):
        half_arrived(6, d)
    go(to_core(6))
    from_core(3).wait_recv()
    work(3, False)
    arrived(4)
    go(half(4, 7, 0))
    go(to_core(4))
    arrived(5)
    go(half(5, 7, 1))
    go(to_core(5))
    from_core(4).wait_recv()
    work(4, False)
    from_core(5).wait_recv()
    work(5, False)
    from_core(6).wait_recv()
    work(6, False)
    for d in range(2):
        half_arrived(7, d)
    go(to_core(7))
    from_core(7).wait_recv()
    work(7, False)
    for s in sends:
        s.wait_send()


def backward(dfac, words, pooled, kron_t):
    _, n_f, emb, _ = pooled.shape
    rows = 8 * HI
    dma = pltpu.SemaphoreType.DMA
    vmem = pl.BlockSpec(memory_space=pltpu.VMEM)
    hbm = pl.BlockSpec(memory_space=pl.ANY)
    return pl.pallas_call(
        bwd_kernel,
        out_shape=(
            jax.ShapeDtypeStruct((n_f, rows, emb), BF16),
            jax.ShapeDtypeStruct((n_f * SUB, KK * SUB), F32),
        ),
        in_specs=[vmem, hbm, hbm, vmem],
        out_specs=(vmem, vmem),
        scratch_shapes=[
            pltpu.VMEM((16,) + dfac.shape, BF16),
            pltpu.VMEM((n_f, rows, emb), F32),
            pltpu.VMEM((n_f, emb, 256), BF16),
            pltpu.VMEM((2, n_f, HI, 256), jnp.int32),
            pltpu.VMEM((2, n_f, emb, 256), BF16),
            dma, dma((2,)), dma((2,)), dma((8,)), dma((8,)), dma((6,)), dma((6,)), dma((2, 2)), dma((2, 2)),
        ],
        compiler_params=pltpu.CompilerParams(collective_id=1, has_side_effects=True, vmem_limit_bytes=VMEM),
        cost_estimate=pl.CostEstimate(flops=20 * 10**9, bytes_accessed=40 * 10**6, transcendentals=0),
    )(dfac, words, pooled, kron_t)


def scatter_sum(x):
    rows = x.shape[0] // 128
    x = x.reshape(8, 16, rows, x.shape[1])
    x = lax.all_to_all(x, "mp", 1, 1, tiled=True).sum(1)
    return lax.all_to_all(x, "replica", 0, 0, tiled=True).sum(0)


def local(indices, lengths, tables, proj, w_hidden, w_out, d_logit):
    n_f = indices.shape[0]
    me = lax.axis_index("mp")
    here = lax.dynamic_slice_in_dim(proj, me * n_f, n_f, 0)
    eye = jnp.eye(SUB, dtype=BF16)
    kron_t = (here[:, None, :, None] * eye[None, :, None, :]).reshape(n_f * SUB, KK * SUB)
    words, pooled, fac = forward(indices, lengths, tables.transpose(0, 2, 1), kron_t.T)
    logits, out_part, hidden_part, dfac = dense(fac, w_hidden, w_out, d_logit)
    table_part, pg = backward(dfac, words, pooled, kron_t)
    table_grad = lax.psum(table_part, "replica").astype(F32)
    pg = jnp.einsum("fakb,ab->fk", pg.reshape(n_f, SUB, KK, SUB), jnp.eye(SUB, dtype=F32), precision="highest")
    pg_all = lax.dynamic_update_slice_in_dim(jnp.zeros(proj.shape, F32), pg, me * n_f, 0)
    place = lax.axis_index("replica") * 16 + me
    pg_all = lax.psum(pg_all, ("replica", "mp"))
    proj_share = lax.dynamic_slice_in_dim(pg_all, place * (proj.shape[0] // 128), proj.shape[0] // 128, 0)
    both = jnp.concatenate([hidden_part, out_part.sum(0)[:, None]], axis=1)
    both = scatter_sum(both)
    return (logits.reshape(-1), table_grad, both[:, :-1], both[:, -1], proj_share)


def solution(mesh):
    in_specs = (
        P("mp", None, "replica"),
        P("mp", "replica"),
        P("mp", None, None),
        P(),
        P(),
        P(),
        P(("replica", "mp")),
    )
    out_specs = (
        P(("replica", "mp")),
        P("mp", None, None),
        P(("replica", "mp"), None),
        P(("replica", "mp")),
        P(("replica", "mp"), None),
    )
    return jax.shard_map(local, mesh=mesh, in_specs=in_specs, out_specs=out_specs, check_vma=False)
```

```python
import functools

import jax
import jax.numpy as jnp
from jax import lax
from jax.experimental import pallas as pl
from jax.experimental.pallas import tpu as pltpu
from jax.sharding import PartitionSpec as P

MESH = pl.DeviceIdType.MESH
K1 = 8
K2 = 8
KK = K1 + K2
SUB = 16
HI = 64
BITS = 4
VMEM = 60 * 1024 * 1024
F32 = jnp.float32
BF16 = jnp.bfloat16


def peers():
    me = lax.axis_index("mp")
    core = lax.rem(me, 2)
    y = lax.rem(lax.div(me, 2), 4)
    z = lax.div(me, 8)
    other = {"mp": me + 1 - 2 * core}
    right = {"mp": z * 8 + lax.rem(y + 1, 4) * 2 + core}
    left = {"mp": z * 8 + lax.rem(y + 3, 4) * 2 + core}
    across = {"mp": (1 - z) * 8 + y * 2 + core}
    return me, core, y, z, other, right, left, across


def barrier(devices):
    sem = pltpu.get_barrier_semaphore()
    for d in devices:
        pl.semaphore_signal(sem, inc=1, device_id=d, device_id_type=MESH)
    pl.semaphore_wait(sem, len(devices))


def remote(src, dst, send, recv, device):
    return pltpu.make_async_remote_copy(
        src_ref=src, dst_ref=dst, send_sem=send, recv_sem=recv, device_id=device, device_id_type=MESH
    )


def digits(words):
    return jnp.concatenate(
        [(lax.shift_right_logical(words, BITS * d) & 15).astype(F32).astype(BF16) for d in range(8)], axis=0
    )


def fwd_kernel(
    idx, lens, tab_t, kron, words_out, pooled_out, fac_out,
    sbuf, rcore, rhalf, rfull, rz, wbuf, pbuf,
    core_s, core_r, half_s, half_r, full_s, full_r, z_s, z_r, w_sem, p_sem,
):
    me, core, y, z, other, right, left, across = peers()
    barrier((other, right, left, across))
    n_f = idx.shape[0]
    emb = tab_t.shape[1]

    def zo_of(t):
        return jnp.where(t < 2, t, jnp.where(t < 6, lax.div(t - 2, 2), t - 6))

    def chunk_of(t):
        dy = jnp.where(t < 2, 2, jnp.where(t < 6, 1 + 2 * lax.rem(t, 2), 0))
        zo = zo_of(t)
        zt = lax.rem(z + 1 + zo, 2)
        return zt * 4 + lax.rem(y + dy, 4)

    def p_copy(t):
        slot = lax.rem(t, 2)
        return pltpu.make_async_copy(pbuf.at[slot], pooled_out.at[chunk_of(t)], p_sem.at[slot])

    def w_copy(t):
        return pltpu.make_async_copy(wbuf.at[t], words_out.at[chunk_of(t)], w_sem.at[t])

    def core_copy(t):
        return remote(sbuf.at[t, 1 - core], rcore.at[t], core_s.at[t], core_r.at[t], other)

    def half_copy(t, zo, d):
        return remote(
            sbuf.at[t, core, pl.ds(d * K1, K1)], rhalf.at[zo, d], half_s.at[zo, d], half_r.at[zo, d], (right, left)[d]
        )

    def full_copy(t, zo, d):
        return remote(sbuf.at[t, core], rfull.at[zo, d], full_s.at[zo, d], full_r.at[zo, d], (right, left)[d])

    def z_copy():
        return remote(sbuf.at[6, core], rz, z_s, z_r, across)

    def compute(t):
        q = chunk_of(t)
        slot = lax.rem(t, 2)
        where = pl.ds(pl.multiple_of(q * 256, 256), 256)

        @pl.when(t >= 2)
        def _():
            p_copy(t - 2).wait()

        def field(f, carry):
            ids = idx[f, :, where]
            live = lens[pl.ds(f, 1), where]
            lane_slot = lax.broadcasted_iota(jnp.int32, ids.shape, 0)
            hi = ids & (HI - 1)
            val = jnp.where(lane_slot < live, jnp.left_shift(1, BITS * lax.shift_right_logical(ids, 6)), 0)
            rows = lax.broadcasted_iota(jnp.int32, (HI, 256), 0)
            words = jnp.zeros((HI, 256), jnp.int32)
            for s in range(8):
                words = words + jnp.where(hi[s : s + 1, :] == rows, val[s : s + 1, :], 0)
            wbuf[t, f] = words
            pooled = jnp.dot(tab_t[f], digits(words), preferred_element_type=F32)
            pbuf[slot, f] = pooled.astype(BF16)
            return carry

        lax.fori_loop(0, n_f, field, 0, unroll=4)
        p_copy(t).start()
        w_copy(t).start()

        def block(eb, carry):
            rows = pl.ds(pl.multiple_of(eb * SUB, SUB), SUB)
            x = pbuf[slot, :, rows, :].reshape(n_f * SUB, 256)
            part = jnp.dot(kron[...], x, preferred_element_type=F32).astype(BF16).reshape(KK, SUB, 256)
            sbuf[t, 0, :, rows, :] = part[:, :, :128]
            sbuf[t, 1, :, rows, :] = part[:, :, 128:]
            return carry

        lax.fori_loop(0, emb // SUB, block, 0, unroll=4)
        core_copy(t).start()

    def add(t, pairs, out=None):
        def one(k, carry, refs):
            total = sbuf[t, core, k].astype(F32)
            for r, first in refs:
                total = total + r[k - first].astype(F32)
            if out is None:
                sbuf[t, core, k] = total.astype(BF16)
            else:
                out[k] = total
            return carry

        lax.fori_loop(0, K1, functools.partial(one, refs=[(r, a) for r, a, b in pairs if a < K1]), 0)
        lax.fori_loop(K1, KK, functools.partial(one, refs=[(r, a) for r, a, b in pairs if b > K1]), 0)

    def pass_on(t):
        core_copy(t).wait_recv()
        mine = (rcore.at[t], 0, KK)

        @pl.when(t < 2)
        def _():
            add(t, [mine])
            half_copy(t, zo_of(t), 0).start()
            half_copy(t, zo_of(t), 1).start()

        for d in range(2):

            @pl.when(jnp.logical_or(t == 2 + d, t == 4 + d))
            def _():
                zo = zo_of(t)
                half_copy(zo, zo, d).wait_recv()
                add(t, [mine, (rhalf.at[zo, d], d * K1, d * K1 + K1)])
                full_copy(t, zo, d).start()

        @pl.when(t == 6)
        def _():
            for d in range(2):
                full_copy(2 + d, 0, d).wait_recv()
            add(t, [mine, (rfull.at[0, 0], 0, KK), (rfull.at[0, 1], 0, KK)])
            z_copy().start()

    def step(t, carry):
        compute(t)

        @pl.when(t >= 1)
        def _():
            pass_on(t - 1)

        return carry

    lax.fori_loop(0, 8, step, 0)
    core_copy(7).wait_recv()
    for d in range(2):
        full_copy(4 + d, 1, d).wait_recv()
    z_copy().wait_recv()
    add(
        7, [(rcore.at[7], 0, KK), (rfull.at[1, 0], 0, KK), (rfull.at[1, 1], 0, KK), (rz, 0, KK)], fac_out
    )

    for t in range(8):
        core_copy(t).wait_send()
        w_copy(t).wait()
    for zo in range(2):
        for d in range(2):
            half_copy(zo, zo, d).wait_send()
            full_copy(2 + 2 * zo + d, zo, d).wait_send()
    z_copy().wait_send()
    p_copy(6).wait()
    p_copy(7).wait()


def forward(indices, lengths, tab_t, kron):
    n_f, emb, _ = tab_t.shape
    dma = pltpu.SemaphoreType.DMA
    vmem = pl.BlockSpec(memory_space=pltpu.VMEM)
    hbm = pl.BlockSpec(memory_space=pl.ANY)
    return pl.pallas_call(
        fwd_kernel,
        out_shape=(
            jax.ShapeDtypeStruct((8, n_f, HI, 256), jnp.int32),
            jax.ShapeDtypeStruct((8, n_f, emb, 256), BF16),
            jax.ShapeDtypeStruct((KK, emb, 128), F32),
        ),
        in_specs=[vmem] * 4,
        out_specs=(hbm, hbm, vmem),
        scratch_shapes=[
            pltpu.VMEM((8, 2, KK, emb, 128), BF16),
            pltpu.VMEM((8, KK, emb, 128), BF16),
            pltpu.VMEM((2, 2, K1, emb, 128), BF16),
            pltpu.VMEM((2, 2, KK, emb, 128), BF16),
            pltpu.VMEM((KK, emb, 128), BF16),
            pltpu.VMEM((8, n_f, HI, 256), jnp.int32),
            pltpu.VMEM((2, n_f, emb, 256), BF16),
            dma((8,)), dma((8,)), dma((2, 2)), dma((2, 2)), dma((2, 2)), dma((2, 2)), dma, dma, dma((8,)), dma((2,)),
        ],
        compiler_params=pltpu.CompilerParams(collective_id=0, has_side_effects=True, vmem_limit_bytes=VMEM),
        cost_estimate=pl.CostEstimate(flops=15 * 10**9, bytes_accessed=40 * 10**6, transcendentals=0),
    )(indices, lengths, tab_t, kron)


def nt(a, b):
    return lax.dot_general(a, b, (((1,), (1,)), ((), ())), preferred_element_type=F32)


def dense_kernel(fac, wh, wh_t, wo_col, wo_row, dl, logits, grads, dfac, inter):
    hid, n_feat = wh.shape
    emb = fac.shape[1]
    step = grads.shape[0] * grads.shape[2]

    def left(i, carry):
        a = fac[i]
        for j in range(K2):
            inter[pl.ds(i * K2 + j, 1), :] = jnp.sum(a * fac[K1 + j], axis=0, keepdims=True)
        return carry

    lax.fori_loop(0, K1, left, 0)
    feat = inter[...].astype(BF16)
    row = dl[...]
    n = row.shape[1]
    d0 = row.astype(BF16)
    r1 = row - d0.astype(F32)
    d1 = r1.astype(BF16)
    d2 = (r1 - d1.astype(F32)).astype(BF16)
    sub = lax.broadcasted_iota(jnp.int32, (n_feat, n), 0)
    d_rows = jnp.where(
        sub == 0, d0.astype(F32), jnp.where(sub == 1, d1.astype(F32), jnp.where(sub == 2, d2.astype(F32), 0.0))
    ).astype(BF16)
    nil = jnp.zeros((n_feat, n), BF16)
    feat_low = jnp.concatenate([feat, nil], axis=0)
    d_high = jnp.concatenate([nil, d_rows], axis=0)

    def top(c, carry):
        logit_acc, d_inter = carry
        at = pl.ds(pl.multiple_of(c * step, step), step)
        v = jnp.dot(wh[at, :], feat, preferred_element_type=F32)
        s = jax.nn.sigmoid(v)
        hidden = (v * s).astype(BF16)
        logit_acc = logit_acc + jnp.dot(wo_row[:, at], hidden, preferred_element_type=F32)
        d_hidden = (wo_col[at, :].astype(F32) * row * s * (1.0 + v * (1.0 - s))).astype(BF16)
        grad = nt(d_hidden, feat_low) + nt(hidden, d_high)
        grads[:, pl.ds(c, 1), :, :] = grad.astype(BF16).reshape(grads.shape[0], 1, grads.shape[2], 2 * n_feat)
        d_inter = d_inter + jnp.dot(wh_t[:, at], d_hidden, preferred_element_type=F32)
        return logit_acc, d_inter

    logit_acc, d_inter = lax.fori_loop(
        0, hid // step, top, (jnp.zeros((8, n), F32), jnp.zeros((n_feat, n), F32))
    )
    logits[...] = logit_acc[0:1]
    inter[...] = d_inter

    def back(eb, carry):
        p = lax.div(eb, emb // SUB // 2)
        rows = pl.ds(pl.multiple_of(eb * SUB, SUB), SUB)
        low = pl.ds(pl.multiple_of(lax.rem(eb, emb // SUB // 2) * SUB, SUB), SUB)
        right = [fac[K1 + j, rows, :] for j in range(K2)]
        d_right = [jnp.zeros((SUB, n), F32) for _ in range(K2)]
        for i in range(K1):
            a = fac[i, rows, :]
            d_left = jnp.zeros((SUB, n), F32)
            for j in range(K2):
                g = inter[pl.ds(i * K2 + j, 1), :]
                d_left = d_left + g * right[j]
                d_right[j] = d_right[j] + g * a
            dfac[p, i, low, :] = d_left.astype(BF16)
        for j in range(K2):
            dfac[p, K1 + j, low, :] = d_right[j].astype(BF16)
        return carry

    lax.fori_loop(0, emb // SUB, back, 0)


def dense(fac, w_hidden, w_out, d_logit):
    hid, feat = w_hidden.shape
    n = d_logit.shape[0]
    wo_row = jnp.broadcast_to(w_out[None, :], (8, hid))
    return pl.pallas_call(
        dense_kernel,
        out_shape=(
            jax.ShapeDtypeStruct((1, n), F32),
            jax.ShapeDtypeStruct((16, 8, hid // 128, 2 * feat), BF16),
            jax.ShapeDtypeStruct((2, KK, fac.shape[1] // 2, n), BF16),
        ),
        scratch_shapes=[pltpu.VMEM((feat, n), F32)],
        compiler_params=pltpu.CompilerParams(vmem_limit_bytes=VMEM),
        cost_estimate=pl.CostEstimate(flops=10**9, bytes_accessed=10**7, transcendentals=10**6),
    )(fac, w_hidden, w_hidden.T, w_out[:, None], wo_row, d_logit[None, :])


def bwd_kernel(
    dfac, words, pooled, kron_t, grads,
    tg_out, hid_out, pg_out,
    gbuf, acc, dpool, wbuf, pbuf, tbuf, t_half, t_full, t_z, pg,
    h_core, h_sum, h_half, h_full, h_z, hx_sum, hx_half, hx_full, hx_z, p_x, p_z, p_all,
    own_sem, w_sem, p_sem, core_s, core_r, ici_s, ici_r, half_s, half_r,
    th_s, th_r, tf_s, tf_r, tz_s, tz_r, gz_s, gz_r, gx_s, gx_r, gh_s, gh_r, h_s, h_r, q_s, q_r,
):
    me, core, y, z, other, right, left, across = peers()
    opposite = {"mp": z * 8 + lax.rem(y + 2, 4) * 2 + core}
    rep = lax.axis_index("replica")
    x = lax.rem(rep, 4)
    zl = lax.div(rep, 4)
    x_to = [None] + [{"replica": zl * 4 + lax.rem(x + d, 4)} for d in (1, 2, 3)]
    x_right, x_left = x_to[1], x_to[3]
    z_near = {"replica": (1 - zl) * 4 + x}
    n_f = tbuf.shape[1]
    width = dpool.shape[1]
    places = ((0, 0), (0, 3), (0, 1), (1, 0), (1, 3), (1, 1), (0, 2), (1, 2))
    order = [(p, n) for p in range(2) for n in (0, 1, 2, 3, 6, 4, 5, 7)]
    sends = []

    def go(copy):
        copy.start()
        sends.append(copy)

    def chip(n):
        dz, dy = places[n]
        return lax.rem(z + dz, 2) * 4 + lax.rem(y + dy, 4)

    def block(n):
        return chip(n) * 2 + core

    def to_core(p, n):
        ref = gbuf.at[p, block(n)]
        return remote(ref, ref, core_s.at[p, n], core_r.at[p, n], other)

    def from_core(p, n):
        ref = gbuf.at[p, chip(n) * 2 + 1 - core]
        remote(ref, ref, core_s.at[p, n], core_r.at[p, n], other).wait_recv()

    def whole(p, n, m, device):
        ref = gbuf.at[p, block(n)]
        return remote(ref, ref, ici_s.at[p, m], ici_r.at[p, m], device)

    def arrived(p, m):
        whole(p, m, m, right).wait_recv()

    def half(p, n, m, d):
        ref = gbuf.at[p, block(n), pl.ds(d * K1, K1)]
        i = (p, m - 6, d)
        return remote(ref, ref, half_s.at[i], half_r.at[i], (right, left)[d])

    def half_arrived(p, m):
        for d in range(2):
            half(p, m, m, d).wait_recv()
        go(to_core(p, m))

    def near(p):
        arrived(p, 1)
        go(half(p, 1, 6, 0))
        go(to_core(p, 1))
        arrived(p, 2)
        go(half(p, 2, 6, 1))
        go(to_core(p, 2))
        arrived(p, 3)
        go(whole(p, 3, 4, right))
        go(whole(p, 3, 5, left))
        go(to_core(p, 3))

    def far(p):
        arrived(p, 4)
        go(half(p, 4, 7, 0))
        go(to_core(p, 4))
        arrived(p, 5)
        go(half(p, 5, 7, 1))
        go(to_core(p, 5))

    def w_copy(n):
        return pltpu.make_async_copy(words.at[chip(n)], wbuf.at[n], w_sem.at[n])

    def p_copy(i):
        p, n = order[i]
        return pltpu.make_async_copy(
            pooled.at[chip(n), :, pl.ds(p * width, width), :], pbuf.at[i % 2], p_sem.at[i % 2]
        )

    def work(p, n):
        i = order.index((p, n))
        p_copy(i).wait()
        if i + 1 < len(order):
            p_copy(i + 1).start()
        if p == 0:
            w_copy(n).wait()
        from_core(p, n)
        slot = i % 2
        base = chip(n) * 2

        def spread(eb, carry):
            rows = pl.ds(pl.multiple_of(eb * SUB, SUB), SUB)
            g = jnp.concatenate(
                [gbuf[p, base + c, :, rows, :].reshape(KK * SUB, 128) for c in range(2)], axis=1
            )
            d = jnp.dot(kron_t[...], g, preferred_element_type=F32).astype(BF16)
            dpool[:, rows, :] = d.reshape(n_f, SUB, 256)
            pg[...] += nt(pbuf[slot, :, rows, :].reshape(n_f * SUB, 256), g)
            return carry

        lax.fori_loop(0, width // SUB, spread, 0, unroll=4)

        def field(f, carry):
            part = nt(digits(wbuf[n, f]), dpool[f])
            if n == 0:
                acc[f] = part
            elif n == 7:
                tbuf[p, f] = (acc[f] + part).astype(BF16)
            else:
                acc[f] += part
            return carry

        lax.fori_loop(0, n_f, field, 0, unroll=4)

    def first(dx, zo):
        return (lax.rem(zl + 1 + zo, 2) * 4 + lax.rem(x + dx, 4)) * 2

    def t_half_copy(p, zo, d):
        i = (p, zo, d)
        return remote(tbuf.at[p, first(2, zo) + d], t_half.at[i], th_s.at[i], th_r.at[i], (x_right, x_left)[d])

    def t_full_copy(p, zo, d):
        i = (p, zo, d)
        src = tbuf.at[p, pl.ds(first(1 + 2 * d, zo), 2)]
        return remote(src, t_full.at[i], tf_s.at[i], tf_r.at[i], (x_right, x_left)[d])

    def t_z_copy(p):
        return remote(tbuf.at[p, pl.ds(first(0, 0), 2)], t_z.at[p], tz_s.at[p], tz_r.at[p], z_near)

    def g_x_copy(p, zb, d, dx=0):
        ref = tg_out.at[p, pl.ds(first(dx, 1 - zb), 2)]
        i = (p, zb, d)
        return remote(ref, ref, gx_s.at[i], gx_r.at[i], (x_right, x_left)[d])

    def g_z_copy(p, zb):
        ref = tg_out.at[p, pl.ds(first(0, 1 - zb), 2)]
        return remote(ref, ref, gz_s.at[p], gz_r.at[p], z_near)

    def g_half_copy(p, zb, d, dx):
        ref = tg_out.at[p, first(dx, 1 - zb) + d]
        i = (p, zb, d)
        return remote(ref, ref, gh_s.at[i], gh_r.at[i], (x_right, x_left)[d])

    def t_start(p):
        for zo in range(2):
            for d in range(2):
                go(t_half_copy(p, zo, d))

    def t_pass(p, zo):
        for d in range(2):
            t_half_copy(p, zo, d).wait_recv()
            at = first(1 + 2 * d, zo) + d
            tbuf[p, at] = (tbuf[p, at].astype(F32) + t_half[p, zo, d].astype(F32)).astype(BF16)
            go(t_full_copy(p, zo, d))

    def t_total(p, zo, k):
        total = tbuf[p, first(0, zo) + k].astype(F32)
        return total + t_full[p, zo, 0, k].astype(F32) + t_full[p, zo, 1, k].astype(F32)

    def t_cross(p):
        for d in range(2):
            t_full_copy(p, 0, d).wait_recv()
        for k in range(2):
            tbuf[p, first(0, 0) + k] = t_total(p, 0, k).astype(BF16)
        go(t_z_copy(p))

    def t_finish(p):
        for d in range(2):
            t_full_copy(p, 1, d).wait_recv()
        t_z_copy(p).wait_recv()
        for k in range(2):
            tg_out[p, first(0, 1) + k] = (t_total(p, 1, k) + t_z[p, k].astype(F32)).astype(BF16)
        go(g_z_copy(p, 0))
        for d in range(2):
            go(g_x_copy(p, 0, d))

    def t_spread(p):
        g_z_copy(p, 1).wait_recv()
        for d in range(2):
            go(g_x_copy(p, 1, d))

    def t_relay(p, zb):
        for d in range(2):
            dx = 3 - 2 * d
            g_x_copy(p, zb, d, dx).wait_recv()
            go(g_half_copy(p, zb, d, dx))

    def t_last(p):
        for zb in range(2):
            for d in range(2):
                g_half_copy(p, zb, d, 2).wait_recv()

    def h_copy(i):
        if i == 0:
            src, dst, to = grads.at[:, 1 - core], h_core, other
        elif i < 3:
            d = i - 1
            src, dst, to = h_sum.at[:, lax.rem(y + 2, 4), pl.ds(d * 128, 128)], h_half.at[d], (right, left)[d]
        elif i < 5:
            d = i - 3
            src, dst, to = h_sum.at[:, lax.rem(y + 1 + 2 * d, 4)], h_full.at[d], (right, left)[d]
        elif i == 5:
            src, dst, to = h_sum.at[1 - z, y], h_z, across
        elif i < 8:
            d = i - 6
            src, dst, to = hx_sum.at[:, lax.rem(x + 2, 4), pl.ds(d * 16, 16)], hx_half.at[d], (x_right, x_left)[d]
        elif i < 10:
            d = i - 8
            src, dst, to = hx_sum.at[:, lax.rem(x + 1 + 2 * d, 4)], hx_full.at[d], (x_right, x_left)[d]
        else:
            src, dst, to = hx_sum.at[1 - zl, x], hx_z, z_near
        return remote(src, dst, h_s.at[i], h_r.at[i], to)

    def wide(v):
        return v.astype(F32)

    def h1():
        h_copy(0).wait_recv()
        for q in range(8):
            total = wide(grads[q, core]) + wide(h_core[q])
            h_sum[q // 4, q % 4] = total.astype(BF16).reshape(h_sum.shape[2:])
        go(h_copy(1))
        go(h_copy(2))

    def h2():
        for d in range(2):
            h_copy(1 + d).wait_recv()
            at, rows = lax.rem(y + 1 + 2 * d, 4), pl.ds(d * 128, 128)
            for k in range(2):
                h_sum[k, at, rows] = (wide(h_sum[k, at, rows]) + wide(h_half[d, k])).astype(BF16)
            go(h_copy(3 + d))

    def h3():
        for d in range(2):
            h_copy(3 + d).wait_recv()
        for k in range(2):
            h_sum[k, y] = (wide(h_sum[k, y]) + wide(h_full[0, k]) + wide(h_full[1, k])).astype(BF16)
        go(h_copy(5))

    def h4():
        h_copy(5).wait_recv()
        total = (wide(h_sum[z, y]) + wide(h_z[...])).astype(BF16).reshape(8, 32, 128)
        for q in range(8):
            hx_sum[q // 4, q % 4] = total[q]
        go(h_copy(6))
        go(h_copy(7))

    def h5():
        for d in range(2):
            h_copy(6 + d).wait_recv()
            at, rows = lax.rem(x + 1 + 2 * d, 4), pl.ds(d * 16, 16)
            for k in range(2):
                hx_sum[k, at, rows] = (wide(hx_sum[k, at, rows]) + wide(hx_half[d, k])).astype(BF16)
            go(h_copy(8 + d))

    def h6():
        for d in range(2):
            h_copy(8 + d).wait_recv()
        for k in range(2):
            hx_sum[k, x] = (wide(hx_sum[k, x]) + wide(hx_full[0, k]) + wide(hx_full[1, k])).astype(BF16)
        go(h_copy(10))

    def h7():
        h_copy(10).wait_recv()
        hid_out[...] = wide(hx_sum[zl, x]) + wide(hx_z[...])

    def q_copy(i):
        if i < 3:
            src, dst, to = p_x.at[3], p_x.at[i], x_to[1 + i]
        elif i == 3:
            src, dst, to = p_z.at[0], p_z.at[1], z_near
        elif i == 4:
            ref = p_all.at[z, y, core]
            src, dst, to = ref, ref, other
        elif i < 8:
            ref = p_all.at[z, y]
            src, dst, to = ref, ref, (right, opposite, left)[i - 5]
        else:
            ref = p_all.at[z]
            src, dst, to = ref, ref, across
        return remote(src, dst, q_s.at[i], q_r.at[i], to)

    def q0():
        a = lax.rem(lax.broadcasted_iota(jnp.int32, pg.shape, 0), SUB)
        b = lax.rem(lax.broadcasted_iota(jnp.int32, pg.shape, 1), SUB)
        p_x[3] = jnp.sum(jnp.where(a == b, pg[...], 0.0).reshape(n_f, SUB, KK * SUB), axis=1)
        for i in range(3):
            go(q_copy(i))

    def q1():
        for i in range(3):
            q_copy(i).wait_recv()
        p_z[0] = p_x[0] + p_x[1] + p_x[2] + p_x[3]
        go(q_copy(3))

    def q2():
        q_copy(3).wait_recv()
        p_all[z, y, core] = p_z[0] + p_z[1]
        go(q_copy(4))

    def q3():
        ref = p_all.at[z, y, 1 - core]
        remote(ref, ref, q_s.at[4], q_r.at[4], other).wait_recv()
        for i in range(3):
            go(q_copy(5 + i))

    def q4():
        for i in range(3):
            ref = p_all.at[z, lax.rem(y + 3 - i, 4)]
            remote(ref, ref, q_s.at[5 + i], q_r.at[5 + i], right).wait_recv()
        go(q_copy(8))

    def q5():
        ref = p_all.at[1 - z]
        remote(ref, ref, q_s.at[8], q_r.at[8], across).wait_recv()
        j = 2 * rep + lax.div(me, 8)
        pg_out[...] = p_all[lax.div(j, 8), lax.rem(lax.div(j, 2), 4), lax.rem(j, 2)]

    own = [pltpu.make_async_copy(dfac.at[p], gbuf.at[p, me], own_sem.at[p]) for p in range(2)]
    for c in own:
        c.start()
    p_copy(0).start()
    for _, n in order[:8]:
        w_copy(n).start()
    pg[...] = jnp.zeros_like(pg)
    barrier((other, right, left, opposite, across, x_to[1], x_to[2], x_to[3], z_near))
    own[0].wait()
    go(whole(0, 0, 1, right))
    go(whole(0, 0, 2, left))
    go(whole(0, 0, 3, across))
    go(to_core(0, 0))
    go(h_copy(0))
    own[1].wait()
    go(to_core(1, 0))
    work(0, 0)
    h1()
    near(0)
    go(whole(1, 0, 3, across))
    work(0, 1)
    h2()
    work(0, 2)
    work(0, 3)
    h3()
    half_arrived(0, 6)
    work(0, 6)
    h4()
    far(0)
    work(0, 4)
    h5()
    work(0, 5)
    half_arrived(0, 7)
    go(whole(1, 0, 1, right))
    go(whole(1, 0, 2, left))
    work(0, 7)
    t_start(0)
    h6()
    work(1, 0)
    t_pass(0, 0)
    near(1)
    t_pass(0, 1)
    work(1, 1)
    t_cross(0)
    work(1, 2)
    h7()
    work(1, 3)
    t_finish(0)
    half_arrived(1, 6)
    work(1, 6)
    t_spread(0)
    far(1)
    t_relay(0, 0)
    work(1, 4)
    work(1, 5)
    t_relay(0, 1)
    half_arrived(1, 7)
    work(1, 7)
    t_start(1)
    t_last(0)
    q0()
    t_pass(1, 0)
    t_pass(1, 1)
    q1()
    q2()
    t_cross(1)
    q3()
    t_finish(1)
    q4()
    t_spread(1)
    t_relay(1, 0)
    q5()
    t_relay(1, 1)
    t_last(1)
    for s in sends:
        s.wait_send()


def backward(dfac, words, pooled, kron_t, grads):
    _, n_f, emb, _ = pooled.shape
    rows = 8 * HI
    width = emb // 2
    n_grad = grads.shape[2]
    grads = grads.reshape(8, 2, 8, n_grad, 128)
    dma = pltpu.SemaphoreType.DMA
    vmem = pl.BlockSpec(memory_space=pltpu.VMEM)
    hbm = pl.BlockSpec(memory_space=pl.ANY)
    a222 = dma((2, 2, 2))
    return pl.pallas_call(
        bwd_kernel,
        out_shape=(
            jax.ShapeDtypeStruct((2, n_f, rows, width), BF16),
            jax.ShapeDtypeStruct((n_grad, 128), F32),
            jax.ShapeDtypeStruct((n_f, KK * SUB), F32),
        ),
        in_specs=[vmem, hbm, hbm, vmem, vmem],
        out_specs=(vmem, vmem, vmem),
        scratch_shapes=[
            pltpu.VMEM((2, 16, KK, width, 128), BF16),
            pltpu.VMEM((n_f, rows, width), F32),
            pltpu.VMEM((n_f, width, 256), BF16),
            pltpu.VMEM((8, n_f, HI, 256), jnp.int32),
            pltpu.VMEM((2, n_f, width, 256), BF16),
            pltpu.VMEM((2, n_f, rows, width), BF16),
            pltpu.VMEM((2, 2, 2, rows, width), BF16),
            pltpu.VMEM((2, 2, 2, 2, rows, width), BF16),
            pltpu.VMEM((2, 2, rows, width), BF16),
            pltpu.VMEM((n_f * SUB, KK * SUB), F32),
            pltpu.VMEM((8, 8, n_grad, 128), BF16),
            pltpu.VMEM((2, 4, 8 * n_grad, 128), BF16),
            pltpu.VMEM((2, 2, 4 * n_grad, 128), BF16),
            pltpu.VMEM((2, 2, 8 * n_grad, 128), BF16),
            pltpu.VMEM((8 * n_grad, 128), BF16),
            pltpu.VMEM((2, 4, n_grad, 128), BF16),
            pltpu.VMEM((2, 2, n_grad // 2, 128), BF16),
            pltpu.VMEM((2, 2, n_grad, 128), BF16),
            pltpu.VMEM((n_grad, 128), BF16),
            pltpu.VMEM((4, n_f, KK * SUB), F32),
            pltpu.VMEM((2, n_f, KK * SUB), F32),
            pltpu.VMEM((2, 4, 2, n_f, KK * SUB), F32),
            dma((2,)), dma((8,)), dma((2,)), dma((2, 8)), dma((2, 8)), dma((2, 6)), dma((2, 6)), a222, a222,
            a222, a222, a222, a222, dma((2,)), dma((2,)), dma((2,)), dma((2,)), a222, a222, a222, a222,
            dma((11,)), dma((11,)), dma((9,)), dma((9,)),
        ],
        compiler_params=pltpu.CompilerParams(collective_id=1, has_side_effects=True, vmem_limit_bytes=VMEM),
        cost_estimate=pl.CostEstimate(flops=20 * 10**9, bytes_accessed=40 * 10**6, transcendentals=0),
    )(dfac, words, pooled, kron_t, grads)


def local(indices, lengths, tables, proj, w_hidden, w_out, d_logit):
    n_f = indices.shape[0]
    me = lax.axis_index("mp")
    here = lax.dynamic_slice_in_dim(proj, me * n_f, n_f, 0)
    eye = jnp.eye(SUB, dtype=BF16)
    kron_t = (here[:, None, :, None] * eye[None, :, None, :]).reshape(n_f * SUB, KK * SUB)
    words, pooled, fac = forward(indices, lengths, tables.transpose(0, 2, 1), kron_t.T)
    logits, grads, dfac = dense(fac, w_hidden, w_out, d_logit)
    tables_sum, dense_sum, pg = backward(dfac, words, pooled, kron_t, grads)
    table_grad = jnp.concatenate([tables_sum[0], tables_sum[1]], axis=2).astype(F32)
    feat = w_hidden.shape[1]
    mine = proj.shape[0] // 128
    pg = lax.dynamic_slice_in_dim(pg, lax.rem(me * mine, n_f), mine, 0)
    return (
        logits.reshape(-1),
        table_grad,
        dense_sum[:, :feat],
        dense_sum[:, feat : feat + 3].sum(1),
        pg.reshape(mine, KK, SUB).sum(2),
    )


def solution(mesh):
    in_specs = (
        P("mp", None, "replica"),
        P("mp", "replica"),
        P("mp", None, None),
        P(),
        P(),
        P(),
        P(("replica", "mp")),
    )
    out_specs = (
        P(("replica", "mp")),
        P("mp", None, None),
        P(("replica", "mp"), None),
        P(("replica", "mp")),
        P(("replica", "mp"), None),
    )
    return jax.shard_map(local, mesh=mesh, in_specs=in_specs, out_specs=out_specs, check_vma=False)
```

```python
import functools

import jax
import jax.numpy as jnp
from jax import lax
from jax.experimental import pallas as pl
from jax.experimental.pallas import tpu as pltpu
from jax.sharding import PartitionSpec as P

MESH = pl.DeviceIdType.MESH
K1 = 8
K2 = 8
KK = K1 + K2
SUB = 16
HI = 64
BITS = 4
VMEM = 60 * 1024 * 1024
LOW = 9
LOW_HALF = 5
GATHER_LOW = (9, 12)
F32 = jnp.float32
BF16 = jnp.bfloat16


def peers():
    me = lax.axis_index("mp")
    core = lax.rem(me, 2)
    y = lax.rem(lax.div(me, 2), 4)
    z = lax.div(me, 8)
    other = {"mp": me + 1 - 2 * core}
    right = {"mp": z * 8 + lax.rem(y + 1, 4) * 2 + core}
    left = {"mp": z * 8 + lax.rem(y + 3, 4) * 2 + core}
    across = {"mp": (1 - z) * 8 + y * 2 + core}
    return me, core, y, z, other, right, left, across


def barrier(devices):
    sem = pltpu.get_barrier_semaphore()
    for d in devices:
        pl.semaphore_signal(sem, inc=1, device_id=d, device_id_type=MESH)
    pl.semaphore_wait(sem, len(devices))


def remote(src, dst, send, recv, device):
    return pltpu.make_async_remote_copy(
        src_ref=src, dst_ref=dst, send_sem=send, recv_sem=recv, device_id=device, device_id_type=MESH
    )


def digits(words):
    return jnp.concatenate(
        [(lax.shift_right_logical(words, BITS * d) & 15).astype(F32).astype(BF16) for d in range(8)], axis=0
    )


def nt(a, b):
    return lax.dot_general(a, b, (((1,), (1,)), ((), ())), preferred_element_type=F32)


def fwd_kernel(
    idx, lens, tab, kron, words_out, pooled_out, fac_out,
    tab_t, sbuf, rcore, rhalf, rfull, rz, rshare, wbuf, pbuf,
    core_s, core_r, half_s, half_r, full_s, full_r, z_s, z_r, share_s, share_r, w_sem, p_sem,
):
    me, core, y, z, other, right, left, across = peers()
    n_f = idx.shape[0]
    emb = tab.shape[2]

    def chunk_of(t):
        u = lax.rem(t, 3)
        early = lax.div(7 - t, 2) > 0
        dy = jnp.where(early, jnp.where(u == 0, 2, 2 * u - 1), 0)
        zo = jnp.where(early, lax.div(t, 3), t - 6)
        return lax.rem(z + 1 + zo, 2) * 4 + lax.rem(y + dy, 4)

    def p_copy(t):
        slot = lax.rem(t, 2)
        return pltpu.make_async_copy(pbuf.at[slot], pooled_out.at[chunk_of(t)], p_sem.at[slot])

    def w_copy(t):
        return pltpu.make_async_copy(wbuf.at[t], words_out.at[chunk_of(t)], w_sem.at[t])

    def core_copy(t):
        return remote(sbuf.at[t, 1 - core], rcore.at[t], core_s.at[t], core_r.at[t], other)

    def half_range(zo, d):
        if zo:
            return d * K1, d * K1 + K1
        return (0, LOW_HALF) if d == 0 else (LOW_HALF, LOW)

    def half_copy(zo, d):
        a, b = half_range(zo, d)
        ks = pl.ds(a, b - a)
        return remote(
            sbuf.at[3 * zo, core, ks], rhalf.at[zo, ks], half_s.at[zo, d], half_r.at[zo, d], (right, left)[d]
        )

    def full_copy(zo, d):
        ks = pl.ds(0, KK if zo else LOW)
        return remote(
            sbuf.at[3 * zo + 1 + d, core, ks], rfull.at[zo, d, ks], full_s.at[zo, d], full_r.at[zo, d], (right, left)[d]
        )

    def share_copy(t):
        return remote(sbuf.at[t, core, pl.ds(LOW, KK - LOW)], rshare.at[t], share_s.at[t], share_r.at[t], across)

    def z_copy():
        return remote(sbuf.at[6, core], rz, z_s, z_r, across)

    def compute(t, start=False):
        q = chunk_of(t)
        slot = lax.rem(t, 2)
        where = pl.ds(pl.multiple_of(q * 256, 256), 256)
        if not start:

            @pl.when(t >= 2)
            def _():
                p_copy(t - 2).wait()

        else:
            eye = (
                lax.broadcasted_iota(jnp.int32, (emb, emb), 0) == lax.broadcasted_iota(jnp.int32, (emb, emb), 1)
            ).astype(F32).astype(BF16)

        def field(f, carry):
            ids = idx[f, :, where]
            live = lens[pl.ds(f, 1), where]
            lane_slot = lax.broadcasted_iota(jnp.int32, ids.shape, 0)
            hi = ids & (HI - 1)
            val = jnp.where(lane_slot < live, jnp.left_shift(1, BITS * lax.shift_right_logical(ids, 6)), 0)
            rows = lax.broadcasted_iota(jnp.int32, (HI, 256), 0)
            words = jnp.zeros((HI, 256), jnp.int32)
            for s in range(8):
                words = words + jnp.where(hi[s : s + 1, :] == rows, val[s : s + 1, :], 0)
            wbuf[t, f] = words
            if start:
                table = nt(eye, tab[f]).astype(BF16)
                tab_t[f] = table
            else:
                table = tab_t[f]
            pooled = jnp.dot(table, digits(words), preferred_element_type=F32)
            pbuf[slot, f] = pooled.astype(BF16)
            return carry

        lax.fori_loop(0, n_f, field, 0, unroll=4)
        p_copy(t).start()
        w_copy(t).start()

        def block(eb, carry):
            rows = pl.ds(pl.multiple_of(eb * SUB, SUB), SUB)
            x = pbuf[slot, :, rows, :].reshape(n_f * SUB, 256)
            part = jnp.dot(kron[...], x, preferred_element_type=F32).astype(BF16).reshape(KK, SUB, 256)
            sbuf[t, 0, :, rows, :] = part[:, :, :128]
            sbuf[t, 1, :, rows, :] = part[:, :, 128:]
            return carry

        lax.fori_loop(0, emb // SUB, block, 0, unroll=4)
        if not start:
            core_copy(t).start()

    def add(t, parts, out=None):
        edges = sorted({0, KK, *(e for _, _, a, b in parts for e in (a, b))})
        for low, high in zip(edges, edges[1:]):
            refs = [(r, base) for r, base, a, b in parts if a <= low and high <= b]

            def one(k, carry, refs=refs):
                total = sbuf[t, core, k].astype(F32)
                for r, base in refs:
                    total = total + r[k - base].astype(F32)
                if out is None:
                    sbuf[t, core, k] = total.astype(BF16)
                else:
                    out[k] = total
                return carry

            lax.fori_loop(low, high, one, 0)

    def near(t):
        core_copy(t).wait_recv()
        return (rcore.at[t], 0, 0, KK)

    def share(t):
        share_copy(t).wait_recv()
        return (rshare.at[t], LOW, LOW, KK)

    def opposite(zo):
        add(3 * zo, [near(3 * zo)] + ([share(0)] if zo else []))
        for d in range(2):
            half_copy(zo, d).start()
        if not zo:
            share_copy(0).start()

    def side(zo, d):
        t = 3 * zo + 1 + d
        half_copy(zo, d).wait_recv()
        add(t, [near(t), (rhalf.at[zo], 0, *half_range(zo, d))] + ([share(1 + d)] if zo else []))
        full_copy(zo, d).start()
        if not zo:
            share_copy(t).start()

    def own(zo):
        for d in range(2):
            full_copy(zo, d).wait_recv()
        parts = [near(6 + zo)] + [(rfull.at[zo, d], 0, 0, KK if zo else LOW) for d in range(2)]
        if zo:
            z_copy().wait_recv()
            add(7, parts + [(rz, 0, 0, KK)], fac_out)
        else:
            add(6, parts)
            z_copy().start()

    def span(a, b):
        def step(t, carry):
            compute(t)
            return carry

        lax.fori_loop(a, b, step, 0)

    compute(0, True)
    barrier((other, right, left, across))
    core_copy(0).start()
    opposite(0)
    span(1, 3)
    side(0, 0)
    side(0, 1)
    span(3, 5)
    opposite(1)
    span(5, 7)
    own(0)
    side(1, 0)
    side(1, 1)
    span(7, 8)
    own(1)

    for t in range(8):
        core_copy(t).wait_send()
        w_copy(t).wait()
    for zo in range(2):
        for d in range(2):
            half_copy(zo, d).wait_send()
            full_copy(zo, d).wait_send()
    for t in range(3):
        share_copy(t).wait_send()
    z_copy().wait_send()
    p_copy(6).wait()
    p_copy(7).wait()


def forward(indices, lengths, tables, kron):
    n_f, _, emb = tables.shape
    dma = pltpu.SemaphoreType.DMA
    vmem = pl.BlockSpec(memory_space=pltpu.VMEM)
    hbm = pl.BlockSpec(memory_space=pl.ANY)
    return pl.pallas_call(
        fwd_kernel,
        out_shape=(
            jax.ShapeDtypeStruct((8, n_f, HI, 256), jnp.int32),
            jax.ShapeDtypeStruct((8, n_f, emb, 256), BF16),
            jax.ShapeDtypeStruct((KK, emb, 128), F32),
        ),
        in_specs=[vmem] * 4,
        out_specs=(hbm, hbm, vmem),
        scratch_shapes=[
            pltpu.VMEM((n_f, emb, 8 * HI), BF16),
            pltpu.VMEM((8, 2, KK, emb, 128), BF16),
            pltpu.VMEM((8, KK, emb, 128), BF16),
            pltpu.VMEM((2, KK, emb, 128), BF16),
            pltpu.VMEM((2, 2, KK, emb, 128), BF16),
            pltpu.VMEM((KK, emb, 128), BF16),
            pltpu.VMEM((3, KK - LOW, emb, 128), BF16),
            pltpu.VMEM((8, n_f, HI, 256), jnp.int32),
            pltpu.VMEM((2, n_f, emb, 256), BF16),
            dma((8,)), dma((8,)), dma((2, 2)), dma((2, 2)), dma((2, 2)), dma((2, 2)), dma, dma, dma((3,)), dma((3,)),
            dma((8,)), dma((2,)),
        ],
        compiler_params=pltpu.CompilerParams(collective_id=0, has_side_effects=True, vmem_limit_bytes=VMEM),
        cost_estimate=pl.CostEstimate(flops=15 * 10**9, bytes_accessed=40 * 10**6, transcendentals=0),
    )(indices, lengths, tables, kron)


def dense_kernel(fac, wh, wh_t, wo_col, wo_row, dl, logits, grads, dfac, inter):
    hid, n_feat = wh.shape
    emb = fac.shape[1]
    step = grads.shape[0] * grads.shape[2]

    def left(i, carry):
        a = fac[i]
        for j in range(K2):
            inter[pl.ds(i * K2 + j, 1), :] = jnp.sum(a * fac[K1 + j], axis=0, keepdims=True)
        return carry

    lax.fori_loop(0, K1, left, 0)
    feat = inter[...].astype(BF16)
    row = dl[...]
    n = row.shape[1]
    d0 = row.astype(BF16)
    r1 = row - d0.astype(F32)
    d1 = r1.astype(BF16)
    d2 = (r1 - d1.astype(F32)).astype(BF16)
    sub = lax.broadcasted_iota(jnp.int32, (n_feat, n), 0)
    d_rows = jnp.where(
        sub == 0, d0.astype(F32), jnp.where(sub == 1, d1.astype(F32), jnp.where(sub == 2, d2.astype(F32), 0.0))
    ).astype(BF16)
    nil = jnp.zeros((n_feat, n), BF16)
    feat_low = jnp.concatenate([feat, nil], axis=0)
    d_high = jnp.concatenate([nil, d_rows], axis=0)

    def top(c, carry):
        logit_acc, d_inter = carry
        at = pl.ds(pl.multiple_of(c * step, step), step)
        v = jnp.dot(wh[at, :], feat, preferred_element_type=F32)
        s = jax.nn.sigmoid(v)
        hidden = (v * s).astype(BF16)
        logit_acc = logit_acc + jnp.dot(wo_row[:, at], hidden, preferred_element_type=F32)
        d_hidden = (wo_col[at, :].astype(F32) * row * s * (1.0 + v * (1.0 - s))).astype(BF16)
        grad = nt(d_hidden, feat_low) + nt(hidden, d_high)
        grads[:, pl.ds(c, 1), :, :] = grad.astype(BF16).reshape(grads.shape[0], 1, grads.shape[2], 2 * n_feat)
        d_inter = d_inter + jnp.dot(wh_t[:, at], d_hidden, preferred_element_type=F32)
        return logit_acc, d_inter

    logit_acc, d_inter = lax.fori_loop(
        0, hid // step, top, (jnp.zeros((8, n), F32), jnp.zeros((n_feat, n), F32))
    )
    logits[...] = logit_acc[0:1]
    inter[...] = d_inter

    def back(eb, carry):
        p = lax.div(eb, emb // SUB // 2)
        rows = pl.ds(pl.multiple_of(eb * SUB, SUB), SUB)
        low = pl.ds(pl.multiple_of(lax.rem(eb, emb // SUB // 2) * SUB, SUB), SUB)
        right = [fac[K1 + j, rows, :] for j in range(K2)]
        d_right = [jnp.zeros((SUB, n), F32) for _ in range(K2)]
        for i in range(K1):
            a = fac[i, rows, :]
            d_left = jnp.zeros((SUB, n), F32)
            for j in range(K2):
                g = inter[pl.ds(i * K2 + j, 1), :]
                d_left = d_left + g * right[j]
                d_right[j] = d_right[j] + g * a
            dfac[p, i, low, :] = d_left.astype(BF16)
        for j in range(K2):
            dfac[p, K1 + j, low, :] = d_right[j].astype(BF16)
        return carry

    lax.fori_loop(0, emb // SUB, back, 0)


def dense(fac, w_hidden, w_out, d_logit):
    hid, feat = w_hidden.shape
    n = d_logit.shape[0]
    wo_row = jnp.broadcast_to(w_out[None, :], (8, hid))
    return pl.pallas_call(
        dense_kernel,
        out_shape=(
            jax.ShapeDtypeStruct((1, n), F32),
            jax.ShapeDtypeStruct((16, 8, hid // 128, 2 * feat), BF16),
            jax.ShapeDtypeStruct((2, KK, fac.shape[1] // 2, n), BF16),
        ),
        scratch_shapes=[pltpu.VMEM((feat, n), F32)],
        compiler_params=pltpu.CompilerParams(vmem_limit_bytes=VMEM),
        cost_estimate=pl.CostEstimate(flops=10**9, bytes_accessed=10**7, transcendentals=10**6),
    )(fac, w_hidden, w_hidden.T, w_out[:, None], wo_row, d_logit[None, :])


def bwd_kernel(
    dfac, words, pooled, kron_t, grads,
    tg_out, hid_out, pg_out,
    gbuf, acc, dpool, wbuf, pbuf, tbuf, t_half, t_full, t_z, pg,
    h_core, h_sum, h_half, h_full, h_z, hx_sum, hx_half, hx_full, hx_z, p_x, p_z, p_all,
    own_sem, w_sem, p_sem, core_s, core_r, ici_s, ici_r, half_s, half_r, rest_s, rest_r,
    th_s, th_r, tf_s, tf_r, tz_s, tz_r, gz_s, gz_r, gx_s, gx_r, gh_s, gh_r, h_s, h_r, q_s, q_r,
):
    me, core, y, z, other, right, left, across = peers()
    opposite = {"mp": z * 8 + lax.rem(y + 2, 4) * 2 + core}
    rep = lax.axis_index("replica")
    x = lax.rem(rep, 4)
    zl = lax.div(rep, 4)
    x_to = [None] + [{"replica": zl * 4 + lax.rem(x + d, 4)} for d in (1, 2, 3)]
    x_right, x_left = x_to[1], x_to[3]
    z_near = {"replica": (1 - zl) * 4 + x}
    n_f = tbuf.shape[1]
    width = dpool.shape[1]
    places = ((0, 0), (0, 3), (0, 1), (1, 0), (1, 3), (1, 1), (0, 2), (1, 2))
    order = [(p, n) for p in range(2) for n in (0, 1, 2, 3, 6, 4, 5, 7)]
    sends = []

    def go(copy):
        copy.start()
        sends.append(copy)

    def chip(n):
        dz, dy = places[n]
        return lax.rem(z + dz, 2) * 4 + lax.rem(y + dy, 4)

    def block(n):
        return chip(n) * 2 + core

    def to_core(p, n):
        ref = gbuf.at[p, block(n)]
        return remote(ref, ref, core_s.at[p, n], core_r.at[p, n], other)

    def from_core(p, n):
        ref = gbuf.at[p, chip(n) * 2 + 1 - core]
        remote(ref, ref, core_s.at[p, n], core_r.at[p, n], other).wait_recv()

    def whole(p, n, m, device):
        ref = gbuf.at[p, block(n), pl.ds(0, GATHER_LOW[p] if m in (4, 5) else KK)]
        return remote(ref, ref, ici_s.at[p, m], ici_r.at[p, m], device)

    def arrived(p, m):
        whole(p, m, m, right).wait_recv()

    def half(p, n, m, d):
        cut, top = (K1, KK) if m == 6 else ((GATHER_LOW[p] + 1) // 2, GATHER_LOW[p])
        ref = gbuf.at[p, block(n), pl.ds(cut, top - cut) if d else pl.ds(0, cut)]
        i = (p, m - 6, d)
        return remote(ref, ref, half_s.at[i], half_r.at[i], (right, left)[d])

    def rest(p, n):
        ref = gbuf.at[p, block(n), pl.ds(GATHER_LOW[p], KK - GATHER_LOW[p])]
        i = (1, 2, 6).index(n)
        return remote(ref, ref, rest_s.at[p, i], rest_r.at[p, i], across)

    def rest_arrived(p, m):
        ref = gbuf.at[p, block(m), pl.ds(GATHER_LOW[p], KK - GATHER_LOW[p])]
        i = (4, 5, 7).index(m)
        remote(ref, ref, rest_s.at[p, i], rest_r.at[p, i], across).wait_recv()

    def half_arrived(p, m):
        for d in range(2):
            half(p, m, m, d).wait_recv()
        if m == 6:
            go(rest(p, 6))
        else:
            rest_arrived(p, 7)
        go(to_core(p, m))

    def near(p):
        for d in range(2):
            arrived(p, 1 + d)
            go(half(p, 1 + d, 6, d))
            go(rest(p, 1 + d))
            go(to_core(p, 1 + d))
        arrived(p, 3)
        go(whole(p, 3, 4, right))
        go(whole(p, 3, 5, left))
        go(to_core(p, 3))

    def far(p):
        for d in range(2):
            arrived(p, 4 + d)
            go(half(p, 4 + d, 7, d))
        for d in range(2):
            rest_arrived(p, 4 + d)
            go(to_core(p, 4 + d))

    def w_copy(n):
        return pltpu.make_async_copy(words.at[chip(n)], wbuf.at[n], w_sem.at[n])

    def p_copy(i):
        p, n = order[i]
        return pltpu.make_async_copy(
            pooled.at[chip(n), :, pl.ds(p * width, width), :], pbuf.at[i % 2], p_sem.at[i % 2]
        )

    def work(p, n):
        i = order.index((p, n))
        p_copy(i).wait()
        if i + 1 < len(order):
            p_copy(i + 1).start()
        if p == 0:
            w_copy(n).wait()
        from_core(p, n)
        slot = i % 2
        base = chip(n) * 2

        def spread(eb, carry):
            rows = pl.ds(pl.multiple_of(eb * SUB, SUB), SUB)
            g = jnp.concatenate(
                [gbuf[p, base + c, :, rows, :].reshape(KK * SUB, 128) for c in range(2)], axis=1
            )
            d = jnp.dot(kron_t[...], g, preferred_element_type=F32).astype(BF16)
            dpool[:, rows, :] = d.reshape(n_f, SUB, 256)
            pg[...] += nt(pbuf[slot, :, rows, :].reshape(n_f * SUB, 256), g)
            return carry

        lax.fori_loop(0, width // SUB, spread, 0, unroll=4)

        def field(f, carry):
            part = nt(digits(wbuf[n, f]), dpool[f])
            if n == 0:
                acc[f] = part
            elif n == 7:
                tbuf[p, f] = (acc[f] + part).astype(BF16)
            else:
                acc[f] += part
            return carry

        lax.fori_loop(0, n_f, field, 0, unroll=4)

    def first(dx, zo):
        return (lax.rem(zl + 1 + zo, 2) * 4 + lax.rem(x + dx, 4)) * 2

    def t_half_copy(p, zo, d):
        i = (p, zo, d)
        return remote(tbuf.at[p, first(2, zo) + d], t_half.at[i], th_s.at[i], th_r.at[i], (x_right, x_left)[d])

    def t_full_copy(p, zo, d):
        i = (p, zo, d)
        src = tbuf.at[p, pl.ds(first(1 + 2 * d, zo), 2)]
        return remote(src, t_full.at[i], tf_s.at[i], tf_r.at[i], (x_right, x_left)[d])

    def t_z_copy(p):
        return remote(tbuf.at[p, pl.ds(first(0, 0), 2)], t_z.at[p], tz_s.at[p], tz_r.at[p], z_near)

    def g_x_copy(p, zb, d, dx=0):
        ref = tg_out.at[p, pl.ds(first(dx, 1 - zb), 2)]
        i = (p, zb, d)
        return remote(ref, ref, gx_s.at[i], gx_r.at[i], (x_right, x_left)[d])

    def g_z_copy(p, zb):
        ref = tg_out.at[p, pl.ds(first(0, 1 - zb), 2)]
        return remote(ref, ref, gz_s.at[p], gz_r.at[p], z_near)

    def g_half_copy(p, zb, d, dx):
        ref = tg_out.at[p, first(dx, 1 - zb) + d]
        i = (p, zb, d)
        return remote(ref, ref, gh_s.at[i], gh_r.at[i], (x_right, x_left)[d])

    def t_start(p):
        for zo in range(2):
            for d in range(2):
                go(t_half_copy(p, zo, d))

    def t_pass(p, zo):
        for d in range(2):
            t_half_copy(p, zo, d).wait_recv()
            at = first(1 + 2 * d, zo) + d
            tbuf[p, at] = (tbuf[p, at].astype(F32) + t_half[p, zo, d].astype(F32)).astype(BF16)
            go(t_full_copy(p, zo, d))

    def t_total(p, zo, k):
        total = tbuf[p, first(0, zo) + k].astype(F32)
        return total + t_full[p, zo, 0, k].astype(F32) + t_full[p, zo, 1, k].astype(F32)

    def t_cross(p):
        for d in range(2):
            t_full_copy(p, 0, d).wait_recv()
        for k in range(2):
            tbuf[p, first(0, 0) + k] = t_total(p, 0, k).astype(BF16)
        go(t_z_copy(p))

    def t_finish(p):
        for d in range(2):
            t_full_copy(p, 1, d).wait_recv()
        t_z_copy(p).wait_recv()
        for k in range(2):
            tg_out[p, first(0, 1) + k] = (t_total(p, 1, k) + t_z[p, k].astype(F32)).astype(BF16)
        go(g_z_copy(p, 0))
        for d in range(2):
            go(g_x_copy(p, 0, d))

    def t_spread(p):
        g_z_copy(p, 1).wait_recv()
        for d in range(2):
            go(g_x_copy(p, 1, d))

    def t_relay(p, zb):
        for d in range(2):
            dx = 3 - 2 * d
            g_x_copy(p, zb, d, dx).wait_recv()
            go(g_half_copy(p, zb, d, dx))

    def t_last(p):
        for zb in range(2):
            for d in range(2):
                g_half_copy(p, zb, d, 2).wait_recv()

    def h_copy(i):
        if i == 0:
            src, dst, to = grads.at[:, 1 - core], h_core, other
        elif i < 3:
            d = i - 1
            src, dst, to = h_sum.at[:, lax.rem(y + 2, 4), pl.ds(d * 128, 128)], h_half.at[d], (right, left)[d]
        elif i < 5:
            d = i - 3
            src, dst, to = h_sum.at[:, lax.rem(y + 1 + 2 * d, 4)], h_full.at[d], (right, left)[d]
        elif i == 5:
            src, dst, to = h_sum.at[1 - z, y], h_z, across
        elif i < 8:
            d = i - 6
            src, dst, to = hx_sum.at[:, lax.rem(x + 2, 4), pl.ds(d * 16, 16)], hx_half.at[d], (x_right, x_left)[d]
        elif i < 10:
            d = i - 8
            src, dst, to = hx_sum.at[:, lax.rem(x + 1 + 2 * d, 4)], hx_full.at[d], (x_right, x_left)[d]
        else:
            src, dst, to = hx_sum.at[1 - zl, x], hx_z, z_near
        return remote(src, dst, h_s.at[i], h_r.at[i], to)

    def wide(v):
        return v.astype(F32)

    def h1():
        h_copy(0).wait_recv()
        for q in range(8):
            total = wide(grads[q, core]) + wide(h_core[q])
            h_sum[q // 4, q % 4] = total.astype(BF16).reshape(h_sum.shape[2:])
        go(h_copy(1))
        go(h_copy(2))

    def h2():
        for d in range(2):
            h_copy(1 + d).wait_recv()
            at, rows = lax.rem(y + 1 + 2 * d, 4), pl.ds(d * 128, 128)
            for k in range(2):
                h_sum[k, at, rows] = (wide(h_sum[k, at, rows]) + wide(h_half[d, k])).astype(BF16)
            go(h_copy(3 + d))

    def h3():
        for d in range(2):
            h_copy(3 + d).wait_recv()
        for k in range(2):
            h_sum[k, y] = (wide(h_sum[k, y]) + wide(h_full[0, k]) + wide(h_full[1, k])).astype(BF16)
        go(h_copy(5))

    def h4():
        h_copy(5).wait_recv()
        total = (wide(h_sum[z, y]) + wide(h_z[...])).astype(BF16).reshape(8, 32, 128)
        for q in range(8):
            hx_sum[q // 4, q % 4] = total[q]
        go(h_copy(6))
        go(h_copy(7))

    def h5():
        for d in range(2):
            h_copy(6 + d).wait_recv()
            at, rows = lax.rem(x + 1 + 2 * d, 4), pl.ds(d * 16, 16)
            for k in range(2):
                hx_sum[k, at, rows] = (wide(hx_sum[k, at, rows]) + wide(hx_half[d, k])).astype(BF16)
            go(h_copy(8 + d))

    def h6():
        for d in range(2):
            h_copy(8 + d).wait_recv()
        for k in range(2):
            hx_sum[k, x] = (wide(hx_sum[k, x]) + wide(hx_full[0, k]) + wide(hx_full[1, k])).astype(BF16)
        go(h_copy(10))

    def h7():
        h_copy(10).wait_recv()
        hid_out[...] = wide(hx_sum[zl, x]) + wide(hx_z[...])

    def q_copy(i):
        if i < 3:
            src, dst, to = p_x.at[3], p_x.at[i], x_to[1 + i]
        elif i == 3:
            src, dst, to = p_z.at[0], p_z.at[1], z_near
        elif i == 4:
            ref = p_all.at[z, y, core]
            src, dst, to = ref, ref, other
        elif i < 8:
            ref = p_all.at[z, y]
            src, dst, to = ref, ref, (right, opposite, left)[i - 5]
        else:
            ref = p_all.at[z]
            src, dst, to = ref, ref, across
        return remote(src, dst, q_s.at[i], q_r.at[i], to)

    def q0():
        a = lax.rem(lax.broadcasted_iota(jnp.int32, pg.shape, 0), SUB)
        b = lax.rem(lax.broadcasted_iota(jnp.int32, pg.shape, 1), SUB)
        p_x[3] = jnp.sum(jnp.where(a == b, pg[...], 0.0).reshape(n_f, SUB, KK * SUB), axis=1)
        for i in range(3):
            go(q_copy(i))

    def q1():
        for i in range(3):
            q_copy(i).wait_recv()
        p_z[0] = p_x[0] + p_x[1] + p_x[2] + p_x[3]
        go(q_copy(3))

    def q2():
        q_copy(3).wait_recv()
        p_all[z, y, core] = p_z[0] + p_z[1]
        go(q_copy(4))

    def q3():
        ref = p_all.at[z, y, 1 - core]
        remote(ref, ref, q_s.at[4], q_r.at[4], other).wait_recv()
        for i in range(3):
            go(q_copy(5 + i))

    def q4():
        for i in range(3):
            ref = p_all.at[z, lax.rem(y + 3 - i, 4)]
            remote(ref, ref, q_s.at[5 + i], q_r.at[5 + i], right).wait_recv()
        go(q_copy(8))

    def q5():
        ref = p_all.at[1 - z]
        remote(ref, ref, q_s.at[8], q_r.at[8], across).wait_recv()
        j = 2 * rep + lax.div(me, 8)
        pg_out[...] = p_all[lax.div(j, 8), lax.rem(lax.div(j, 2), 4), lax.rem(j, 2)]

    own = [pltpu.make_async_copy(dfac.at[p], gbuf.at[p, me], own_sem.at[p]) for p in range(2)]
    for c in own:
        c.start()
    p_copy(0).start()
    for _, n in order[:8]:
        w_copy(n).start()
    pg[...] = jnp.zeros_like(pg)
    barrier((other, right, left, opposite, across, x_to[1], x_to[2], x_to[3], z_near))
    own[0].wait()
    go(whole(0, 0, 1, right))
    go(whole(0, 0, 2, left))
    go(whole(0, 0, 3, across))
    go(to_core(0, 0))
    go(h_copy(0))
    own[1].wait()
    go(to_core(1, 0))
    work(0, 0)
    h1()
    near(0)
    go(whole(1, 0, 3, across))
    work(0, 1)
    h2()
    work(0, 2)
    work(0, 3)
    h3()
    half_arrived(0, 6)
    work(0, 6)
    h4()
    far(0)
    work(0, 4)
    h5()
    work(0, 5)
    half_arrived(0, 7)
    go(whole(1, 0, 1, right))
    go(whole(1, 0, 2, left))
    work(0, 7)
    t_start(0)
    h6()
    work(1, 0)
    t_pass(0, 0)
    near(1)
    t_pass(0, 1)
    work(1, 1)
    t_cross(0)
    work(1, 2)
    h7()
    work(1, 3)
    t_finish(0)
    half_arrived(1, 6)
    work(1, 6)
    t_spread(0)
    far(1)
    t_relay(0, 0)
    work(1, 4)
    work(1, 5)
    t_relay(0, 1)
    half_arrived(1, 7)
    work(1, 7)
    t_start(1)
    t_last(0)
    q0()
    t_pass(1, 0)
    t_pass(1, 1)
    q1()
    q2()
    t_cross(1)
    q3()
    t_finish(1)
    q4()
    t_spread(1)
    t_relay(1, 0)
    q5()
    t_relay(1, 1)
    t_last(1)
    for s in sends:
        s.wait_send()


def backward(dfac, words, pooled, kron_t, grads):
    _, n_f, emb, _ = pooled.shape
    rows = 8 * HI
    width = emb // 2
    n_grad = grads.shape[2]
    grads = grads.reshape(8, 2, 8, n_grad, 128)
    dma = pltpu.SemaphoreType.DMA
    vmem = pl.BlockSpec(memory_space=pltpu.VMEM)
    hbm = pl.BlockSpec(memory_space=pl.ANY)
    a222 = dma((2, 2, 2))
    return pl.pallas_call(
        bwd_kernel,
        out_shape=(
            jax.ShapeDtypeStruct((2, n_f, rows, width), BF16),
            jax.ShapeDtypeStruct((n_grad, 128), F32),
            jax.ShapeDtypeStruct((n_f, KK * SUB), F32),
        ),
        in_specs=[vmem, hbm, hbm, vmem, vmem],
        out_specs=(vmem, vmem, vmem),
        scratch_shapes=[
            pltpu.VMEM((2, 16, KK, width, 128), BF16),
            pltpu.VMEM((n_f, rows, width), F32),
            pltpu.VMEM((n_f, width, 256), BF16),
            pltpu.VMEM((8, n_f, HI, 256), jnp.int32),
            pltpu.VMEM((2, n_f, width, 256), BF16),
            pltpu.VMEM((2, n_f, rows, width), BF16),
            pltpu.VMEM((2, 2, 2, rows, width), BF16),
            pltpu.VMEM((2, 2, 2, 2, rows, width), BF16),
            pltpu.VMEM((2, 2, rows, width), BF16),
            pltpu.VMEM((n_f * SUB, KK * SUB), F32),
            pltpu.VMEM((8, 8, n_grad, 128), BF16),
            pltpu.VMEM((2, 4, 8 * n_grad, 128), BF16),
            pltpu.VMEM((2, 2, 4 * n_grad, 128), BF16),
            pltpu.VMEM((2, 2, 8 * n_grad, 128), BF16),
            pltpu.VMEM((8 * n_grad, 128), BF16),
            pltpu.VMEM((2, 4, n_grad, 128), BF16),
            pltpu.VMEM((2, 2, n_grad // 2, 128), BF16),
            pltpu.VMEM((2, 2, n_grad, 128), BF16),
            pltpu.VMEM((n_grad, 128), BF16),
            pltpu.VMEM((4, n_f, KK * SUB), F32),
            pltpu.VMEM((2, n_f, KK * SUB), F32),
            pltpu.VMEM((2, 4, 2, n_f, KK * SUB), F32),
            dma((2,)), dma((8,)), dma((2,)), dma((2, 8)), dma((2, 8)), dma((2, 6)), dma((2, 6)), a222, a222,
            dma((2, 3)), dma((2, 3)),
            a222, a222, a222, a222, dma((2,)), dma((2,)), dma((2,)), dma((2,)), a222, a222, a222, a222,
            dma((11,)), dma((11,)), dma((9,)), dma((9,)),
        ],
        compiler_params=pltpu.CompilerParams(collective_id=1, has_side_effects=True, vmem_limit_bytes=VMEM),
        cost_estimate=pl.CostEstimate(flops=20 * 10**9, bytes_accessed=40 * 10**6, transcendentals=0),
    )(dfac, words, pooled, kron_t, grads)


def local(indices, lengths, tables, proj, w_hidden, w_out, d_logit):
    n_f = indices.shape[0]
    me = lax.axis_index("mp")
    here = lax.dynamic_slice_in_dim(proj, me * n_f, n_f, 0)
    eye = jnp.eye(SUB, dtype=BF16)
    kron_t = (here[:, None, :, None] * eye[None, :, None, :]).reshape(n_f * SUB, KK * SUB)
    words, pooled, fac = forward(indices, lengths, tables, kron_t.T)
    logits, grads, dfac = dense(fac, w_hidden, w_out, d_logit)
    tables_sum, dense_sum, pg = backward(dfac, words, pooled, kron_t, grads)
    table_grad = jnp.concatenate([tables_sum[0], tables_sum[1]], axis=2).astype(F32)
    feat = w_hidden.shape[1]
    mine = proj.shape[0] // 128
    pg = lax.dynamic_slice_in_dim(pg, lax.rem(me * mine, n_f), mine, 0)
    return (
        logits.reshape(-1),
        table_grad,
        dense_sum[:, :feat],
        dense_sum[:, feat : feat + 3].sum(1),
        pg.reshape(mine, KK, SUB).sum(2),
    )


def solution(mesh):
    in_specs = (
        P("mp", None, "replica"),
        P("mp", "replica"),
        P("mp", None, None),
        P(),
        P(),
        P(),
        P(("replica", "mp")),
    )
    out_specs = (
        P(("replica", "mp")),
        P("mp", None, None),
        P(("replica", "mp"), None),
        P(("replica", "mp")),
        P(("replica", "mp"), None),
    )
    return jax.shard_map(local, mesh=mesh, in_specs=in_specs, out_specs=out_specs, check_vma=False)
```

```python
import functools

import jax
import jax.numpy as jnp
from jax import lax
from jax.experimental import pallas as pl
from jax.experimental.pallas import tpu as pltpu
from jax.sharding import PartitionSpec as P

MESH = pl.DeviceIdType.MESH
K1 = 8
K2 = 8
KK = K1 + K2
SUB = 16
HI = 64
BITS = 4
VMEM = 60 * 1024 * 1024
LOW = 9
LOW_HALF = 5
GATHER_LOW = (9, 12)
F32 = jnp.float32
BF16 = jnp.bfloat16


def peers():
    me = lax.axis_index("mp")
    core = lax.rem(me, 2)
    y = lax.rem(lax.div(me, 2), 4)
    z = lax.div(me, 8)
    other = {"mp": me + 1 - 2 * core}
    right = {"mp": z * 8 + lax.rem(y + 1, 4) * 2 + core}
    left = {"mp": z * 8 + lax.rem(y + 3, 4) * 2 + core}
    across = {"mp": (1 - z) * 8 + y * 2 + core}
    return me, core, y, z, other, right, left, across


def barrier(devices):
    sem = pltpu.get_barrier_semaphore()
    for d in devices:
        pl.semaphore_signal(sem, inc=1, device_id=d, device_id_type=MESH)
    pl.semaphore_wait(sem, len(devices))


def remote(src, dst, send, recv, device):
    return pltpu.make_async_remote_copy(
        src_ref=src, dst_ref=dst, send_sem=send, recv_sem=recv, device_id=device, device_id_type=MESH
    )


def digits(words):
    return jnp.concatenate(
        [(lax.shift_right_logical(words, BITS * d) & 15).astype(F32).astype(BF16) for d in range(8)], axis=0
    )


def nt(a, b):
    return lax.dot_general(a, b, (((1,), (1,)), ((), ())), preferred_element_type=F32)


def tn(a, b):
    return lax.dot_general(a, b, (((0,), (0,)), ((), ())), preferred_element_type=F32)


def spread_out(here, flip):
    n = here.shape[0] * SUB
    owner = lax.div(lax.broadcasted_iota(jnp.int32, (n, KK), 0), SUB)
    pick = (owner == lax.broadcasted_iota(jnp.int32, (n, KK), 1)).astype(F32).astype(BF16)
    rows = (nt(pick, here) if flip else jnp.dot(pick, here, preferred_element_type=F32)).astype(BF16)
    full = nt(rows, pick)
    a = lax.rem(lax.broadcasted_iota(jnp.int32, (n, n), 0), SUB)
    b = lax.rem(lax.broadcasted_iota(jnp.int32, (n, n), 1), SUB)
    return jnp.where(a == b, full, 0.0).astype(BF16)


def fwd_kernel(
    idx, lens, tab, proj, words_out, pooled_out, fac_out,
    kron, tab_t, sbuf, rcore, rhalf, rfull, rz, rshare, wbuf, pbuf,
    core_s, core_r, half_s, half_r, full_s, full_r, z_s, z_r, share_s, share_r, w_sem, p_sem,
):
    me, core, y, z, other, right, left, across = peers()
    n_f = idx.shape[0]
    emb = tab.shape[2]

    def chunk_of(t):
        u = lax.rem(t, 3)
        early = lax.div(7 - t, 2) > 0
        dy = jnp.where(early, jnp.where(u == 0, 2, 2 * u - 1), 0)
        zo = jnp.where(early, lax.div(t, 3), t - 6)
        return lax.rem(z + 1 + zo, 2) * 4 + lax.rem(y + dy, 4)

    def p_copy(t):
        slot = lax.rem(t, 2)
        return pltpu.make_async_copy(pbuf.at[slot], pooled_out.at[chunk_of(t)], p_sem.at[slot])

    def w_copy(t):
        return pltpu.make_async_copy(wbuf.at[t], words_out.at[chunk_of(t)], w_sem.at[t])

    def core_copy(t):
        return remote(sbuf.at[t, 1 - core], rcore.at[t], core_s.at[t], core_r.at[t], other)

    def half_range(zo, d):
        if zo:
            return d * K1, d * K1 + K1
        return (0, LOW_HALF) if d == 0 else (LOW_HALF, LOW)

    def half_copy(zo, d):
        a, b = half_range(zo, d)
        ks = pl.ds(a, b - a)
        return remote(
            sbuf.at[3 * zo, core, ks], rhalf.at[zo, ks], half_s.at[zo, d], half_r.at[zo, d], (right, left)[d]
        )

    def full_copy(zo, d):
        ks = pl.ds(0, KK if zo else LOW)
        return remote(
            sbuf.at[3 * zo + 1 + d, core, ks], rfull.at[zo, d, ks], full_s.at[zo, d], full_r.at[zo, d], (right, left)[d]
        )

    def share_copy(t):
        return remote(sbuf.at[t, core, pl.ds(LOW, KK - LOW)], rshare.at[t], share_s.at[t], share_r.at[t], across)

    def z_copy():
        return remote(sbuf.at[6, core], rz, z_s, z_r, across)

    def compute(t, start=False):
        q = chunk_of(t)
        slot = lax.rem(t, 2)
        where = pl.ds(pl.multiple_of(q * 256, 256), 256)
        if not start:

            @pl.when(t >= 2)
            def _():
                p_copy(t - 2).wait()

        else:
            eye = (
                lax.broadcasted_iota(jnp.int32, (emb, emb), 0) == lax.broadcasted_iota(jnp.int32, (emb, emb), 1)
            ).astype(F32).astype(BF16)

        def field(f, carry):
            ids = idx[f, :, where]
            live = lens[pl.ds(f, 1), where]
            lane_slot = lax.broadcasted_iota(jnp.int32, ids.shape, 0)
            hi = ids & (HI - 1)
            val = jnp.where(lane_slot < live, jnp.left_shift(1, BITS * lax.shift_right_logical(ids, 6)), 0)
            rows = lax.broadcasted_iota(jnp.int32, (HI, 256), 0)
            words = jnp.zeros((HI, 256), jnp.int32)
            for s in range(8):
                words = words + jnp.where(hi[s : s + 1, :] == rows, val[s : s + 1, :], 0)
            wbuf[t, f] = words
            if start:
                table = nt(eye, tab[f]).astype(BF16)
                tab_t[f] = table
            else:
                table = tab_t[f]
            pooled = jnp.dot(table, digits(words), preferred_element_type=F32)
            pbuf[slot, f] = pooled.astype(BF16)
            return carry

        lax.fori_loop(0, n_f, field, 0, unroll=4)
        p_copy(t).start()
        w_copy(t).start()

        def block(eb, carry):
            rows = pl.ds(pl.multiple_of(eb * SUB, SUB), SUB)
            x = pbuf[slot, :, rows, :].reshape(n_f * SUB, 256)
            part = jnp.dot(kron[...], x, preferred_element_type=F32).astype(BF16).reshape(KK, SUB, 256)
            sbuf[t, 0, :, rows, :] = part[:, :, :128]
            sbuf[t, 1, :, rows, :] = part[:, :, 128:]
            return carry

        lax.fori_loop(0, emb // SUB, block, 0, unroll=4)
        if not start:
            core_copy(t).start()

    def add(t, parts, out=None):
        edges = sorted({0, KK, *(e for _, _, a, b in parts for e in (a, b))})
        for low, high in zip(edges, edges[1:]):
            refs = [(r, base) for r, base, a, b in parts if a <= low and high <= b]

            def one(k, carry, refs=refs):
                total = sbuf[t, core, k].astype(F32)
                for r, base in refs:
                    total = total + r[k - base].astype(F32)
                if out is None:
                    sbuf[t, core, k] = total.astype(BF16)
                else:
                    out[k] = total
                return carry

            lax.fori_loop(low, high, one, 0)

    def near(t):
        core_copy(t).wait_recv()
        return (rcore.at[t], 0, 0, KK)

    def share(t):
        share_copy(t).wait_recv()
        return (rshare.at[t], LOW, LOW, KK)

    def opposite(zo):
        add(3 * zo, [near(3 * zo)] + ([share(0)] if zo else []))
        for d in range(2):
            half_copy(zo, d).start()
        if not zo:
            share_copy(0).start()

    def side(zo, d):
        t = 3 * zo + 1 + d
        half_copy(zo, d).wait_recv()
        add(t, [near(t), (rhalf.at[zo], 0, *half_range(zo, d))] + ([share(1 + d)] if zo else []))
        full_copy(zo, d).start()
        if not zo:
            share_copy(t).start()

    def own(zo):
        for d in range(2):
            full_copy(zo, d).wait_recv()
        parts = [near(6 + zo)] + [(rfull.at[zo, d], 0, 0, KK if zo else LOW) for d in range(2)]
        if zo:
            z_copy().wait_recv()
            add(7, parts + [(rz, 0, 0, KK)], fac_out)
        else:
            add(6, parts)
            z_copy().start()

    def span(a, b):
        def step(t, carry):
            compute(t)
            return carry

        lax.fori_loop(a, b, step, 0)

    kron[...] = spread_out(proj[pl.ds(pl.multiple_of(me * n_f, n_f), n_f), :], True)
    compute(0, True)
    barrier((other, right, left, across))
    core_copy(0).start()
    opposite(0)
    span(1, 3)
    side(0, 0)
    side(0, 1)
    span(3, 5)
    opposite(1)
    span(5, 7)
    own(0)
    side(1, 0)
    side(1, 1)
    span(7, 8)
    own(1)

    for t in range(8):
        core_copy(t).wait_send()
        w_copy(t).wait()
    for zo in range(2):
        for d in range(2):
            half_copy(zo, d).wait_send()
            full_copy(zo, d).wait_send()
    for t in range(3):
        share_copy(t).wait_send()
    z_copy().wait_send()
    p_copy(6).wait()
    p_copy(7).wait()


def forward(indices, lengths, tables, proj):
    n_f, _, emb = tables.shape
    dma = pltpu.SemaphoreType.DMA
    vmem = pl.BlockSpec(memory_space=pltpu.VMEM)
    hbm = pl.BlockSpec(memory_space=pl.ANY)
    return pl.pallas_call(
        fwd_kernel,
        out_shape=(
            jax.ShapeDtypeStruct((8, n_f, HI, 256), jnp.int32),
            jax.ShapeDtypeStruct((8, n_f, emb, 256), BF16),
            jax.ShapeDtypeStruct((KK, emb, 128), F32),
        ),
        in_specs=[vmem] * 4,
        out_specs=(hbm, hbm, vmem),
        scratch_shapes=[
            pltpu.VMEM((n_f * SUB, KK * SUB), BF16),
            pltpu.VMEM((n_f, emb, 8 * HI), BF16),
            pltpu.VMEM((8, 2, KK, emb, 128), BF16),
            pltpu.VMEM((8, KK, emb, 128), BF16),
            pltpu.VMEM((2, KK, emb, 128), BF16),
            pltpu.VMEM((2, 2, KK, emb, 128), BF16),
            pltpu.VMEM((KK, emb, 128), BF16),
            pltpu.VMEM((3, KK - LOW, emb, 128), BF16),
            pltpu.VMEM((8, n_f, HI, 256), jnp.int32),
            pltpu.VMEM((2, n_f, emb, 256), BF16),
            dma((8,)), dma((8,)), dma((2, 2)), dma((2, 2)), dma((2, 2)), dma((2, 2)), dma, dma, dma((3,)), dma((3,)),
            dma((8,)), dma((2,)),
        ],
        compiler_params=pltpu.CompilerParams(collective_id=0, has_side_effects=True, vmem_limit_bytes=VMEM),
        cost_estimate=pl.CostEstimate(flops=15 * 10**9, bytes_accessed=40 * 10**6, transcendentals=0),
    )(indices, lengths, tables, proj)


def dense_kernel(fac, wh_t, wo_row, dl, logits, grads, dfac, inter):
    n_feat, hid = wh_t.shape
    emb = fac.shape[1]
    step = grads.shape[0] * grads.shape[2]

    def left(i, carry):
        a = fac[i]
        for j in range(K2):
            inter[pl.ds(i * K2 + j, 1), :] = jnp.sum(a * fac[K1 + j], axis=0, keepdims=True)
        return carry

    lax.fori_loop(0, K1, left, 0)
    feat = inter[...].astype(BF16)
    row = dl[...]
    n = row.shape[1]
    d0 = row.astype(BF16)
    r1 = row - d0.astype(F32)
    d1 = r1.astype(BF16)
    d2 = (r1 - d1.astype(F32)).astype(BF16)
    sub = lax.broadcasted_iota(jnp.int32, (n_feat, n), 0)
    d_rows = jnp.where(
        sub == 0, d0.astype(F32), jnp.where(sub == 1, d1.astype(F32), jnp.where(sub == 2, d2.astype(F32), 0.0))
    ).astype(BF16)
    nil = jnp.zeros((n_feat, n), BF16)
    feat_low = jnp.concatenate([feat, nil], axis=0)
    d_high = jnp.concatenate([nil, d_rows], axis=0)
    ones = jnp.ones((8, n), BF16)

    def top(c, carry):
        logit_acc, d_inter = carry
        at = pl.ds(pl.multiple_of(c * step, step), step)
        w = wh_t[:, at]
        v = tn(w, feat)
        wo = jnp.broadcast_to(wo_row[:, at].astype(F32), (8, step))
        top_row = lax.broadcasted_iota(jnp.int32, (8, step), 0) == 0
        wo_cols = tn(jnp.where(top_row, wo, 0.0).astype(BF16), ones)
        s = jax.nn.sigmoid(v)
        hidden = (v * s).astype(BF16)
        logit_acc = logit_acc + jnp.dot(wo.astype(BF16), hidden, preferred_element_type=F32)
        d_hidden = (wo_cols * row * s * (1.0 + v * (1.0 - s))).astype(BF16)
        grad = nt(d_hidden, feat_low) + nt(hidden, d_high)
        grads[:, pl.ds(c, 1), :, :] = grad.astype(BF16).reshape(grads.shape[0], 1, grads.shape[2], 2 * n_feat)
        d_inter = d_inter + jnp.dot(w, d_hidden, preferred_element_type=F32)
        return logit_acc, d_inter

    logit_acc, d_inter = lax.fori_loop(
        0, hid // step, top, (jnp.zeros((8, n), F32), jnp.zeros((n_feat, n), F32))
    )
    logits[...] = logit_acc[0:1]
    inter[...] = d_inter

    def back(eb, carry):
        p = lax.div(eb, emb // SUB // 2)
        rows = pl.ds(pl.multiple_of(eb * SUB, SUB), SUB)
        low = pl.ds(pl.multiple_of(lax.rem(eb, emb // SUB // 2) * SUB, SUB), SUB)
        right = [fac[K1 + j, rows, :] for j in range(K2)]
        d_right = [jnp.zeros((SUB, n), F32) for _ in range(K2)]
        for i in range(K1):
            a = fac[i, rows, :]
            d_left = jnp.zeros((SUB, n), F32)
            for j in range(K2):
                g = inter[pl.ds(i * K2 + j, 1), :]
                d_left = d_left + g * right[j]
                d_right[j] = d_right[j] + g * a
            dfac[p, i, low, :] = d_left.astype(BF16)
        for j in range(K2):
            dfac[p, K1 + j, low, :] = d_right[j].astype(BF16)
        return carry

    lax.fori_loop(0, emb // SUB, back, 0)


def dense(fac, w_hidden, w_out, d_logit):
    hid, feat = w_hidden.shape
    n = d_logit.shape[0]
    return pl.pallas_call(
        dense_kernel,
        out_shape=(
            jax.ShapeDtypeStruct((1, n), F32),
            jax.ShapeDtypeStruct((16, 8, hid // 128, 2 * feat), BF16),
            jax.ShapeDtypeStruct((2, KK, fac.shape[1] // 2, n), BF16),
        ),
        scratch_shapes=[pltpu.VMEM((feat, n), F32)],
        compiler_params=pltpu.CompilerParams(vmem_limit_bytes=VMEM),
        cost_estimate=pl.CostEstimate(flops=10**9, bytes_accessed=10**7, transcendentals=10**6),
    )(fac, w_hidden.T, w_out[None, :], d_logit[None, :])


def bwd_kernel(
    dfac, words, pooled, proj, grads,
    tg_low, tg_high, hid_out, pg_out,
    kron_t, gbuf, acc, dpool, wbuf, pbuf, tbuf, t_half, t_full, t_z, pg,
    h_core, h_sum, h_half, h_full, h_z, hx_sum, hx_half, hx_full, hx_z, p_x, p_z, p_all,
    own_sem, w_sem, p_sem, core_s, core_r, ici_s, ici_r, half_s, half_r, rest_s, rest_r,
    th_s, th_r, tf_s, tf_r, tz_s, tz_r, gz_s, gz_r, gx_s, gx_r, gh_s, gh_r, h_s, h_r, q_s, q_r,
):
    me, core, y, z, other, right, left, across = peers()
    opposite = {"mp": z * 8 + lax.rem(y + 2, 4) * 2 + core}
    rep = lax.axis_index("replica")
    x = lax.rem(rep, 4)
    zl = lax.div(rep, 4)
    x_to = [None] + [{"replica": zl * 4 + lax.rem(x + d, 4)} for d in (1, 2, 3)]
    x_right, x_left = x_to[1], x_to[3]
    z_near = {"replica": (1 - zl) * 4 + x}
    n_f = tbuf.shape[1]
    width = dpool.shape[1]
    places = ((0, 0), (0, 3), (0, 1), (1, 0), (1, 3), (1, 1), (0, 2), (1, 2))
    order = [(p, n) for p in range(2) for n in (0, 1, 2, 3, 6, 4, 5, 7)]
    sends = []
    tg_out = (tg_low, tg_high)

    def go(copy):
        copy.start()
        sends.append(copy)

    def chip(n):
        dz, dy = places[n]
        return lax.rem(z + dz, 2) * 4 + lax.rem(y + dy, 4)

    def block(n):
        return chip(n) * 2 + core

    def to_core(p, n):
        ref = gbuf.at[p, block(n)]
        return remote(ref, ref, core_s.at[p, n], core_r.at[p, n], other)

    def from_core(p, n):
        ref = gbuf.at[p, chip(n) * 2 + 1 - core]
        remote(ref, ref, core_s.at[p, n], core_r.at[p, n], other).wait_recv()

    def whole(p, n, m, device):
        ref = gbuf.at[p, block(n), pl.ds(0, GATHER_LOW[p] if m in (4, 5) else KK)]
        return remote(ref, ref, ici_s.at[p, m], ici_r.at[p, m], device)

    def arrived(p, m):
        whole(p, m, m, right).wait_recv()

    def half(p, n, m, d):
        cut, top = (K1, KK) if m == 6 else ((GATHER_LOW[p] + 1) // 2, GATHER_LOW[p])
        ref = gbuf.at[p, block(n), pl.ds(cut, top - cut) if d else pl.ds(0, cut)]
        i = (p, m - 6, d)
        return remote(ref, ref, half_s.at[i], half_r.at[i], (right, left)[d])

    def rest(p, n):
        ref = gbuf.at[p, block(n), pl.ds(GATHER_LOW[p], KK - GATHER_LOW[p])]
        i = (1, 2, 6).index(n)
        return remote(ref, ref, rest_s.at[p, i], rest_r.at[p, i], across)

    def rest_arrived(p, m):
        ref = gbuf.at[p, block(m), pl.ds(GATHER_LOW[p], KK - GATHER_LOW[p])]
        i = (4, 5, 7).index(m)
        remote(ref, ref, rest_s.at[p, i], rest_r.at[p, i], across).wait_recv()

    def half_arrived(p, m):
        for d in range(2):
            half(p, m, m, d).wait_recv()
        if m == 6:
            go(rest(p, 6))
        else:
            rest_arrived(p, 7)
        go(to_core(p, m))

    def near(p):
        for d in range(2):
            arrived(p, 1 + d)
            go(half(p, 1 + d, 6, d))
            go(rest(p, 1 + d))
            go(to_core(p, 1 + d))
        arrived(p, 3)
        go(whole(p, 3, 4, right))
        go(whole(p, 3, 5, left))
        go(to_core(p, 3))

    def far(p):
        for d in range(2):
            arrived(p, 4 + d)
            go(half(p, 4 + d, 7, d))
        for d in range(2):
            rest_arrived(p, 4 + d)
            go(to_core(p, 4 + d))

    def w_copy(n):
        return pltpu.make_async_copy(words.at[chip(n)], wbuf.at[n], w_sem.at[n])

    def p_copy(i):
        p, n = order[i]
        return pltpu.make_async_copy(
            pooled.at[chip(n), :, pl.ds(p * width, width), :], pbuf.at[i % 2], p_sem.at[i % 2]
        )

    def work(p, n):
        i = order.index((p, n))
        p_copy(i).wait()
        if i + 1 < len(order):
            p_copy(i + 1).start()
        if p == 0:
            w_copy(n).wait()
        from_core(p, n)
        slot = i % 2
        base = chip(n) * 2

        def spread(eb, carry):
            rows = pl.ds(pl.multiple_of(eb * SUB, SUB), SUB)
            g = jnp.concatenate(
                [gbuf[p, base + c, :, rows, :].reshape(KK * SUB, 128) for c in range(2)], axis=1
            )
            d = jnp.dot(kron_t[...], g, preferred_element_type=F32).astype(BF16)
            dpool[:, rows, :] = d.reshape(n_f, SUB, 256)
            pg[...] += nt(pbuf[slot, :, rows, :].reshape(n_f * SUB, 256), g)
            return carry

        lax.fori_loop(0, width // SUB, spread, 0, unroll=4)

        def field(f, carry):
            part = nt(digits(wbuf[n, f]), dpool[f])
            if n == 0:
                acc[f] = part
            elif n == 7:
                tbuf[p, f] = (acc[f] + part).astype(BF16)
            else:
                acc[f] += part
            return carry

        lax.fori_loop(0, n_f, field, 0, unroll=4)

    def first(dx, zo):
        return (lax.rem(zl + 1 + zo, 2) * 4 + lax.rem(x + dx, 4)) * 2

    def t_half_copy(p, zo, d):
        i = (p, zo, d)
        return remote(tbuf.at[p, first(2, zo) + d], t_half.at[i], th_s.at[i], th_r.at[i], (x_right, x_left)[d])

    def t_full_copy(p, zo, d):
        i = (p, zo, d)
        src = tbuf.at[p, pl.ds(first(1 + 2 * d, zo), 2)]
        return remote(src, t_full.at[i], tf_s.at[i], tf_r.at[i], (x_right, x_left)[d])

    def t_z_copy(p):
        return remote(tbuf.at[p, pl.ds(first(0, 0), 2)], t_z.at[p], tz_s.at[p], tz_r.at[p], z_near)

    def g_x_copy(p, zb, d, dx=0):
        ref = tg_out[p].at[pl.ds(first(dx, 1 - zb), 2)]
        i = (p, zb, d)
        return remote(ref, ref, gx_s.at[i], gx_r.at[i], (x_right, x_left)[d])

    def g_z_copy(p, zb):
        ref = tg_out[p].at[pl.ds(first(0, 1 - zb), 2)]
        return remote(ref, ref, gz_s.at[p], gz_r.at[p], z_near)

    def g_half_copy(p, zb, d, dx):
        ref = tg_out[p].at[first(dx, 1 - zb) + d]
        i = (p, zb, d)
        return remote(ref, ref, gh_s.at[i], gh_r.at[i], (x_right, x_left)[d])

    def t_start(p):
        for zo in range(2):
            for d in range(2):
                go(t_half_copy(p, zo, d))

    def t_pass(p, zo):
        for d in range(2):
            t_half_copy(p, zo, d).wait_recv()
            at = first(1 + 2 * d, zo) + d
            tbuf[p, at] = (tbuf[p, at].astype(F32) + t_half[p, zo, d].astype(F32)).astype(BF16)
            go(t_full_copy(p, zo, d))

    def t_total(p, zo, k):
        total = tbuf[p, first(0, zo) + k].astype(F32)
        return total + t_full[p, zo, 0, k].astype(F32) + t_full[p, zo, 1, k].astype(F32)

    def t_cross(p):
        for d in range(2):
            t_full_copy(p, 0, d).wait_recv()
        for k in range(2):
            tbuf[p, first(0, 0) + k] = t_total(p, 0, k).astype(BF16)
        go(t_z_copy(p))

    def t_finish(p):
        for d in range(2):
            t_full_copy(p, 1, d).wait_recv()
        t_z_copy(p).wait_recv()
        for k in range(2):
            tg_out[p][first(0, 1) + k] = (t_total(p, 1, k) + t_z[p, k].astype(F32)).astype(BF16)
        go(g_z_copy(p, 0))
        for d in range(2):
            go(g_x_copy(p, 0, d))

    def t_spread(p):
        g_z_copy(p, 1).wait_recv()
        for d in range(2):
            go(g_x_copy(p, 1, d))

    def t_relay(p, zb):
        for d in range(2):
            dx = 3 - 2 * d
            g_x_copy(p, zb, d, dx).wait_recv()
            go(g_half_copy(p, zb, d, dx))

    def t_last(p):
        for zb in range(2):
            for d in range(2):
                g_half_copy(p, zb, d, 2).wait_recv()

    def h_copy(i):
        if i == 0:
            src, dst, to = grads.at[:, 1 - core], h_core, other
        elif i < 3:
            d = i - 1
            src, dst, to = h_sum.at[:, lax.rem(y + 2, 4), pl.ds(d * 128, 128)], h_half.at[d], (right, left)[d]
        elif i < 5:
            d = i - 3
            src, dst, to = h_sum.at[:, lax.rem(y + 1 + 2 * d, 4)], h_full.at[d], (right, left)[d]
        elif i == 5:
            src, dst, to = h_sum.at[1 - z, y], h_z, across
        elif i < 8:
            d = i - 6
            src, dst, to = hx_sum.at[:, lax.rem(x + 2, 4), pl.ds(d * 16, 16)], hx_half.at[d], (x_right, x_left)[d]
        elif i < 10:
            d = i - 8
            src, dst, to = hx_sum.at[:, lax.rem(x + 1 + 2 * d, 4)], hx_full.at[d], (x_right, x_left)[d]
        else:
            src, dst, to = hx_sum.at[1 - zl, x], hx_z, z_near
        return remote(src, dst, h_s.at[i], h_r.at[i], to)

    def wide(v):
        return v.astype(F32)

    def h1():
        h_copy(0).wait_recv()
        for q in range(8):
            total = wide(grads[q, core]) + wide(h_core[q])
            h_sum[q // 4, q % 4] = total.astype(BF16).reshape(h_sum.shape[2:])
        go(h_copy(1))
        go(h_copy(2))

    def h2():
        for d in range(2):
            h_copy(1 + d).wait_recv()
            at, rows = lax.rem(y + 1 + 2 * d, 4), pl.ds(d * 128, 128)
            for k in range(2):
                h_sum[k, at, rows] = (wide(h_sum[k, at, rows]) + wide(h_half[d, k])).astype(BF16)
            go(h_copy(3 + d))

    def h3():
        for d in range(2):
            h_copy(3 + d).wait_recv()
        for k in range(2):
            h_sum[k, y] = (wide(h_sum[k, y]) + wide(h_full[0, k]) + wide(h_full[1, k])).astype(BF16)
        go(h_copy(5))

    def h4():
        h_copy(5).wait_recv()
        total = (wide(h_sum[z, y]) + wide(h_z[...])).astype(BF16).reshape(8, 32, 128)
        for q in range(8):
            hx_sum[q // 4, q % 4] = total[q]
        go(h_copy(6))
        go(h_copy(7))

    def h5():
        for d in range(2):
            h_copy(6 + d).wait_recv()
            at, rows = lax.rem(x + 1 + 2 * d, 4), pl.ds(d * 16, 16)
            for k in range(2):
                hx_sum[k, at, rows] = (wide(hx_sum[k, at, rows]) + wide(hx_half[d, k])).astype(BF16)
            go(h_copy(8 + d))

    def h6():
        for d in range(2):
            h_copy(8 + d).wait_recv()
        for k in range(2):
            hx_sum[k, x] = (wide(hx_sum[k, x]) + wide(hx_full[0, k]) + wide(hx_full[1, k])).astype(BF16)
        go(h_copy(10))

    def h7():
        h_copy(10).wait_recv()
        hid_out[...] = wide(hx_sum[zl, x]) + wide(hx_z[...])

    def q_copy(i):
        if i < 3:
            src, dst, to = p_x.at[3], p_x.at[i], x_to[1 + i]
        elif i == 3:
            src, dst, to = p_z.at[0], p_z.at[1], z_near
        elif i == 4:
            ref = p_all.at[z, y, core]
            src, dst, to = ref, ref, other
        elif i < 8:
            ref = p_all.at[z, y]
            src, dst, to = ref, ref, (right, opposite, left)[i - 5]
        else:
            ref = p_all.at[z]
            src, dst, to = ref, ref, across
        return remote(src, dst, q_s.at[i], q_r.at[i], to)

    def q0():
        a = lax.rem(lax.broadcasted_iota(jnp.int32, pg.shape, 0), SUB)
        b = lax.rem(lax.broadcasted_iota(jnp.int32, pg.shape, 1), SUB)
        p_x[3] = jnp.sum(jnp.where(a == b, pg[...], 0.0).reshape(n_f, SUB, KK * SUB), axis=1)
        for i in range(3):
            go(q_copy(i))

    def q1():
        for i in range(3):
            q_copy(i).wait_recv()
        p_z[0] = p_x[0] + p_x[1] + p_x[2] + p_x[3]
        go(q_copy(3))

    def q2():
        q_copy(3).wait_recv()
        p_all[z, y, core] = p_z[0] + p_z[1]
        go(q_copy(4))

    def q3():
        ref = p_all.at[z, y, 1 - core]
        remote(ref, ref, q_s.at[4], q_r.at[4], other).wait_recv()
        for i in range(3):
            go(q_copy(5 + i))

    def q4():
        for i in range(3):
            ref = p_all.at[z, lax.rem(y + 3 - i, 4)]
            remote(ref, ref, q_s.at[5 + i], q_r.at[5 + i], right).wait_recv()
        go(q_copy(8))

    def q5():
        ref = p_all.at[1 - z]
        remote(ref, ref, q_s.at[8], q_r.at[8], across).wait_recv()
        j = 2 * rep + lax.div(me, 8)
        pg_out[...] = p_all[lax.div(j, 8), lax.rem(lax.div(j, 2), 4), lax.rem(j, 2)]

    own = [pltpu.make_async_copy(dfac.at[p], gbuf.at[p, me], own_sem.at[p]) for p in range(2)]
    for c in own:
        c.start()
    p_copy(0).start()
    for _, n in order[:8]:
        w_copy(n).start()
    pg[...] = jnp.zeros_like(pg)
    kron_t[...] = spread_out(proj[pl.ds(pl.multiple_of(me * n_f, n_f), n_f), :], False)
    barrier((other, right, left, opposite, across, x_to[1], x_to[2], x_to[3], z_near))
    own[0].wait()
    for i, to in enumerate((right, left, across)):
        go(whole(0, 0, 1 + i, to))
    go(to_core(0, 0))
    own[1].wait()
    go(to_core(1, 0))
    go(h_copy(0))
    work(0, 0)
    near(0)
    work(0, 1)
    work(0, 2)
    work(0, 3)
    half_arrived(0, 6)
    work(0, 6)
    far(0)
    for i, to in enumerate((right, left, across)):
        go(whole(1, 0, 1 + i, to))
    work(0, 4)
    work(0, 5)
    half_arrived(0, 7)
    work(0, 7)
    t_start(0)
    work(1, 0)
    t_pass(0, 0)
    near(1)
    t_pass(0, 1)
    work(1, 1)
    t_cross(0)
    work(1, 2)
    half_arrived(1, 6)
    work(1, 3)
    t_finish(0)
    far(1)
    work(1, 6)
    t_spread(0)
    work(1, 4)
    t_relay(0, 0)
    work(1, 5)
    half_arrived(1, 7)
    t_relay(0, 1)
    h1()
    work(1, 7)
    t_start(1)
    q0()
    t_last(0)
    h2()
    t_pass(1, 0)
    q1()
    t_pass(1, 1)
    h3()
    q2()
    t_cross(1)
    h4()
    q3()
    t_finish(1)
    h5()
    q4()
    t_spread(1)
    h6()
    t_relay(1, 0)
    q5()
    h7()
    t_relay(1, 1)
    t_last(1)
    for s in sends:
        s.wait_send()


def backward(dfac, words, pooled, proj, grads):
    _, n_f, emb, _ = pooled.shape
    rows = 8 * HI
    width = emb // 2
    n_grad = grads.shape[2]
    grads = grads.reshape(8, 2, 8, n_grad, 128)
    dma = pltpu.SemaphoreType.DMA
    vmem = pl.BlockSpec(memory_space=pltpu.VMEM)
    hbm = pl.BlockSpec(memory_space=pl.ANY)
    a222 = dma((2, 2, 2))
    return pl.pallas_call(
        bwd_kernel,
        out_shape=(
            jax.ShapeDtypeStruct((n_f, rows, width), BF16),
            jax.ShapeDtypeStruct((n_f, rows, width), BF16),
            jax.ShapeDtypeStruct((n_grad, 128), F32),
            jax.ShapeDtypeStruct((n_f, KK * SUB), F32),
        ),
        in_specs=[vmem, hbm, hbm, vmem, vmem],
        out_specs=(vmem, vmem, vmem, vmem),
        scratch_shapes=[
            pltpu.VMEM((n_f * SUB, KK * SUB), BF16),
            pltpu.VMEM((2, 16, KK, width, 128), BF16),
            pltpu.VMEM((n_f, rows, width), F32),
            pltpu.VMEM((n_f, width, 256), BF16),
            pltpu.VMEM((8, n_f, HI, 256), jnp.int32),
            pltpu.VMEM((2, n_f, width, 256), BF16),
            pltpu.VMEM((2, n_f, rows, width), BF16),
            pltpu.VMEM((2, 2, 2, rows, width), BF16),
            pltpu.VMEM((2, 2, 2, 2, rows, width), BF16),
            pltpu.VMEM((2, 2, rows, width), BF16),
            pltpu.VMEM((n_f * SUB, KK * SUB), F32),
            pltpu.VMEM((8, 8, n_grad, 128), BF16),
            pltpu.VMEM((2, 4, 8 * n_grad, 128), BF16),
            pltpu.VMEM((2, 2, 4 * n_grad, 128), BF16),
            pltpu.VMEM((2, 2, 8 * n_grad, 128), BF16),
            pltpu.VMEM((8 * n_grad, 128), BF16),
            pltpu.VMEM((2, 4, n_grad, 128), BF16),
            pltpu.VMEM((2, 2, n_grad // 2, 128), BF16),
            pltpu.VMEM((2, 2, n_grad, 128), BF16),
            pltpu.VMEM((n_grad, 128), BF16),
            pltpu.VMEM((4, n_f, KK * SUB), F32),
            pltpu.VMEM((2, n_f, KK * SUB), F32),
            pltpu.VMEM((2, 4, 2, n_f, KK * SUB), F32),
            dma((2,)), dma((8,)), dma((2,)), dma((2, 8)), dma((2, 8)), dma((2, 6)), dma((2, 6)), a222, a222,
            dma((2, 3)), dma((2, 3)),
            a222, a222, a222, a222, dma((2,)), dma((2,)), dma((2,)), dma((2,)), a222, a222, a222, a222,
            dma((11,)), dma((11,)), dma((9,)), dma((9,)),
        ],
        compiler_params=pltpu.CompilerParams(collective_id=1, has_side_effects=True, vmem_limit_bytes=VMEM),
        cost_estimate=pl.CostEstimate(flops=20 * 10**9, bytes_accessed=40 * 10**6, transcendentals=0),
    )(dfac, words, pooled, proj, grads)


def local(indices, lengths, tables, proj, w_hidden, w_out, d_logit):
    n_f = indices.shape[0]
    me = lax.axis_index("mp")
    words, pooled, fac = forward(indices, lengths, tables, proj)
    logits, grads, dfac = dense(fac, w_hidden, w_out, d_logit)
    low, high, dense_sum, pg = backward(dfac, words, pooled, proj, grads)
    table_grad = jnp.concatenate([low, high], axis=2).astype(F32)
    feat = w_hidden.shape[1]
    mine = proj.shape[0] // 128
    pg = lax.dynamic_slice_in_dim(pg, lax.rem(me * mine, n_f), mine, 0)
    return (
        logits.reshape(-1),
        table_grad,
        dense_sum[:, :feat],
        dense_sum[:, feat : feat + 3].sum(1),
        pg.reshape(mine, KK, SUB).sum(2),
    )


def solution(mesh):
    in_specs = (
        P("mp", None, "replica"),
        P("mp", "replica"),
        P("mp", None, None),
        P(),
        P(),
        P(),
        P(("replica", "mp")),
    )
    out_specs = (
        P(("replica", "mp")),
        P("mp", None, None),
        P(("replica", "mp"), None),
        P(("replica", "mp")),
        P(("replica", "mp"), None),
    )
    return jax.shard_map(local, mesh=mesh, in_specs=in_specs, out_specs=out_specs, check_vma=False)
```

```python
import functools

import jax
import jax.numpy as jnp
from jax import lax
from jax.experimental import pallas as pl
from jax.experimental.pallas import tpu as pltpu
from jax.sharding import PartitionSpec as P

MESH = pl.DeviceIdType.MESH
K1 = 8
K2 = 8
KK = K1 + K2
SUB = 16
HI = 64
BITS = 4
VMEM = 60 * 1024 * 1024
LOW = 9
LOW_HALF = 5
HIGH_HALF = 13
GATHER_LOW = (9, 12)
X_FIRST = (512, 288)
F32 = jnp.float32
BF16 = jnp.bfloat16


def peers():
    me = lax.axis_index("mp")
    core = lax.rem(me, 2)
    y = lax.rem(lax.div(me, 2), 4)
    z = lax.div(me, 8)
    other = {"mp": me + 1 - 2 * core}
    right = {"mp": z * 8 + lax.rem(y + 1, 4) * 2 + core}
    left = {"mp": z * 8 + lax.rem(y + 3, 4) * 2 + core}
    across = {"mp": (1 - z) * 8 + y * 2 + core}
    return me, core, y, z, other, right, left, across


def barrier(devices):
    sem = pltpu.get_barrier_semaphore()
    for d in devices:
        pl.semaphore_signal(sem, inc=1, device_id=d, device_id_type=MESH)
    pl.semaphore_wait(sem, len(devices))


def remote(src, dst, send, recv, device):
    return pltpu.make_async_remote_copy(
        src_ref=src, dst_ref=dst, send_sem=send, recv_sem=recv, device_id=device, device_id_type=MESH
    )


def digits(words):
    return jnp.concatenate(
        [(lax.shift_right_logical(words, BITS * d) & 15).astype(F32).astype(BF16) for d in range(8)], axis=0
    )


def nt(a, b):
    return lax.dot_general(a, b, (((1,), (1,)), ((), ())), preferred_element_type=F32)


def tn(a, b):
    return lax.dot_general(a, b, (((0,), (0,)), ((), ())), preferred_element_type=F32)


def spread_out(here, flip):
    n = here.shape[0] * SUB
    owner = lax.div(lax.broadcasted_iota(jnp.int32, (n, KK), 0), SUB)
    pick = (owner == lax.broadcasted_iota(jnp.int32, (n, KK), 1)).astype(F32).astype(BF16)
    rows = (nt(pick, here) if flip else jnp.dot(pick, here, preferred_element_type=F32)).astype(BF16)
    full = nt(rows, pick)
    a = lax.rem(lax.broadcasted_iota(jnp.int32, (n, n), 0), SUB)
    b = lax.rem(lax.broadcasted_iota(jnp.int32, (n, n), 1), SUB)
    return jnp.where(a == b, full, 0.0).astype(BF16)


def fwd_kernel(
    idx, lens, tab, proj, words_out, pooled_out, fac_out,
    kron, tab_t, sbuf, rcore, rhalf, rfull, rz, rshare, wbuf, pbuf,
    core_s, core_r, half_s, half_r, full_s, full_r, z_s, z_r, share_s, share_r, w_sem, p_sem,
):
    me, core, y, z, other, right, left, across = peers()
    n_f = idx.shape[0]
    emb = tab.shape[2]

    def chunk_of(t):
        early, late = 1 - jnp.minimum(lax.div(t, 2), 1), lax.div(t, 6)
        mid = 1 - early - late
        dy = early * 2 + mid * (1 + 2 * lax.rem(t, 2))
        zo = early * t + mid * lax.div(t - 2 + 2 * early, 2) + late * (t - 6)
        return lax.rem(z + 1 + zo, 2) * 4 + lax.rem(y + dy, 4)

    def p_copy(t):
        slot = lax.rem(t, 2)
        return pltpu.make_async_copy(pbuf.at[slot], pooled_out.at[chunk_of(t)], p_sem.at[slot])

    def w_copy(t):
        return pltpu.make_async_copy(wbuf.at[t], words_out.at[chunk_of(t)], w_sem.at[t])

    def core_copy(t):
        return remote(sbuf.at[t, 1 - core], rcore.at[t], core_s.at[t], core_r.at[t], other)

    def half_range(part, d):
        return ((0, LOW_HALF), (LOW_HALF, LOW), (LOW, HIGH_HALF), (HIGH_HALF, KK))[2 * part + d]

    def half_copy(i, d):
        low, high = half_range(i // 2, d)
        zo, ks = min(i, 1), pl.ds(low, high - low)
        return remote(
            sbuf.at[zo, core, ks], rhalf.at[zo, ks], half_s.at[i, d], half_r.at[i, d], (right, left)[d]
        )

    def full_copy(zo, d):
        ks = pl.ds(0, KK if zo else LOW)
        return remote(
            sbuf.at[2 + 2 * zo + d, core, ks], rfull.at[zo, d, ks], full_s.at[zo, d], full_r.at[zo, d], (right, left)[d]
        )

    def share_copy(i):
        t = (0, 2, 3)[i]
        return remote(sbuf.at[t, core, pl.ds(LOW, KK - LOW)], rshare.at[i], share_s.at[i], share_r.at[i], across)

    def z_copy():
        return remote(sbuf.at[6, core], rz, z_s, z_r, across)

    def compute(t, start=False):
        q = chunk_of(t)
        slot = lax.rem(t, 2)
        where = pl.ds(pl.multiple_of(q * 256, 256), 256)
        if not start:

            @pl.when(t >= 2)
            def _():
                p_copy(t - 2).wait()

        else:
            eye = (
                lax.broadcasted_iota(jnp.int32, (emb, emb), 0) == lax.broadcasted_iota(jnp.int32, (emb, emb), 1)
            ).astype(F32).astype(BF16)

        def field(f, carry):
            ids = idx[f, :, where]
            live = lens[pl.ds(f, 1), where]
            lane_slot = lax.broadcasted_iota(jnp.int32, ids.shape, 0)
            hi = ids & (HI - 1)
            val = jnp.where(lane_slot < live, jnp.left_shift(1, BITS * lax.shift_right_logical(ids, 6)), 0)
            rows = lax.broadcasted_iota(jnp.int32, (HI, 256), 0)
            words = jnp.zeros((HI, 256), jnp.int32)
            for s in range(8):
                words = words + jnp.where(hi[s : s + 1, :] == rows, val[s : s + 1, :], 0)
            wbuf[t, f] = words
            if start:
                table = nt(eye, tab[f]).astype(BF16)
                tab_t[f] = table
            else:
                table = tab_t[f]
            pooled = jnp.dot(table, digits(words), preferred_element_type=F32)
            pbuf[slot, f] = pooled.astype(BF16)
            return carry

        lax.fori_loop(0, n_f, field, 0, unroll=8)
        p_copy(t).start()
        w_copy(t).start()

        def block(eb, carry):
            rows = pl.ds(pl.multiple_of(eb * SUB, SUB), SUB)
            x = pbuf[slot, :, rows, :].reshape(n_f * SUB, 256)
            part = jnp.dot(kron[...], x, preferred_element_type=F32).astype(BF16).reshape(KK, SUB, 256)
            sbuf[t, 0, :, rows, :] = part[:, :, :128]
            sbuf[t, 1, :, rows, :] = part[:, :, 128:]
            return carry

        lax.fori_loop(0, emb // SUB, block, 0, unroll=8)
        if not start:
            core_copy(t).start()

    def add(t, parts, out=None):
        edges = sorted({e for _, _, a, b in parts for e in (a, b)})
        for low, high in zip(edges, edges[1:]):
            refs = [(r, base) for r, base, a, b in parts if a <= low and high <= b]

            def one(k, carry, refs=refs):
                total = sbuf[t, core, k].astype(F32)
                for r, base in refs:
                    total = total + r[k - base].astype(F32)
                if out is None:
                    sbuf[t, core, k] = total.astype(BF16)
                else:
                    out[k] = total
                return carry

            lax.fori_loop(low, high, one, 0)

    def near(t):
        core_copy(t).wait_recv()
        return (rcore.at[t], 0, 0, KK)

    def share(i):
        share_copy(i).wait_recv()
        return (rshare.at[i], LOW, LOW, KK)

    def opposite(zo):
        add(zo, [near(zo)])
        for d in range(2):
            half_copy(zo, d).start()
        if not zo:
            share_copy(0).start()

    def opposite_rest():
        add(1, [share(0)])
        for d in range(2):
            half_copy(2, d).start()

    def side(zo, d):
        t = 2 + 2 * zo + d
        half_copy(zo, d).wait_recv()
        parts = [near(t), (rhalf.at[zo], 0, *half_range(0, d))]
        if zo:
            half_copy(2, d).wait_recv()
            parts += [(rhalf.at[zo], 0, *half_range(1, d)), share(1 + d)]
        add(t, parts)
        full_copy(zo, d).start()
        if not zo:
            share_copy(1 + d).start()

    def own(zo):
        for d in range(2):
            full_copy(zo, d).wait_recv()
        parts = [near(6 + zo)] + [(rfull.at[zo, d], 0, 0, KK if zo else LOW) for d in range(2)]
        if zo:
            z_copy().wait_recv()
            add(7, parts + [(rz, 0, 0, KK)], fac_out)
        else:
            add(6, parts)
            z_copy().start()

    def span(a, b):
        def step(t, carry):
            compute(t)
            return carry

        lax.fori_loop(a, b, step, 0)

    kron[...] = spread_out(proj[pl.ds(pl.multiple_of(me * n_f, n_f), n_f), :], True)
    compute(0, True)
    barrier((other, right, left, across))
    core_copy(0).start()
    opposite(0)
    span(1, 2)
    opposite(1)
    span(2, 3)
    side(0, 0)
    opposite_rest()
    span(3, 4)
    side(0, 1)
    span(4, 7)
    own(0)
    side(1, 0)
    side(1, 1)
    span(7, 8)
    own(1)

    for t in range(8):
        core_copy(t).wait_send()
        w_copy(t).wait()
    for zo in range(2):
        for d in range(2):
            full_copy(zo, d).wait_send()
    for i in range(3):
        for d in range(2):
            half_copy(i, d).wait_send()
    for t in range(3):
        share_copy(t).wait_send()
    z_copy().wait_send()
    p_copy(6).wait()
    p_copy(7).wait()


def forward(indices, lengths, tables, proj):
    n_f, _, emb = tables.shape
    dma = pltpu.SemaphoreType.DMA
    vmem = pl.BlockSpec(memory_space=pltpu.VMEM)
    hbm = pl.BlockSpec(memory_space=pl.ANY)
    return pl.pallas_call(
        fwd_kernel,
        out_shape=(
            jax.ShapeDtypeStruct((8, n_f, HI, 256), jnp.int32),
            jax.ShapeDtypeStruct((8, n_f, emb, 256), BF16),
            jax.ShapeDtypeStruct((KK, emb, 128), F32),
        ),
        in_specs=[vmem] * 4,
        out_specs=(hbm, hbm, vmem),
        scratch_shapes=[
            pltpu.VMEM((n_f * SUB, KK * SUB), BF16),
            pltpu.VMEM((n_f, emb, 8 * HI), BF16),
            pltpu.VMEM((8, 2, KK, emb, 128), BF16),
            pltpu.VMEM((8, KK, emb, 128), BF16),
            pltpu.VMEM((2, KK, emb, 128), BF16),
            pltpu.VMEM((2, 2, KK, emb, 128), BF16),
            pltpu.VMEM((KK, emb, 128), BF16),
            pltpu.VMEM((3, KK - LOW, emb, 128), BF16),
            pltpu.VMEM((8, n_f, HI, 256), jnp.int32),
            pltpu.VMEM((2, n_f, emb, 256), BF16),
            dma((8,)), dma((8,)), dma((3, 2)), dma((3, 2)), dma((2, 2)), dma((2, 2)), dma, dma, dma((3,)), dma((3,)),
            dma((8,)), dma((2,)),
        ],
        compiler_params=pltpu.CompilerParams(collective_id=0, has_side_effects=True, vmem_limit_bytes=VMEM),
        cost_estimate=pl.CostEstimate(flops=15 * 10**9, bytes_accessed=40 * 10**6, transcendentals=0),
    )(indices, lengths, tables, proj)


def dense_kernel(fac, wh_t, wo_row, dl, logits, grads, dfac, inter):
    n_feat, hid = wh_t.shape
    emb = fac.shape[1]
    step = grads.shape[0] * grads.shape[2]

    def left(i, carry):
        a = fac[i]
        for j in range(K2):
            inter[pl.ds(i * K2 + j, 1), :] = jnp.sum(a * fac[K1 + j], axis=0, keepdims=True)
        return carry

    lax.fori_loop(0, K1, left, 0, unroll=2)
    feat = inter[...].astype(BF16)
    row = dl[...]
    n = row.shape[1]
    d0 = row.astype(BF16)
    r1 = row - d0.astype(F32)
    d1 = r1.astype(BF16)
    d2 = (r1 - d1.astype(F32)).astype(BF16)
    sub = lax.broadcasted_iota(jnp.int32, (n_feat, n), 0)
    d_rows = jnp.where(
        sub == 0, d0.astype(F32), jnp.where(sub == 1, d1.astype(F32), jnp.where(sub == 2, d2.astype(F32), 0.0))
    ).astype(BF16)
    nil = jnp.zeros((n_feat, n), BF16)
    feat_low = jnp.concatenate([feat, nil], axis=0)
    d_high = jnp.concatenate([nil, d_rows], axis=0)
    ones = jnp.ones((8, n), BF16)

    def top(c, carry):
        logit_acc, d_inter = carry
        at = pl.ds(pl.multiple_of(c * step, step), step)
        w = wh_t[:, at]
        v = tn(w, feat)
        wo = jnp.broadcast_to(wo_row[:, at].astype(F32), (8, step))
        top_row = lax.broadcasted_iota(jnp.int32, (8, step), 0) == 0
        wo_cols = tn(jnp.where(top_row, wo, 0.0).astype(BF16), ones)
        s = jax.nn.sigmoid(v)
        hidden = (v * s).astype(BF16)
        logit_acc = logit_acc + jnp.dot(wo.astype(BF16), hidden, preferred_element_type=F32)
        d_hidden = (wo_cols * row * s * (1.0 + v * (1.0 - s))).astype(BF16)
        grad = nt(d_hidden, feat_low) + nt(hidden, d_high)
        grads[:, pl.ds(c, 1), :, :] = grad.astype(BF16).reshape(grads.shape[0], 1, grads.shape[2], 2 * n_feat)
        d_inter = d_inter + jnp.dot(w, d_hidden, preferred_element_type=F32)
        return logit_acc, d_inter

    logit_acc, d_inter = lax.fori_loop(
        0, hid // step, top, (jnp.zeros((8, n), F32), jnp.zeros((n_feat, n), F32)), unroll=2
    )
    logits[...] = logit_acc[0:1]
    inter[...] = d_inter

    def back(eb, carry):
        p = lax.div(eb, emb // SUB // 2)
        rows = pl.ds(pl.multiple_of(eb * SUB, SUB), SUB)
        low = pl.ds(pl.multiple_of(lax.rem(eb, emb // SUB // 2) * SUB, SUB), SUB)
        right = [fac[K1 + j, rows, :] for j in range(K2)]
        d_right = [jnp.zeros((SUB, n), F32) for _ in range(K2)]
        for i in range(K1):
            a = fac[i, rows, :]
            d_left = jnp.zeros((SUB, n), F32)
            for j in range(K2):
                g = inter[pl.ds(i * K2 + j, 1), :]
                d_left = d_left + g * right[j]
                d_right[j] = d_right[j] + g * a
            dfac[p, i, low, :] = d_left.astype(BF16)
        for j in range(K2):
            dfac[p, K1 + j, low, :] = d_right[j].astype(BF16)
        return carry

    lax.fori_loop(0, emb // SUB, back, 0, unroll=2)


def dense(fac, w_hidden, w_out, d_logit):
    hid, feat = w_hidden.shape
    n = d_logit.shape[0]
    return pl.pallas_call(
        dense_kernel,
        out_shape=(
            jax.ShapeDtypeStruct((1, n), F32),
            jax.ShapeDtypeStruct((16, 8, hid // 128, 2 * feat), BF16),
            jax.ShapeDtypeStruct((2, KK, fac.shape[1] // 2, n), BF16),
        ),
        scratch_shapes=[pltpu.VMEM((feat, n), F32)],
        compiler_params=pltpu.CompilerParams(vmem_limit_bytes=VMEM),
        cost_estimate=pl.CostEstimate(flops=10**9, bytes_accessed=10**7, transcendentals=10**6),
    )(fac, w_hidden.T, w_out[None, :], d_logit[None, :])


def bwd_kernel(
    dfac, words, pooled, proj, grads,
    tg_low, tg_high, hid_out, pg_out,
    kron_t, gbuf, acc, dpool, wbuf, pbuf, tbuf, t_half, t_full, t_z, t_share, pg,
    h_core, h_sum, h_half, h_full, h_z, hx_sum, hx_half, hx_full, hx_z, p_x, p_z, p_all,
    own_sem, w_sem, p_sem, core_s, core_r, ici_s, ici_r, half_s, half_r, rest_s, rest_r, ts_s, ts_r, gr_s, gr_r,
    th_s, th_r, tf_s, tf_r, tz_s, tz_r, gz_s, gz_r, gx_s, gx_r, gh_s, gh_r, h_s, h_r, q_s, q_r,
):
    me, core, y, z, other, right, left, across = peers()
    opposite = {"mp": z * 8 + lax.rem(y + 2, 4) * 2 + core}
    rep = lax.axis_index("replica")
    x = lax.rem(rep, 4)
    zl = lax.div(rep, 4)
    x_to = [None] + [{"replica": zl * 4 + lax.rem(x + d, 4)} for d in (1, 2, 3)]
    x_right, x_left = x_to[1], x_to[3]
    z_near = {"replica": (1 - zl) * 4 + x}
    n_f = tbuf.shape[1]
    width = dpool.shape[1]
    places = ((0, 0), (0, 3), (0, 1), (1, 0), (1, 3), (1, 1), (0, 2), (1, 2))
    order = [(p, n) for p in range(2) for n in (0, 1, 2, 3, 6, 4, 5, 7)]
    sends = []
    tg_out = (tg_low, tg_high)

    def go(copy):
        copy.start()
        sends.append(copy)

    def chip(n):
        dz, dy = places[n]
        return lax.rem(z + dz, 2) * 4 + lax.rem(y + dy, 4)

    def block(n):
        return chip(n) * 2 + core

    def to_core(p, n):
        ref = gbuf.at[p, block(n)]
        return remote(ref, ref, core_s.at[p, n], core_r.at[p, n], other)

    def from_core(p, n):
        ref = gbuf.at[p, chip(n) * 2 + 1 - core]
        remote(ref, ref, core_s.at[p, n], core_r.at[p, n], other).wait_recv()

    def whole(p, n, m, device):
        ref = gbuf.at[p, block(n), pl.ds(0, GATHER_LOW[p] if m in (4, 5) else KK)]
        return remote(ref, ref, ici_s.at[p, m], ici_r.at[p, m], device)

    def arrived(p, m):
        whole(p, m, m, right).wait_recv()

    def half(p, n, m, d):
        cut, top = (K1, KK) if m == 6 else ((GATHER_LOW[p] + 1) // 2, GATHER_LOW[p])
        ref = gbuf.at[p, block(n), pl.ds(cut, top - cut) if d else pl.ds(0, cut)]
        i = (p, m - 6, d)
        return remote(ref, ref, half_s.at[i], half_r.at[i], (right, left)[d])

    def rest(p, n):
        ref = gbuf.at[p, block(n), pl.ds(GATHER_LOW[p], KK - GATHER_LOW[p])]
        i = (1, 2, 6).index(n)
        return remote(ref, ref, rest_s.at[p, i], rest_r.at[p, i], across)

    def rest_arrived(p, m):
        ref = gbuf.at[p, block(m), pl.ds(GATHER_LOW[p], KK - GATHER_LOW[p])]
        i = (4, 5, 7).index(m)
        remote(ref, ref, rest_s.at[p, i], rest_r.at[p, i], across).wait_recv()

    def half_arrived(p, m):
        for d in range(2):
            half(p, m, m, d).wait_recv()
        if m == 6:
            go(rest(p, 6))
        else:
            rest_arrived(p, 7)
        go(to_core(p, m))

    def near(p):
        for d in range(2):
            arrived(p, 1 + d)
            go(half(p, 1 + d, 6, d))
            go(rest(p, 1 + d))
            go(to_core(p, 1 + d))
        arrived(p, 3)
        go(whole(p, 3, 4, right))
        go(whole(p, 3, 5, left))
        go(to_core(p, 3))

    def far(p):
        for d in range(2):
            arrived(p, 4 + d)
            go(half(p, 4 + d, 7, d))
        for d in range(2):
            rest_arrived(p, 4 + d)
            go(to_core(p, 4 + d))

    def w_copy(n):
        return pltpu.make_async_copy(words.at[chip(n)], wbuf.at[n], w_sem.at[n])

    def p_copy(i):
        p, n = order[i]
        return pltpu.make_async_copy(
            pooled.at[chip(n), :, pl.ds(p * width, width), :], pbuf.at[i % 2], p_sem.at[i % 2]
        )

    def work(p, n):
        i = order.index((p, n))
        p_copy(i).wait()
        if i + 1 < len(order):
            p_copy(i + 1).start()
        if p == 0:
            w_copy(n).wait()
        from_core(p, n)
        slot = i % 2
        base = chip(n) * 2

        def spread(eb, carry):
            rows = pl.ds(pl.multiple_of(eb * SUB, SUB), SUB)
            g = jnp.concatenate(
                [gbuf[p, base + c, :, rows, :].reshape(KK * SUB, 128) for c in range(2)], axis=1
            )
            d = jnp.dot(kron_t[...], g, preferred_element_type=F32).astype(BF16)
            dpool[:, rows, :] = d.reshape(n_f, SUB, 256)
            pg[...] += nt(pbuf[slot, :, rows, :].reshape(n_f * SUB, 256), g)
            return carry

        lax.fori_loop(0, width // SUB, spread, 0, unroll=8)

        def field(f, carry):
            part = nt(digits(wbuf[n, f]), dpool[f])
            if n == 0:
                acc[f] = part
            elif n == 7:
                tbuf[p, f] = (acc[f] + part).astype(BF16)
            else:
                acc[f] += part
            return carry

        lax.fori_loop(0, n_f, field, 0, unroll=8)

    def first(dx, zo):
        return (lax.rem(zl + 1 + zo, 2) * 4 + lax.rem(x + dx, 4)) * 2

    n_rows = tbuf.shape[2]

    def low(p, zo):
        return pl.ds(0, n_rows if zo else X_FIRST[p])

    def high(p):
        return pl.ds(X_FIRST[p], n_rows - X_FIRST[p])

    def split(p):
        return X_FIRST[p] < n_rows

    def t_half_copy(p, zo, d):
        i = (p, zo, d)
        src = tbuf.at[p, first(2, zo) + d, low(p, zo)]
        return remote(src, t_half.at[p, zo, d, low(p, zo)], th_s.at[i], th_r.at[i], (x_right, x_left)[d])

    def t_full_copy(p, zo, d):
        i = (p, zo, d)
        src = tbuf.at[p, pl.ds(first(1 + 2 * d, zo), 2), low(p, zo)]
        return remote(src, t_full.at[p, zo, d, :, low(p, zo)], tf_s.at[i], tf_r.at[i], (x_right, x_left)[d])

    def t_share_copy(p, i):
        src = tbuf.at[p, pl.ds(first((2, 1, 3)[i], 0), 2), high(p)]
        return remote(src, t_share.at[i], ts_s.at[i], ts_r.at[i], z_near)

    def t_z_copy(p):
        return remote(tbuf.at[p, pl.ds(first(0, 0), 2)], t_z.at[p], tz_s.at[p], tz_r.at[p], z_near)

    def g_x_copy(p, zb, d, dx=0):
        ref = tg_out[p].at[pl.ds(first(dx, 1 - zb), 2), low(p, 1 - zb)]
        i = (p, zb, d)
        return remote(ref, ref, gx_s.at[i], gx_r.at[i], (x_right, x_left)[d])

    def g_z_copy(p, zb):
        ref = tg_out[p].at[pl.ds(first(0, 1 - zb), 2)]
        return remote(ref, ref, gz_s.at[p], gz_r.at[p], z_near)

    def g_half_copy(p, zb, d, dx):
        ref = tg_out[p].at[first(dx, 1 - zb) + d, low(p, 1 - zb)]
        i = (p, zb, d)
        return remote(ref, ref, gh_s.at[i], gh_r.at[i], (x_right, x_left)[d])

    def g_rest_copy(p, zb, i):
        ref = tg_out[p].at[pl.ds(first((3, 1, 2)[i], 1 - zb), 2), high(p)]
        return remote(ref, ref, gr_s.at[i], gr_r.at[i], z_near)

    def t_start(p):
        for zo in range(1 if split(p) else 2):
            for d in range(2):
                go(t_half_copy(p, zo, d))
        if split(p):
            go(t_share_copy(p, 0))

    def take_share(p, i):
        t_share_copy(p, i).wait_recv()
        for k in range(2):
            at = first((2, 1, 3)[i], 1) + k
            tbuf[p, at, high(p)] = (tbuf[p, at, high(p)].astype(F32) + t_share[i, k].astype(F32)).astype(BF16)

    def t_open(p):
        go(t_share_copy(p, 1))
        go(t_share_copy(p, 2))
        take_share(p, 0)
        for d in range(2):
            go(t_half_copy(p, 1, d))

    def t_pass(p, zo):
        for d in range(2):
            t_half_copy(p, zo, d).wait_recv()
            at, rows = first(1 + 2 * d, zo) + d, low(p, zo)
            tbuf[p, at, rows] = (tbuf[p, at, rows].astype(F32) + t_half[p, zo, d, rows].astype(F32)).astype(BF16)
            if zo and split(p):
                take_share(p, 1 + d)
            go(t_full_copy(p, zo, d))

    def t_total(p, zo, k):
        rows = low(p, zo)
        total = tbuf[p, first(0, zo) + k, rows].astype(F32)
        return total + t_full[p, zo, 0, k, rows].astype(F32) + t_full[p, zo, 1, k, rows].astype(F32)

    def t_cross(p):
        for d in range(2):
            t_full_copy(p, 0, d).wait_recv()
        for k in range(2):
            tbuf[p, first(0, 0) + k, low(p, 0)] = t_total(p, 0, k).astype(BF16)
        go(t_z_copy(p))

    def t_finish(p):
        for d in range(2):
            t_full_copy(p, 1, d).wait_recv()
        t_z_copy(p).wait_recv()
        for k in range(2):
            tg_out[p][first(0, 1) + k] = (t_total(p, 1, k) + t_z[p, k].astype(F32)).astype(BF16)
        go(g_z_copy(p, 0))
        for d in range(2):
            go(g_x_copy(p, 0, d))

    def t_spread(p):
        g_z_copy(p, 1).wait_recv()
        for d in range(2):
            go(g_x_copy(p, 1, d))

    def t_relay(p, zb):
        for d in range(2):
            dx = 3 - 2 * d
            g_x_copy(p, zb, d, dx).wait_recv()
            go(g_half_copy(p, zb, d, dx))
            if not zb and split(p):
                go(g_rest_copy(p, 0, d))

    def t_last(p, zb):
        for d in range(2):
            g_half_copy(p, zb, d, 2).wait_recv()
        if split(p):
            if zb:
                for i in range(3):
                    g_rest_copy(p, 1, i).wait_recv()
            else:
                go(g_rest_copy(p, 0, 2))

    def h_copy(i):
        if i == 0:
            src, dst, to = grads.at[:, 1 - core], h_core, other
        elif i < 3:
            d = i - 1
            src, dst, to = h_sum.at[:, lax.rem(y + 2, 4), pl.ds(d * 128, 128)], h_half.at[d], (right, left)[d]
        elif i < 5:
            d = i - 3
            src, dst, to = h_sum.at[:, lax.rem(y + 1 + 2 * d, 4)], h_full.at[d], (right, left)[d]
        elif i == 5:
            src, dst, to = h_sum.at[1 - z, y], h_z, across
        elif i < 8:
            d = i - 6
            src, dst, to = hx_sum.at[:, lax.rem(x + 2, 4), pl.ds(d * 16, 16)], hx_half.at[d], (x_right, x_left)[d]
        elif i < 10:
            d = i - 8
            src, dst, to = hx_sum.at[:, lax.rem(x + 1 + 2 * d, 4)], hx_full.at[d], (x_right, x_left)[d]
        else:
            src, dst, to = hx_sum.at[1 - zl, x], hx_z, z_near
        return remote(src, dst, h_s.at[i], h_r.at[i], to)

    def wide(v):
        return v.astype(F32)

    def h1():
        h_copy(0).wait_recv()
        for q in range(8):
            total = wide(grads[q, core]) + wide(h_core[q])
            h_sum[q // 4, q % 4] = total.astype(BF16).reshape(h_sum.shape[2:])
        go(h_copy(1))
        go(h_copy(2))

    def h2():
        for d in range(2):
            h_copy(1 + d).wait_recv()
            at, rows = lax.rem(y + 1 + 2 * d, 4), pl.ds(d * 128, 128)
            for k in range(2):
                h_sum[k, at, rows] = (wide(h_sum[k, at, rows]) + wide(h_half[d, k])).astype(BF16)
            go(h_copy(3 + d))

    def h3():
        for d in range(2):
            h_copy(3 + d).wait_recv()
        for k in range(2):
            h_sum[k, y] = (wide(h_sum[k, y]) + wide(h_full[0, k]) + wide(h_full[1, k])).astype(BF16)
        go(h_copy(5))

    def h4():
        h_copy(5).wait_recv()
        total = (wide(h_sum[z, y]) + wide(h_z[...])).astype(BF16).reshape(8, 32, 128)
        for q in range(8):
            hx_sum[q // 4, q % 4] = total[q]
        go(h_copy(6))
        go(h_copy(7))

    def h5():
        for d in range(2):
            h_copy(6 + d).wait_recv()
            at, rows = lax.rem(x + 1 + 2 * d, 4), pl.ds(d * 16, 16)
            for k in range(2):
                hx_sum[k, at, rows] = (wide(hx_sum[k, at, rows]) + wide(hx_half[d, k])).astype(BF16)
            go(h_copy(8 + d))

    def h6():
        for d in range(2):
            h_copy(8 + d).wait_recv()
        for k in range(2):
            hx_sum[k, x] = (wide(hx_sum[k, x]) + wide(hx_full[0, k]) + wide(hx_full[1, k])).astype(BF16)
        go(h_copy(10))

    def h7():
        h_copy(10).wait_recv()
        hid_out[...] = wide(hx_sum[zl, x]) + wide(hx_z[...])

    def q_copy(i):
        if i < 3:
            src, dst, to = p_x.at[3], p_x.at[i], x_to[1 + i]
        elif i == 3:
            src, dst, to = p_z.at[0], p_z.at[1], z_near
        elif i == 4:
            ref = p_all.at[z, y, core]
            src, dst, to = ref, ref, other
        elif i < 8:
            ref = p_all.at[z, y]
            src, dst, to = ref, ref, (right, opposite, left)[i - 5]
        else:
            ref = p_all.at[z]
            src, dst, to = ref, ref, across
        return remote(src, dst, q_s.at[i], q_r.at[i], to)

    def q0():
        a = lax.rem(lax.broadcasted_iota(jnp.int32, pg.shape, 0), SUB)
        b = lax.rem(lax.broadcasted_iota(jnp.int32, pg.shape, 1), SUB)
        p_x[3] = jnp.sum(jnp.where(a == b, pg[...], 0.0).reshape(n_f, SUB, KK * SUB), axis=1)
        for i in range(3):
            go(q_copy(i))

    def q1():
        for i in range(3):
            q_copy(i).wait_recv()
        p_z[0] = p_x[0] + p_x[1] + p_x[2] + p_x[3]
        go(q_copy(3))

    def q2():
        q_copy(3).wait_recv()
        p_all[z, y, core] = p_z[0] + p_z[1]
        go(q_copy(4))

    def q3():
        ref = p_all.at[z, y, 1 - core]
        remote(ref, ref, q_s.at[4], q_r.at[4], other).wait_recv()
        for i in range(3):
            go(q_copy(5 + i))

    def q4():
        for i in range(3):
            ref = p_all.at[z, lax.rem(y + 3 - i, 4)]
            remote(ref, ref, q_s.at[5 + i], q_r.at[5 + i], right).wait_recv()
        go(q_copy(8))

    def q5():
        ref = p_all.at[1 - z]
        remote(ref, ref, q_s.at[8], q_r.at[8], across).wait_recv()
        j = 2 * rep + lax.div(me, 8)
        pg_out[...] = p_all[lax.div(j, 8), lax.rem(lax.div(j, 2), 4), lax.rem(j, 2)]

    own = [pltpu.make_async_copy(dfac.at[p], gbuf.at[p, me], own_sem.at[p]) for p in range(2)]
    for c in own:
        c.start()
    p_copy(0).start()
    for _, n in order[:8]:
        w_copy(n).start()
    pg[...] = jnp.zeros_like(pg)
    kron_t[...] = spread_out(proj[pl.ds(pl.multiple_of(me * n_f, n_f), n_f), :], False)
    barrier((other, right, left, opposite, across, x_to[1], x_to[2], x_to[3], z_near))
    own[0].wait()
    for i, to in enumerate((right, left, across)):
        go(whole(0, 0, 1 + i, to))
    go(to_core(0, 0))
    own[1].wait()
    go(to_core(1, 0))
    go(h_copy(0))
    work(0, 0)
    near(0)
    work(0, 1)
    work(0, 2)
    work(0, 3)
    half_arrived(0, 6)
    work(0, 6)
    far(0)
    for i, to in enumerate((right, left, across)):
        go(whole(1, 0, 1 + i, to))
    work(0, 4)
    work(0, 5)
    half_arrived(0, 7)
    work(0, 7)
    t_start(0)
    work(1, 0)
    t_pass(0, 0)
    near(1)
    t_pass(0, 1)
    work(1, 1)
    t_cross(0)
    work(1, 2)
    half_arrived(1, 6)
    work(1, 3)
    t_finish(0)
    far(1)
    work(1, 6)
    t_spread(0)
    work(1, 4)
    t_relay(0, 0)
    work(1, 5)
    half_arrived(1, 7)
    t_relay(0, 1)
    h1()
    work(1, 7)
    t_start(1)
    q0()
    t_last(0, 0)
    t_last(0, 1)
    h2()
    t_open(1)
    t_pass(1, 0)
    q1()
    t_pass(1, 1)
    h3()
    q2()
    t_cross(1)
    h4()
    q3()
    t_finish(1)
    h5()
    q4()
    t_spread(1)
    h6()
    t_relay(1, 0)
    t_last(1, 0)
    q5()
    h7()
    t_relay(1, 1)
    t_last(1, 1)
    for s in sends:
        s.wait_send()


def backward(dfac, words, pooled, proj, grads):
    _, n_f, emb, _ = pooled.shape
    rows = 8 * HI
    width = emb // 2
    n_grad = grads.shape[2]
    grads = grads.reshape(8, 2, 8, n_grad, 128)
    dma = pltpu.SemaphoreType.DMA
    vmem = pl.BlockSpec(memory_space=pltpu.VMEM)
    hbm = pl.BlockSpec(memory_space=pl.ANY)
    a222 = dma((2, 2, 2))
    return pl.pallas_call(
        bwd_kernel,
        out_shape=(
            jax.ShapeDtypeStruct((n_f, rows, width), BF16),
            jax.ShapeDtypeStruct((n_f, rows, width), BF16),
            jax.ShapeDtypeStruct((n_grad, 128), F32),
            jax.ShapeDtypeStruct((n_f, KK * SUB), F32),
        ),
        in_specs=[vmem, hbm, hbm, vmem, vmem],
        out_specs=(vmem, vmem, vmem, vmem),
        scratch_shapes=[
            pltpu.VMEM((n_f * SUB, KK * SUB), BF16),
            pltpu.VMEM((2, 16, KK, width, 128), BF16),
            pltpu.VMEM((n_f, rows, width), F32),
            pltpu.VMEM((n_f, width, 256), BF16),
            pltpu.VMEM((8, n_f, HI, 256), jnp.int32),
            pltpu.VMEM((2, n_f, width, 256), BF16),
            pltpu.VMEM((2, n_f, rows, width), BF16),
            pltpu.VMEM((2, 2, 2, rows, width), BF16),
            pltpu.VMEM((2, 2, 2, 2, rows, width), BF16),
            pltpu.VMEM((2, 2, rows, width), BF16),
            pltpu.VMEM((3, 2, rows - X_FIRST[1], width), BF16),
            pltpu.VMEM((n_f * SUB, KK * SUB), F32),
            pltpu.VMEM((8, 8, n_grad, 128), BF16),
            pltpu.VMEM((2, 4, 8 * n_grad, 128), BF16),
            pltpu.VMEM((2, 2, 4 * n_grad, 128), BF16),
            pltpu.VMEM((2, 2, 8 * n_grad, 128), BF16),
            pltpu.VMEM((8 * n_grad, 128), BF16),
            pltpu.VMEM((2, 4, n_grad, 128), BF16),
            pltpu.VMEM((2, 2, n_grad // 2, 128), BF16),
            pltpu.VMEM((2, 2, n_grad, 128), BF16),
            pltpu.VMEM((n_grad, 128), BF16),
            pltpu.VMEM((4, n_f, KK * SUB), F32),
            pltpu.VMEM((2, n_f, KK * SUB), F32),
            pltpu.VMEM((2, 4, 2, n_f, KK * SUB), F32),
            dma((2,)), dma((8,)), dma((2,)), dma((2, 8)), dma((2, 8)), dma((2, 6)), dma((2, 6)), a222, a222,
            dma((2, 3)), dma((2, 3)), dma((3,)), dma((3,)), dma((3,)), dma((3,)),
            a222, a222, a222, a222, dma((2,)), dma((2,)), dma((2,)), dma((2,)), a222, a222, a222, a222,
            dma((11,)), dma((11,)), dma((9,)), dma((9,)),
        ],
        compiler_params=pltpu.CompilerParams(collective_id=1, has_side_effects=True, vmem_limit_bytes=VMEM),
        cost_estimate=pl.CostEstimate(flops=20 * 10**9, bytes_accessed=40 * 10**6, transcendentals=0),
    )(dfac, words, pooled, proj, grads)


def local(indices, lengths, tables, proj, w_hidden, w_out, d_logit):
    n_f = indices.shape[0]
    me = lax.axis_index("mp")
    words, pooled, fac = forward(indices, lengths, tables, proj)
    logits, grads, dfac = dense(fac, w_hidden, w_out, d_logit)
    low, high, dense_sum, pg = backward(dfac, words, pooled, proj, grads)
    table_grad = jnp.concatenate([low, high], axis=2).astype(F32)
    feat = w_hidden.shape[1]
    mine = proj.shape[0] // 128
    pg = lax.dynamic_slice_in_dim(pg, lax.rem(me * mine, n_f), mine, 0)
    return (
        logits.reshape(-1),
        table_grad,
        dense_sum[:, :feat],
        dense_sum[:, feat : feat + 3].sum(1),
        pg.reshape(mine, KK, SUB).sum(2),
    )


def solution(mesh):
    in_specs = (
        P("mp", None, "replica"),
        P("mp", "replica"),
        P("mp", None, None),
        P(),
        P(),
        P(),
        P(("replica", "mp")),
    )
    out_specs = (
        P(("replica", "mp")),
        P("mp", None, None),
        P(("replica", "mp"), None),
        P(("replica", "mp")),
        P(("replica", "mp"), None),
    )
    return jax.shard_map(local, mesh=mesh, in_specs=in_specs, out_specs=out_specs, check_vma=False)
```

```python
import functools

import jax
import jax.numpy as jnp
from jax import lax
from jax.experimental import pallas as pl
from jax.experimental.pallas import tpu as pltpu
from jax.sharding import PartitionSpec as P

MESH = pl.DeviceIdType.MESH
K1 = 8
K2 = 8
KK = K1 + K2
SUB = 16
HI = 64
BITS = 4
VMEM = 60 * 1024 * 1024
LOW = 9
LOW_HALF = 5
HIGH_HALF = 13
GATHER_LOW = (9, 12)
X_FIRST = (512, 288)
F32 = jnp.float32
BF16 = jnp.bfloat16


def peers():
    me = lax.axis_index("mp")
    core = lax.rem(me, 2)
    y = lax.rem(lax.div(me, 2), 4)
    z = lax.div(me, 8)
    other = {"mp": me + 1 - 2 * core}
    right = {"mp": z * 8 + lax.rem(y + 1, 4) * 2 + core}
    left = {"mp": z * 8 + lax.rem(y + 3, 4) * 2 + core}
    across = {"mp": (1 - z) * 8 + y * 2 + core}
    return me, core, y, z, other, right, left, across


def barrier(devices):
    sem = pltpu.get_barrier_semaphore()
    for d in devices:
        pl.semaphore_signal(sem, inc=1, device_id=d, device_id_type=MESH)
    pl.semaphore_wait(sem, len(devices))


def remote(src, dst, send, recv, device):
    return pltpu.make_async_remote_copy(
        src_ref=src, dst_ref=dst, send_sem=send, recv_sem=recv, device_id=device, device_id_type=MESH
    )


def digits(words):
    return jnp.concatenate(
        [(lax.shift_right_logical(words, BITS * d) & 15).astype(F32).astype(BF16) for d in range(8)], axis=0
    )


def nt(a, b):
    return lax.dot_general(a, b, (((1,), (1,)), ((), ())), preferred_element_type=F32)


def tn(a, b):
    return lax.dot_general(a, b, (((0,), (0,)), ((), ())), preferred_element_type=F32)


def spread_out(here, flip):
    n = here.shape[0] * SUB
    owner = lax.div(lax.broadcasted_iota(jnp.int32, (n, KK), 0), SUB)
    pick = (owner == lax.broadcasted_iota(jnp.int32, (n, KK), 1)).astype(F32).astype(BF16)
    rows = (nt(pick, here) if flip else jnp.dot(pick, here, preferred_element_type=F32)).astype(BF16)
    full = nt(rows, pick)
    a = lax.rem(lax.broadcasted_iota(jnp.int32, (n, n), 0), SUB)
    b = lax.rem(lax.broadcasted_iota(jnp.int32, (n, n), 1), SUB)
    return jnp.where(a == b, full, 0.0).astype(BF16)


def fwd_kernel(
    idx, lens, tab, proj, words_out, pooled_out, fac_out,
    kron, tab_t, sbuf, rcore, rhalf, rfull, rz, rshare, wbuf, pbuf,
    core_s, core_r, half_s, half_r, full_s, full_r, z_s, z_r, share_s, share_r, w_sem, p_sem,
):
    me, core, y, z, other, right, left, across = peers()
    n_f = idx.shape[0]
    emb = tab.shape[2]

    def chunk_of(t):
        early, late = 1 - jnp.minimum(lax.div(t, 2), 1), lax.div(t, 6)
        mid = 1 - early - late
        dy = early * 2 + mid * (1 + 2 * lax.rem(t, 2))
        zo = early * t + mid * lax.div(t - 2 + 2 * early, 2) + late * (t - 6)
        return lax.rem(z + 1 + zo, 2) * 4 + lax.rem(y + dy, 4)

    def p_copy(t):
        slot = lax.rem(t, 2)
        return pltpu.make_async_copy(pbuf.at[slot], pooled_out.at[chunk_of(t)], p_sem.at[slot])

    def w_copy(t):
        return pltpu.make_async_copy(wbuf.at[t], words_out.at[chunk_of(t)], w_sem.at[t])

    def core_copy(t):
        return remote(sbuf.at[t, 1 - core], rcore.at[t], core_s.at[t], core_r.at[t], other)

    def half_range(part, d):
        return ((0, LOW_HALF), (LOW_HALF, LOW), (LOW, HIGH_HALF), (HIGH_HALF, KK))[2 * part + d]

    def half_copy(i, d):
        low, high = half_range(i // 2, d)
        zo, ks = min(i, 1), pl.ds(low, high - low)
        return remote(
            sbuf.at[zo, core, ks], rhalf.at[zo, ks], half_s.at[i, d], half_r.at[i, d], (right, left)[d]
        )

    def full_copy(zo, d):
        ks = pl.ds(0, KK if zo else LOW)
        return remote(
            sbuf.at[2 + 2 * zo + d, core, ks], rfull.at[zo, d, ks], full_s.at[zo, d], full_r.at[zo, d], (right, left)[d]
        )

    def share_copy(i):
        t = (0, 2, 3, 6)[i]
        return remote(sbuf.at[t, core, pl.ds(LOW, KK - LOW)], rshare.at[i], share_s.at[i], share_r.at[i], across)

    def z_copy():
        return remote(sbuf.at[6, core, pl.ds(0, LOW)], rz, z_s, z_r, across)

    def compute(t, start=False):
        q = chunk_of(t)
        slot = lax.rem(t, 2)
        where = pl.ds(pl.multiple_of(q * 256, 256), 256)
        if not start:

            @pl.when(t >= 2)
            def _():
                p_copy(t - 2).wait()

        else:
            eye = (
                lax.broadcasted_iota(jnp.int32, (emb, emb), 0) == lax.broadcasted_iota(jnp.int32, (emb, emb), 1)
            ).astype(F32).astype(BF16)

        def field(f, carry):
            ids = idx[f, :, where]
            live = lens[pl.ds(f, 1), where]
            lane_slot = lax.broadcasted_iota(jnp.int32, ids.shape, 0)
            hi = ids & (HI - 1)
            val = jnp.where(lane_slot < live, jnp.left_shift(1, BITS * lax.shift_right_logical(ids, 6)), 0)
            rows = lax.broadcasted_iota(jnp.int32, (HI, 256), 0)
            words = jnp.zeros((HI, 256), jnp.int32)
            for s in range(8):
                words = words + jnp.where(hi[s : s + 1, :] == rows, val[s : s + 1, :], 0)
            wbuf[t, f] = words
            if start:
                table = nt(eye, tab[f]).astype(BF16)
                tab_t[f] = table
            else:
                table = tab_t[f]
            pooled = jnp.dot(table, digits(words), preferred_element_type=F32)
            pbuf[slot, f] = pooled.astype(BF16)
            return carry

        lax.fori_loop(0, n_f, field, 0, unroll=4)
        p_copy(t).start()
        w_copy(t).start()

        def block(eb, carry):
            rows = pl.ds(pl.multiple_of(eb * SUB, SUB), SUB)
            x = pbuf[slot, :, rows, :].reshape(n_f * SUB, 256)
            part = jnp.dot(kron[...], x, preferred_element_type=F32).astype(BF16).reshape(KK, SUB, 256)
            sbuf[t, 0, :, rows, :] = part[:, :, :128]
            sbuf[t, 1, :, rows, :] = part[:, :, 128:]
            return carry

        lax.fori_loop(0, emb // SUB, block, 0, unroll=8)
        if not start:
            core_copy(t).start()

    def add(t, parts, out=None):
        edges = sorted({e for _, _, a, b in parts for e in (a, b)})
        for low, high in zip(edges, edges[1:]):
            refs = [(r, base) for r, base, a, b in parts if a <= low and high <= b]

            def one(k, carry, refs=refs):
                total = sbuf[t, core, k].astype(F32)
                for r, base in refs:
                    total = total + r[k - base].astype(F32)
                if out is None:
                    sbuf[t, core, k] = total.astype(BF16)
                else:
                    out[k] = total
                return carry

            lax.fori_loop(low, high, one, 0)

    def near(t):
        core_copy(t).wait_recv()
        return (rcore.at[t], 0, 0, KK)

    def share(i):
        share_copy(i).wait_recv()
        return (rshare.at[i], LOW, LOW, KK)

    def opposite(zo):
        add(zo, [near(zo)])
        for d in range(2):
            half_copy(zo, d).start()
        if not zo:
            share_copy(0).start()

    def opposite_rest():
        add(1, [share(0)])
        for d in range(2):
            half_copy(2, d).start()

    def side(zo, d):
        t = 2 + 2 * zo + d
        half_copy(zo, d).wait_recv()
        parts = [near(t), (rhalf.at[zo], 0, *half_range(0, d))]
        if zo:
            half_copy(2, d).wait_recv()
            parts += [(rhalf.at[zo], 0, *half_range(1, d)), share(1 + d)]
        add(t, parts)
        full_copy(zo, d).start()
        if not zo:
            share_copy(1 + d).start()

    def own_share():
        add(6, [near(6)])
        share_copy(3).start()

    def own(zo):
        for d in range(2):
            full_copy(zo, d).wait_recv()
        parts = [(rfull.at[zo, d], 0, 0, KK if zo else LOW) for d in range(2)]
        if zo:
            z_copy().wait_recv()
            add(7, [near(7), *parts, (rz, 0, 0, LOW), share(3)], fac_out)
        else:
            add(6, parts)
            z_copy().start()

    def span(a, b):
        def step(t, carry):
            compute(t)
            return carry

        lax.fori_loop(a, b, step, 0)

    kron[...] = spread_out(proj[pl.ds(pl.multiple_of(me * n_f, n_f), n_f), :], True)
    compute(0, True)
    barrier((other, right, left, across))
    core_copy(0).start()
    opposite(0)
    span(1, 2)
    opposite(1)
    span(2, 3)
    side(0, 0)
    opposite_rest()
    span(3, 4)
    side(0, 1)
    span(4, 6)
    side(1, 0)
    side(1, 1)
    span(6, 7)
    own_share()
    own(0)
    span(7, 8)
    own(1)

    for t in range(8):
        core_copy(t).wait_send()
        w_copy(t).wait()
    for zo in range(2):
        for d in range(2):
            full_copy(zo, d).wait_send()
    for i in range(3):
        for d in range(2):
            half_copy(i, d).wait_send()
    for i in range(4):
        share_copy(i).wait_send()
    z_copy().wait_send()
    p_copy(6).wait()
    p_copy(7).wait()


def forward(indices, lengths, tables, proj):
    n_f, _, emb = tables.shape
    dma = pltpu.SemaphoreType.DMA
    vmem = pl.BlockSpec(memory_space=pltpu.VMEM)
    hbm = pl.BlockSpec(memory_space=pl.ANY)
    return pl.pallas_call(
        fwd_kernel,
        out_shape=(
            jax.ShapeDtypeStruct((8, n_f, HI, 256), jnp.int32),
            jax.ShapeDtypeStruct((8, n_f, emb, 256), BF16),
            jax.ShapeDtypeStruct((KK, emb, 128), F32),
        ),
        in_specs=[vmem] * 4,
        out_specs=(hbm, hbm, vmem),
        scratch_shapes=[
            pltpu.VMEM((n_f * SUB, KK * SUB), BF16),
            pltpu.VMEM((n_f, emb, 8 * HI), BF16),
            pltpu.VMEM((8, 2, KK, emb, 128), BF16),
            pltpu.VMEM((8, KK, emb, 128), BF16),
            pltpu.VMEM((2, KK, emb, 128), BF16),
            pltpu.VMEM((2, 2, KK, emb, 128), BF16),
            pltpu.VMEM((LOW, emb, 128), BF16),
            pltpu.VMEM((4, KK - LOW, emb, 128), BF16),
            pltpu.VMEM((8, n_f, HI, 256), jnp.int32),
            pltpu.VMEM((2, n_f, emb, 256), BF16),
            dma((8,)), dma((8,)), dma((3, 2)), dma((3, 2)), dma((2, 2)), dma((2, 2)), dma, dma, dma((4,)), dma((4,)),
            dma((8,)), dma((2,)),
        ],
        compiler_params=pltpu.CompilerParams(collective_id=0, has_side_effects=True, vmem_limit_bytes=VMEM),
        cost_estimate=pl.CostEstimate(flops=15 * 10**9, bytes_accessed=40 * 10**6, transcendentals=0),
    )(indices, lengths, tables, proj)


def dense_kernel(fac, wh_t, wo_row, dl, logits, grads, dfac, inter):
    n_feat, hid = wh_t.shape
    emb = fac.shape[1]
    step = grads.shape[0] * grads.shape[2]

    def left(i, carry):
        a = fac[i]
        for j in range(K2):
            inter[pl.ds(i * K2 + j, 1), :] = jnp.sum(a * fac[K1 + j], axis=0, keepdims=True)
        return carry

    lax.fori_loop(0, K1, left, 0, unroll=2)
    feat = inter[...].astype(BF16)
    row = dl[...]
    n = row.shape[1]
    d0 = row.astype(BF16)
    r1 = row - d0.astype(F32)
    d1 = r1.astype(BF16)
    d2 = (r1 - d1.astype(F32)).astype(BF16)
    sub = lax.broadcasted_iota(jnp.int32, (n_feat, n), 0)
    d_rows = jnp.where(
        sub == 0, d0.astype(F32), jnp.where(sub == 1, d1.astype(F32), jnp.where(sub == 2, d2.astype(F32), 0.0))
    ).astype(BF16)
    nil = jnp.zeros((n_feat, n), BF16)
    feat_low = jnp.concatenate([feat, nil], axis=0)
    d_high = jnp.concatenate([nil, d_rows], axis=0)
    ones = jnp.ones((8, n), BF16)

    def top(c, carry):
        logit_acc, d_inter = carry
        at = pl.ds(pl.multiple_of(c * step, step), step)
        w = wh_t[:, at]
        v = tn(w, feat)
        wo = jnp.broadcast_to(wo_row[:, at].astype(F32), (8, step))
        top_row = lax.broadcasted_iota(jnp.int32, (8, step), 0) == 0
        wo_cols = tn(jnp.where(top_row, wo, 0.0).astype(BF16), ones)
        s = jax.nn.sigmoid(v)
        hidden = (v * s).astype(BF16)
        logit_acc = logit_acc + jnp.dot(wo.astype(BF16), hidden, preferred_element_type=F32)
        d_hidden = (wo_cols * row * s * (1.0 + v * (1.0 - s))).astype(BF16)
        grad = nt(d_hidden, feat_low) + nt(hidden, d_high)
        grads[:, pl.ds(c, 1), :, :] = grad.astype(BF16).reshape(grads.shape[0], 1, grads.shape[2], 2 * n_feat)
        d_inter = d_inter + jnp.dot(w, d_hidden, preferred_element_type=F32)
        return logit_acc, d_inter

    logit_acc, d_inter = lax.fori_loop(
        0, hid // step, top, (jnp.zeros((8, n), F32), jnp.zeros((n_feat, n), F32)), unroll=2
    )
    logits[...] = logit_acc[0:1]
    inter[...] = d_inter

    def back(eb, carry):
        p = lax.div(eb, emb // SUB // 2)
        rows = pl.ds(pl.multiple_of(eb * SUB, SUB), SUB)
        low = pl.ds(pl.multiple_of(lax.rem(eb, emb // SUB // 2) * SUB, SUB), SUB)
        right = [fac[K1 + j, rows, :] for j in range(K2)]
        d_right = [jnp.zeros((SUB, n), F32) for _ in range(K2)]
        for i in range(K1):
            a = fac[i, rows, :]
            d_left = jnp.zeros((SUB, n), F32)
            for j in range(K2):
                g = inter[pl.ds(i * K2 + j, 1), :]
                d_left = d_left + g * right[j]
                d_right[j] = d_right[j] + g * a
            dfac[p, i, low, :] = d_left.astype(BF16)
        for j in range(K2):
            dfac[p, K1 + j, low, :] = d_right[j].astype(BF16)
        return carry

    lax.fori_loop(0, emb // SUB, back, 0, unroll=2)


def dense(fac, w_hidden, w_out, d_logit):
    hid, feat = w_hidden.shape
    n = d_logit.shape[0]
    return pl.pallas_call(
        dense_kernel,
        out_shape=(
            jax.ShapeDtypeStruct((1, n), F32),
            jax.ShapeDtypeStruct((16, 8, hid // 128, 2 * feat), BF16),
            jax.ShapeDtypeStruct((2, KK, fac.shape[1] // 2, n), BF16),
        ),
        scratch_shapes=[pltpu.VMEM((feat, n), F32)],
        compiler_params=pltpu.CompilerParams(vmem_limit_bytes=VMEM),
        cost_estimate=pl.CostEstimate(flops=10**9, bytes_accessed=10**7, transcendentals=10**6),
    )(fac, w_hidden.T, w_out[None, :], d_logit[None, :])


def bwd_kernel(
    dfac, words, pooled, proj, grads,
    tg_low, tg_high, hid_out, pg_out,
    kron_t, gbuf, acc, dpool, wbuf, pbuf, tbuf, t_half, t_full, t_z, t_share, pg,
    h_core, h_sum, h_half, h_full, h_z, hx_sum, hx_half, hx_full, hx_z, p_x, p_z, p_all,
    own_sem, w_sem, p_sem, core_s, core_r, ici_s, ici_r, half_s, half_r, rest_s, rest_r, ts_s, ts_r, gr_s, gr_r,
    th_s, th_r, tf_s, tf_r, tz_s, tz_r, gz_s, gz_r, gx_s, gx_r, gh_s, gh_r, h_s, h_r, q_s, q_r,
):
    me, core, y, z, other, right, left, across = peers()
    opposite = {"mp": z * 8 + lax.rem(y + 2, 4) * 2 + core}
    rep = lax.axis_index("replica")
    x = lax.rem(rep, 4)
    zl = lax.div(rep, 4)
    x_to = [None] + [{"replica": zl * 4 + lax.rem(x + d, 4)} for d in (1, 2, 3)]
    x_right, x_left = x_to[1], x_to[3]
    z_near = {"replica": (1 - zl) * 4 + x}
    n_f = tbuf.shape[1]
    width = dpool.shape[1]
    places = ((0, 0), (0, 3), (0, 1), (1, 0), (1, 3), (1, 1), (0, 2), (1, 2))
    order = [(p, n) for p in range(2) for n in (0, 1, 2, 3, 6, 4, 5, 7)]
    sends = []
    tg_out = (tg_low, tg_high)

    def go(copy):
        copy.start()
        sends.append(copy)

    def chip(n):
        dz, dy = places[n]
        return lax.rem(z + dz, 2) * 4 + lax.rem(y + dy, 4)

    def block(n):
        return chip(n) * 2 + core

    def to_core(p, n):
        ref = gbuf.at[p, block(n)]
        return remote(ref, ref, core_s.at[p, n], core_r.at[p, n], other)

    def from_core(p, n):
        ref = gbuf.at[p, chip(n) * 2 + 1 - core]
        remote(ref, ref, core_s.at[p, n], core_r.at[p, n], other).wait_recv()

    def whole(p, n, m, device):
        ref = gbuf.at[p, block(n), pl.ds(0, GATHER_LOW[p] if m in (4, 5) else KK)]
        return remote(ref, ref, ici_s.at[p, m], ici_r.at[p, m], device)

    def arrived(p, m):
        whole(p, m, m, right).wait_recv()

    def half(p, n, m, d):
        cut, top = (K1, KK) if m == 6 else ((GATHER_LOW[p] + 1) // 2, GATHER_LOW[p])
        ref = gbuf.at[p, block(n), pl.ds(cut, top - cut) if d else pl.ds(0, cut)]
        i = (p, m - 6, d)
        return remote(ref, ref, half_s.at[i], half_r.at[i], (right, left)[d])

    def rest(p, n):
        ref = gbuf.at[p, block(n), pl.ds(GATHER_LOW[p], KK - GATHER_LOW[p])]
        i = (1, 2, 6).index(n)
        return remote(ref, ref, rest_s.at[p, i], rest_r.at[p, i], across)

    def rest_arrived(p, m):
        ref = gbuf.at[p, block(m), pl.ds(GATHER_LOW[p], KK - GATHER_LOW[p])]
        i = (4, 5, 7).index(m)
        remote(ref, ref, rest_s.at[p, i], rest_r.at[p, i], across).wait_recv()

    def half_arrived(p, m):
        for d in range(2):
            half(p, m, m, d).wait_recv()
        if m == 6:
            go(rest(p, 6))
        else:
            rest_arrived(p, 7)
        go(to_core(p, m))

    def near(p):
        for d in range(2):
            arrived(p, 1 + d)
            go(half(p, 1 + d, 6, d))
            go(rest(p, 1 + d))
            go(to_core(p, 1 + d))
        arrived(p, 3)
        go(whole(p, 3, 4, right))
        go(whole(p, 3, 5, left))
        go(to_core(p, 3))

    def far(p):
        for d in range(2):
            arrived(p, 4 + d)
            go(half(p, 4 + d, 7, d))
        for d in range(2):
            rest_arrived(p, 4 + d)
            go(to_core(p, 4 + d))

    def w_copy(n):
        return pltpu.make_async_copy(words.at[chip(n)], wbuf.at[n], w_sem.at[n])

    def p_copy(i):
        p, n = order[i]
        return pltpu.make_async_copy(
            pooled.at[chip(n), :, pl.ds(p * width, width), :], pbuf.at[i % 2], p_sem.at[i % 2]
        )

    def work(p, n):
        i = order.index((p, n))
        p_copy(i).wait()
        if i + 1 < len(order):
            p_copy(i + 1).start()
        if p == 0:
            w_copy(n).wait()
        from_core(p, n)
        slot = i % 2
        base = chip(n) * 2

        def spread(eb, carry):
            rows = pl.ds(pl.multiple_of(eb * SUB, SUB), SUB)
            g = jnp.concatenate(
                [gbuf[p, base + c, :, rows, :].reshape(KK * SUB, 128) for c in range(2)], axis=1
            )
            d = jnp.dot(kron_t[...], g, preferred_element_type=F32).astype(BF16)
            dpool[:, rows, :] = d.reshape(n_f, SUB, 256)
            pg[...] += nt(pbuf[slot, :, rows, :].reshape(n_f * SUB, 256), g)
            return carry

        lax.fori_loop(0, width // SUB, spread, 0, unroll=8)

        def field(f, carry):
            part = nt(digits(wbuf[n, f]), dpool[f])
            if n == 0:
                acc[f] = part
            elif n == 7:
                tbuf[p, f] = (acc[f] + part).astype(BF16)
            else:
                acc[f] += part
            return carry

        lax.fori_loop(0, n_f, field, 0, unroll=4)

    def first(dx, zo):
        return (lax.rem(zl + 1 + zo, 2) * 4 + lax.rem(x + dx, 4)) * 2

    n_rows = tbuf.shape[2]

    def low(p, zo):
        return pl.ds(0, n_rows if zo else X_FIRST[p])

    def high(p):
        return pl.ds(X_FIRST[p], n_rows - X_FIRST[p])

    def split(p):
        return X_FIRST[p] < n_rows

    def t_half_copy(p, zo, d):
        i = (p, zo, d)
        src = tbuf.at[p, first(2, zo) + d, low(p, zo)]
        return remote(src, t_half.at[p, zo, d, low(p, zo)], th_s.at[i], th_r.at[i], (x_right, x_left)[d])

    def t_full_copy(p, zo, d):
        i = (p, zo, d)
        src = tbuf.at[p, pl.ds(first(1 + 2 * d, zo), 2), low(p, zo)]
        return remote(src, t_full.at[p, zo, d, :, low(p, zo)], tf_s.at[i], tf_r.at[i], (x_right, x_left)[d])

    def t_share_copy(p, i):
        src = tbuf.at[p, pl.ds(first((2, 1, 3)[i], 0), 2), high(p)]
        return remote(src, t_share.at[i], ts_s.at[i], ts_r.at[i], z_near)

    def t_z_copy(p):
        return remote(tbuf.at[p, pl.ds(first(0, 0), 2)], t_z.at[p], tz_s.at[p], tz_r.at[p], z_near)

    def g_x_copy(p, zb, d, dx=0):
        ref = tg_out[p].at[pl.ds(first(dx, 1 - zb), 2), low(p, 1 - zb)]
        i = (p, zb, d)
        return remote(ref, ref, gx_s.at[i], gx_r.at[i], (x_right, x_left)[d])

    def g_z_copy(p, zb):
        ref = tg_out[p].at[pl.ds(first(0, 1 - zb), 2)]
        return remote(ref, ref, gz_s.at[p], gz_r.at[p], z_near)

    def g_half_copy(p, zb, d, dx):
        ref = tg_out[p].at[first(dx, 1 - zb) + d, low(p, 1 - zb)]
        i = (p, zb, d)
        return remote(ref, ref, gh_s.at[i], gh_r.at[i], (x_right, x_left)[d])

    def g_rest_copy(p, zb, i):
        ref = tg_out[p].at[pl.ds(first((3, 1, 2)[i], 1 - zb), 2), high(p)]
        return remote(ref, ref, gr_s.at[i], gr_r.at[i], z_near)

    def t_start(p):
        for zo in range(1 if split(p) else 2):
            for d in range(2):
                go(t_half_copy(p, zo, d))
        if split(p):
            go(t_share_copy(p, 0))

    def take_share(p, i):
        t_share_copy(p, i).wait_recv()
        for k in range(2):
            at = first((2, 1, 3)[i], 1) + k
            tbuf[p, at, high(p)] = (tbuf[p, at, high(p)].astype(F32) + t_share[i, k].astype(F32)).astype(BF16)

    def t_open(p):
        go(t_share_copy(p, 1))
        go(t_share_copy(p, 2))
        take_share(p, 0)
        for d in range(2):
            go(t_half_copy(p, 1, d))

    def t_pass(p, zo):
        for d in range(2):
            t_half_copy(p, zo, d).wait_recv()
            at, rows = first(1 + 2 * d, zo) + d, low(p, zo)
            tbuf[p, at, rows] = (tbuf[p, at, rows].astype(F32) + t_half[p, zo, d, rows].astype(F32)).astype(BF16)
            if zo and split(p):
                take_share(p, 1 + d)
            go(t_full_copy(p, zo, d))

    def t_total(p, zo, k):
        rows = low(p, zo)
        total = tbuf[p, first(0, zo) + k, rows].astype(F32)
        return total + t_full[p, zo, 0, k, rows].astype(F32) + t_full[p, zo, 1, k, rows].astype(F32)

    def t_cross(p):
        for d in range(2):
            t_full_copy(p, 0, d).wait_recv()
        for k in range(2):
            tbuf[p, first(0, 0) + k, low(p, 0)] = t_total(p, 0, k).astype(BF16)
        go(t_z_copy(p))

    def t_finish(p):
        for d in range(2):
            t_full_copy(p, 1, d).wait_recv()
        t_z_copy(p).wait_recv()
        for k in range(2):
            tg_out[p][first(0, 1) + k] = (t_total(p, 1, k) + t_z[p, k].astype(F32)).astype(BF16)
        go(g_z_copy(p, 0))
        for d in range(2):
            go(g_x_copy(p, 0, d))

    def t_spread(p):
        g_z_copy(p, 1).wait_recv()
        for d in range(2):
            go(g_x_copy(p, 1, d))

    def t_relay(p, zb):
        for d in range(2):
            dx = 3 - 2 * d
            g_x_copy(p, zb, d, dx).wait_recv()
            go(g_half_copy(p, zb, d, dx))
            if not zb and split(p):
                go(g_rest_copy(p, 0, d))

    def t_last(p, zb):
        for d in range(2):
            g_half_copy(p, zb, d, 2).wait_recv()
        if split(p):
            if zb:
                for i in range(3):
                    g_rest_copy(p, 1, i).wait_recv()
            else:
                go(g_rest_copy(p, 0, 2))

    def h_copy(i):
        if i == 0:
            src, dst, to = grads.at[:, 1 - core], h_core, other
        elif i < 3:
            d = i - 1
            src, dst, to = h_sum.at[:, lax.rem(y + 2, 4), pl.ds(d * 128, 128)], h_half.at[d], (right, left)[d]
        elif i < 5:
            d = i - 3
            src, dst, to = h_sum.at[:, lax.rem(y + 1 + 2 * d, 4)], h_full.at[d], (right, left)[d]
        elif i == 5:
            src, dst, to = h_sum.at[1 - z, y], h_z, across
        elif i < 8:
            d = i - 6
            src, dst, to = hx_sum.at[:, lax.rem(x + 2, 4), pl.ds(d * 16, 16)], hx_half.at[d], (x_right, x_left)[d]
        elif i < 10:
            d = i - 8
            src, dst, to = hx_sum.at[:, lax.rem(x + 1 + 2 * d, 4)], hx_full.at[d], (x_right, x_left)[d]
        else:
            src, dst, to = hx_sum.at[1 - zl, x], hx_z, z_near
        return remote(src, dst, h_s.at[i], h_r.at[i], to)

    def wide(v):
        return v.astype(F32)

    def h1():
        h_copy(0).wait_recv()
        for q in range(8):
            total = wide(grads[q, core]) + wide(h_core[q])
            h_sum[q // 4, q % 4] = total.astype(BF16).reshape(h_sum.shape[2:])
        go(h_copy(1))
        go(h_copy(2))

    def h2():
        for d in range(2):
            h_copy(1 + d).wait_recv()
            at, rows = lax.rem(y + 1 + 2 * d, 4), pl.ds(d * 128, 128)
            for k in range(2):
                h_sum[k, at, rows] = (wide(h_sum[k, at, rows]) + wide(h_half[d, k])).astype(BF16)
            go(h_copy(3 + d))

    def h3():
        for d in range(2):
            h_copy(3 + d).wait_recv()
        for k in range(2):
            h_sum[k, y] = (wide(h_sum[k, y]) + wide(h_full[0, k]) + wide(h_full[1, k])).astype(BF16)
        go(h_copy(5))

    def h4():
        h_copy(5).wait_recv()
        total = (wide(h_sum[z, y]) + wide(h_z[...])).astype(BF16).reshape(8, 32, 128)
        for q in range(8):
            hx_sum[q // 4, q % 4] = total[q]
        go(h_copy(6))
        go(h_copy(7))

    def h5():
        for d in range(2):
            h_copy(6 + d).wait_recv()
            at, rows = lax.rem(x + 1 + 2 * d, 4), pl.ds(d * 16, 16)
            for k in range(2):
                hx_sum[k, at, rows] = (wide(hx_sum[k, at, rows]) + wide(hx_half[d, k])).astype(BF16)
            go(h_copy(8 + d))

    def h6():
        for d in range(2):
            h_copy(8 + d).wait_recv()
        for k in range(2):
            hx_sum[k, x] = (wide(hx_sum[k, x]) + wide(hx_full[0, k]) + wide(hx_full[1, k])).astype(BF16)
        go(h_copy(10))

    def h7():
        h_copy(10).wait_recv()
        hid_out[...] = wide(hx_sum[zl, x]) + wide(hx_z[...])

    def q_copy(i):
        if i < 3:
            src, dst, to = p_x.at[3], p_x.at[i], x_to[1 + i]
        elif i == 3:
            src, dst, to = p_z.at[0], p_z.at[1], z_near
        elif i == 4:
            ref = p_all.at[z, y, core]
            src, dst, to = ref, ref, other
        elif i < 8:
            ref = p_all.at[z, y]
            src, dst, to = ref, ref, (right, opposite, left)[i - 5]
        else:
            ref = p_all.at[z]
            src, dst, to = ref, ref, across
        return remote(src, dst, q_s.at[i], q_r.at[i], to)

    def q0():
        a = lax.rem(lax.broadcasted_iota(jnp.int32, pg.shape, 0), SUB)
        b = lax.rem(lax.broadcasted_iota(jnp.int32, pg.shape, 1), SUB)
        p_x[3] = jnp.sum(jnp.where(a == b, pg[...], 0.0).reshape(n_f, SUB, KK * SUB), axis=1)
        for i in range(3):
            go(q_copy(i))

    def q1():
        for i in range(3):
            q_copy(i).wait_recv()
        p_z[0] = p_x[0] + p_x[1] + p_x[2] + p_x[3]
        go(q_copy(3))

    def q2():
        q_copy(3).wait_recv()
        p_all[z, y, core] = p_z[0] + p_z[1]
        go(q_copy(4))

    def q3():
        ref = p_all.at[z, y, 1 - core]
        remote(ref, ref, q_s.at[4], q_r.at[4], other).wait_recv()
        for i in range(3):
            go(q_copy(5 + i))

    def q4():
        for i in range(3):
            ref = p_all.at[z, lax.rem(y + 3 - i, 4)]
            remote(ref, ref, q_s.at[5 + i], q_r.at[5 + i], right).wait_recv()
        go(q_copy(8))

    def q5():
        ref = p_all.at[1 - z]
        remote(ref, ref, q_s.at[8], q_r.at[8], across).wait_recv()
        j = 2 * rep + lax.div(me, 8)
        pg_out[...] = p_all[lax.div(j, 8), lax.rem(lax.div(j, 2), 4), lax.rem(j, 2)]

    own = [pltpu.make_async_copy(dfac.at[p], gbuf.at[p, me], own_sem.at[p]) for p in range(2)]
    for c in own:
        c.start()
    p_copy(0).start()
    for _, n in order[:8]:
        w_copy(n).start()
    pg[...] = jnp.zeros_like(pg)
    kron_t[...] = spread_out(proj[pl.ds(pl.multiple_of(me * n_f, n_f), n_f), :], False)
    barrier((other, right, left, opposite, across, x_to[1], x_to[2], x_to[3], z_near))
    own[0].wait()
    for i, to in enumerate((right, left, across)):
        go(whole(0, 0, 1 + i, to))
    go(to_core(0, 0))
    own[1].wait()
    go(to_core(1, 0))
    go(h_copy(0))
    work(0, 0)
    near(0)
    work(0, 1)
    work(0, 2)
    work(0, 3)
    half_arrived(0, 6)
    work(0, 6)
    far(0)
    for i, to in enumerate((right, left, across)):
        go(whole(1, 0, 1 + i, to))
    work(0, 4)
    work(0, 5)
    half_arrived(0, 7)
    work(0, 7)
    t_start(0)
    near(1)
    work(1, 0)
    t_pass(0, 0)
    work(1, 1)
    t_pass(0, 1)
    work(1, 2)
    t_cross(0)
    half_arrived(1, 6)
    work(1, 3)
    far(1)
    t_finish(0)
    work(1, 6)
    half_arrived(1, 7)
    work(1, 4)
    t_spread(0)
    work(1, 5)
    t_relay(0, 0)
    h1()
    work(1, 7)
    t_start(1)
    q0()
    t_open(1)
    t_relay(0, 1)
    h2()
    t_pass(1, 0)
    q1()
    t_pass(1, 1)
    h3()
    q2()
    t_cross(1)
    h4()
    q3()
    t_finish(1)
    h5()
    q4()
    t_spread(1)
    h6()
    t_relay(1, 0)
    t_last(1, 0)
    t_relay(1, 1)
    q5()
    h7()
    t_last(0, 0)
    t_last(0, 1)
    t_last(1, 1)
    for s in sends:
        s.wait_send()


def backward(dfac, words, pooled, proj, grads):
    _, n_f, emb, _ = pooled.shape
    rows = 8 * HI
    width = emb // 2
    n_grad = grads.shape[2]
    grads = grads.reshape(8, 2, 8, n_grad, 128)
    dma = pltpu.SemaphoreType.DMA
    vmem = pl.BlockSpec(memory_space=pltpu.VMEM)
    hbm = pl.BlockSpec(memory_space=pl.ANY)
    a222 = dma((2, 2, 2))
    return pl.pallas_call(
        bwd_kernel,
        out_shape=(
            jax.ShapeDtypeStruct((n_f, rows, width), BF16),
            jax.ShapeDtypeStruct((n_f, rows, width), BF16),
            jax.ShapeDtypeStruct((n_grad, 128), F32),
            jax.ShapeDtypeStruct((n_f, KK * SUB), F32),
        ),
        in_specs=[vmem, hbm, hbm, vmem, vmem],
        out_specs=(vmem, vmem, vmem, vmem),
        scratch_shapes=[
            pltpu.VMEM((n_f * SUB, KK * SUB), BF16),
            pltpu.VMEM((2, 16, KK, width, 128), BF16),
            pltpu.VMEM((n_f, rows, width), F32),
            pltpu.VMEM((n_f, width, 256), BF16),
            pltpu.VMEM((8, n_f, HI, 256), jnp.int32),
            pltpu.VMEM((2, n_f, width, 256), BF16),
            pltpu.VMEM((2, n_f, rows, width), BF16),
            pltpu.VMEM((2, 2, 2, rows, width), BF16),
            pltpu.VMEM((2, 2, 2, 2, rows, width), BF16),
            pltpu.VMEM((2, 2, rows, width), BF16),
            pltpu.VMEM((3, 2, rows - X_FIRST[1], width), BF16),
            pltpu.VMEM((n_f * SUB, KK * SUB), F32),
            pltpu.VMEM((8, 8, n_grad, 128), BF16),
            pltpu.VMEM((2, 4, 8 * n_grad, 128), BF16),
            pltpu.VMEM((2, 2, 4 * n_grad, 128), BF16),
            pltpu.VMEM((2, 2, 8 * n_grad, 128), BF16),
            pltpu.VMEM((8 * n_grad, 128), BF16),
            pltpu.VMEM((2, 4, n_grad, 128), BF16),
            pltpu.VMEM((2, 2, n_grad // 2, 128), BF16),
            pltpu.VMEM((2, 2, n_grad, 128), BF16),
            pltpu.VMEM((n_grad, 128), BF16),
            pltpu.VMEM((4, n_f, KK * SUB), F32),
            pltpu.VMEM((2, n_f, KK * SUB), F32),
            pltpu.VMEM((2, 4, 2, n_f, KK * SUB), F32),
            dma((2,)), dma((8,)), dma((2,)), dma((2, 8)), dma((2, 8)), dma((2, 6)), dma((2, 6)), a222, a222,
            dma((2, 3)), dma((2, 3)), dma((3,)), dma((3,)), dma((3,)), dma((3,)),
            a222, a222, a222, a222, dma((2,)), dma((2,)), dma((2,)), dma((2,)), a222, a222, a222, a222,
            dma((11,)), dma((11,)), dma((9,)), dma((9,)),
        ],
        compiler_params=pltpu.CompilerParams(collective_id=1, has_side_effects=True, vmem_limit_bytes=VMEM),
        cost_estimate=pl.CostEstimate(flops=20 * 10**9, bytes_accessed=40 * 10**6, transcendentals=0),
    )(dfac, words, pooled, proj, grads)


def local(indices, lengths, tables, proj, w_hidden, w_out, d_logit):
    n_f = indices.shape[0]
    me = lax.axis_index("mp")
    words, pooled, fac = forward(indices, lengths, tables, proj)
    logits, grads, dfac = dense(fac, w_hidden, w_out, d_logit)
    low, high, dense_sum, pg = backward(dfac, words, pooled, proj, grads)
    table_grad = jnp.concatenate([low, high], axis=2).astype(F32)
    feat = w_hidden.shape[1]
    mine = proj.shape[0] // 128
    pg = lax.dynamic_slice_in_dim(pg, lax.rem(me * mine, n_f), mine, 0)
    return (
        logits.reshape(-1),
        table_grad,
        dense_sum[:, :feat],
        dense_sum[:, feat : feat + 3].sum(1),
        pg.reshape(mine, KK, SUB).sum(2),
    )


def solution(mesh):
    in_specs = (
        P("mp", None, "replica"),
        P("mp", "replica"),
        P("mp", None, None),
        P(),
        P(),
        P(),
        P(("replica", "mp")),
    )
    out_specs = (
        P(("replica", "mp")),
        P("mp", None, None),
        P(("replica", "mp"), None),
        P(("replica", "mp")),
        P(("replica", "mp"), None),
    )
    return jax.shard_map(local, mesh=mesh, in_specs=in_specs, out_specs=out_specs, check_vma=False)
```

```python
import functools

import jax
import jax.numpy as jnp
from jax import lax
from jax.experimental import pallas as pl
from jax.experimental.pallas import tpu as pltpu
from jax.sharding import PartitionSpec as P

MESH = pl.DeviceIdType.MESH
K1 = 8
K2 = 8
KK = K1 + K2
SUB = 16
HI = 64
BITS = 4
VMEM = 60 * 1024 * 1024
LOW = 9
LOW_HALF = 5
HIGH_HALF = 13
GATHER_LOW = (9, 12)
X_FIRST = (512, 288)
F32 = jnp.float32
BF16 = jnp.bfloat16


def peers():
    me = lax.axis_index("mp")
    core = lax.rem(me, 2)
    y = lax.rem(lax.div(me, 2), 4)
    z = lax.div(me, 8)
    other = {"mp": me + 1 - 2 * core}
    right = {"mp": z * 8 + lax.rem(y + 1, 4) * 2 + core}
    left = {"mp": z * 8 + lax.rem(y + 3, 4) * 2 + core}
    across = {"mp": (1 - z) * 8 + y * 2 + core}
    return me, core, y, z, other, right, left, across


def barrier(devices):
    sem = pltpu.get_barrier_semaphore()
    for d in devices:
        pl.semaphore_signal(sem, inc=1, device_id=d, device_id_type=MESH)
    pl.semaphore_wait(sem, len(devices))


def remote(src, dst, send, recv, device):
    return pltpu.make_async_remote_copy(
        src_ref=src, dst_ref=dst, send_sem=send, recv_sem=recv, device_id=device, device_id_type=MESH
    )


def digits(words):
    return jnp.concatenate(
        [(lax.shift_right_logical(words, BITS * d) & 15).astype(F32).astype(BF16) for d in range(8)], axis=0
    )


def nt(a, b):
    return lax.dot_general(a, b, (((1,), (1,)), ((), ())), preferred_element_type=F32)


def tn(a, b):
    return lax.dot_general(a, b, (((0,), (0,)), ((), ())), preferred_element_type=F32)


def spread_out(here, flip):
    n = here.shape[0] * SUB
    owner = lax.div(lax.broadcasted_iota(jnp.int32, (n, KK), 0), SUB)
    pick = (owner == lax.broadcasted_iota(jnp.int32, (n, KK), 1)).astype(F32).astype(BF16)
    rows = (nt(pick, here) if flip else jnp.dot(pick, here, preferred_element_type=F32)).astype(BF16)
    full = nt(rows, pick)
    a = lax.rem(lax.broadcasted_iota(jnp.int32, (n, n), 0), SUB)
    b = lax.rem(lax.broadcasted_iota(jnp.int32, (n, n), 1), SUB)
    return jnp.where(a == b, full, 0.0).astype(BF16)


def fwd_kernel(
    idx, lens, tab, proj, words_out, pooled_out, fac_out,
    kron, tab_t, sbuf, rcore, rhalf, rfull, rz, rshare, wbuf, pbuf,
    core_s, core_r, half_s, half_r, full_s, full_r, z_s, z_r, share_s, share_r, w_sem, p_sem,
):
    me, core, y, z, other, right, left, across = peers()
    n_f = idx.shape[0]
    emb = tab.shape[2]

    def chunk_of(t):
        early, late = 1 - jnp.minimum(lax.div(t, 2), 1), lax.div(t, 6)
        mid = 1 - early - late
        dy = early * 2 + mid * (1 + 2 * lax.rem(t, 2))
        zo = early * t + mid * lax.div(t - 2 + 2 * early, 2) + late * (t - 6)
        return lax.rem(z + 1 + zo, 2) * 4 + lax.rem(y + dy, 4)

    def p_copy(t):
        slot = lax.rem(t, 2)
        return pltpu.make_async_copy(pbuf.at[slot], pooled_out.at[chunk_of(t)], p_sem.at[slot])

    def w_copy(t):
        return pltpu.make_async_copy(wbuf.at[t], words_out.at[chunk_of(t)], w_sem.at[t])

    def core_copy(t):
        return remote(sbuf.at[t, 1 - core], rcore.at[t], core_s.at[t], core_r.at[t], other)

    def half_range(part, d):
        return ((0, LOW_HALF), (LOW_HALF, LOW), (LOW, HIGH_HALF), (HIGH_HALF, KK))[2 * part + d]

    def half_copy(i, d):
        low, high = half_range(i // 2, d)
        zo, ks = min(i, 1), pl.ds(low, high - low)
        return remote(
            sbuf.at[zo, core, ks], rhalf.at[zo, ks], half_s.at[i, d], half_r.at[i, d], (right, left)[d]
        )

    def full_copy(zo, d):
        ks = pl.ds(0, KK if zo else LOW)
        return remote(
            sbuf.at[2 + 2 * zo + d, core, ks], rfull.at[zo, d, ks], full_s.at[zo, d], full_r.at[zo, d], (right, left)[d]
        )

    def share_copy(i):
        t = (0, 2, 3)[i]
        return remote(sbuf.at[t, core, pl.ds(LOW, KK - LOW)], rshare.at[i], share_s.at[i], share_r.at[i], across)

    def z_copy():
        return remote(sbuf.at[6, core], rz, z_s, z_r, across)

    def compute(t, start=False):
        q = chunk_of(t)
        slot = lax.rem(t, 2)
        where = pl.ds(pl.multiple_of(q * 256, 256), 256)
        if not start:

            @pl.when(t >= 2)
            def _():
                p_copy(t - 2).wait()

        else:
            eye = (
                lax.broadcasted_iota(jnp.int32, (emb, emb), 0) == lax.broadcasted_iota(jnp.int32, (emb, emb), 1)
            ).astype(F32).astype(BF16)

        def field(f, carry):
            ids = idx[f, :, where]
            live = lens[pl.ds(f, 1), where]
            lane_slot = lax.broadcasted_iota(jnp.int32, ids.shape, 0)
            hi = ids & (HI - 1)
            val = jnp.where(lane_slot < live, jnp.left_shift(1, BITS * lax.shift_right_logical(ids, 6)), 0)
            rows = lax.broadcasted_iota(jnp.int32, (HI, 256), 0)
            words = jnp.zeros((HI, 256), jnp.int32)
            for s in range(8):
                words = words + jnp.where(hi[s : s + 1, :] == rows, val[s : s + 1, :], 0)
            wbuf[t, f] = words
            if start:
                table = nt(eye, tab[f]).astype(BF16)
                tab_t[f] = table
            else:
                table = tab_t[f]
            pooled = jnp.dot(table, digits(words), preferred_element_type=F32)
            pbuf[slot, f] = pooled.astype(BF16)
            return carry

        lax.fori_loop(0, n_f, field, 0, unroll=8)
        p_copy(t).start()
        w_copy(t).start()

        def block(eb, carry):
            rows = pl.ds(pl.multiple_of(eb * SUB, SUB), SUB)
            x = pbuf[slot, :, rows, :].reshape(n_f * SUB, 256)
            part = jnp.dot(kron[...], x, preferred_element_type=F32).astype(BF16).reshape(KK, SUB, 256)
            sbuf[t, 0, :, rows, :] = part[:, :, :128]
            sbuf[t, 1, :, rows, :] = part[:, :, 128:]
            return carry

        lax.fori_loop(0, emb // SUB, block, 0, unroll=8)
        if not start:
            core_copy(t).start()

    def add(t, parts, out=None):
        edges = sorted({e for _, _, a, b in parts for e in (a, b)})
        for low, high in zip(edges, edges[1:]):
            refs = [(r, base) for r, base, a, b in parts if a <= low and high <= b]

            def one(k, carry, refs=refs):
                total = sbuf[t, core, k].astype(F32)
                for r, base in refs:
                    total = total + r[k - base].astype(F32)
                if out is None:
                    sbuf[t, core, k] = total.astype(BF16)
                else:
                    out[k] = total
                return carry

            lax.fori_loop(low, high, one, 0)

    def near(t):
        core_copy(t).wait_recv()
        return (rcore.at[t], 0, 0, KK)

    def share(i):
        share_copy(i).wait_recv()
        return (rshare.at[i], LOW, LOW, KK)

    def opposite(zo):
        add(zo, [near(zo)])
        for d in range(2):
            half_copy(zo, d).start()
        if not zo:
            share_copy(0).start()

    def opposite_rest():
        add(1, [share(0)])
        for d in range(2):
            half_copy(2, d).start()

    def side(zo, d):
        t = 2 + 2 * zo + d
        half_copy(zo, d).wait_recv()
        parts = [near(t), (rhalf.at[zo], 0, *half_range(0, d))]
        if zo:
            half_copy(2, d).wait_recv()
            parts += [(rhalf.at[zo], 0, *half_range(1, d)), share(1 + d)]
        add(t, parts)
        full_copy(zo, d).start()
        if not zo:
            share_copy(1 + d).start()

    def own(zo):
        for d in range(2):
            full_copy(zo, d).wait_recv()
        parts = [near(6 + zo)] + [(rfull.at[zo, d], 0, 0, KK if zo else LOW) for d in range(2)]
        if zo:
            z_copy().wait_recv()
            add(7, parts + [(rz, 0, 0, KK)], fac_out)
        else:
            add(6, parts)
            z_copy().start()

    def span(a, b):
        def step(t, carry):
            compute(t)
            return carry

        lax.fori_loop(a, b, step, 0)

    kron[...] = spread_out(proj[pl.ds(pl.multiple_of(me * n_f, n_f), n_f), :], True)
    compute(0, True)
    barrier((other, right, left, across))
    core_copy(0).start()
    opposite(0)
    span(1, 2)
    opposite(1)
    span(2, 3)
    side(0, 0)
    opposite_rest()
    span(3, 4)
    side(0, 1)
    span(4, 7)
    own(0)
    side(1, 0)
    side(1, 1)
    span(7, 8)
    own(1)

    for t in range(8):
        core_copy(t).wait_send()
        w_copy(t).wait()
    for zo in range(2):
        for d in range(2):
            full_copy(zo, d).wait_send()
    for i in range(3):
        for d in range(2):
            half_copy(i, d).wait_send()
    for t in range(3):
        share_copy(t).wait_send()
    z_copy().wait_send()
    p_copy(6).wait()
    p_copy(7).wait()


def forward(indices, lengths, tables, proj):
    n_f, _, emb = tables.shape
    dma = pltpu.SemaphoreType.DMA
    vmem = pl.BlockSpec(memory_space=pltpu.VMEM)
    hbm = pl.BlockSpec(memory_space=pl.ANY)
    return pl.pallas_call(
        fwd_kernel,
        out_shape=(
            jax.ShapeDtypeStruct((8, n_f, HI, 256), jnp.int32),
            jax.ShapeDtypeStruct((8, n_f, emb, 256), BF16),
            jax.ShapeDtypeStruct((KK, emb, 128), F32),
        ),
        in_specs=[vmem] * 4,
        out_specs=(hbm, hbm, vmem),
        scratch_shapes=[
            pltpu.VMEM((n_f * SUB, KK * SUB), BF16),
            pltpu.VMEM((n_f, emb, 8 * HI), BF16),
            pltpu.VMEM((8, 2, KK, emb, 128), BF16),
            pltpu.VMEM((8, KK, emb, 128), BF16),
            pltpu.VMEM((2, KK, emb, 128), BF16),
            pltpu.VMEM((2, 2, KK, emb, 128), BF16),
            pltpu.VMEM((KK, emb, 128), BF16),
            pltpu.VMEM((3, KK - LOW, emb, 128), BF16),
            pltpu.VMEM((8, n_f, HI, 256), jnp.int32),
            pltpu.VMEM((2, n_f, emb, 256), BF16),
            dma((8,)), dma((8,)), dma((3, 2)), dma((3, 2)), dma((2, 2)), dma((2, 2)), dma, dma, dma((3,)), dma((3,)),
            dma((8,)), dma((2,)),
        ],
        compiler_params=pltpu.CompilerParams(collective_id=0, has_side_effects=True, vmem_limit_bytes=VMEM),
        cost_estimate=pl.CostEstimate(flops=15 * 10**9, bytes_accessed=40 * 10**6, transcendentals=0),
    )(indices, lengths, tables, proj)


def dense_kernel(fac, wh_t, wo_row, dl, logits, grads, dfac, inter):
    n_feat, hid = wh_t.shape
    emb = fac.shape[1]
    step = grads.shape[0] * grads.shape[2]

    def left(i, carry):
        a = fac[i]
        for j in range(K2):
            inter[pl.ds(i * K2 + j, 1), :] = jnp.sum(a * fac[K1 + j], axis=0, keepdims=True)
        return carry

    lax.fori_loop(0, K1, left, 0, unroll=2)
    feat = inter[...].astype(BF16)
    row = dl[...]
    n = row.shape[1]
    d0 = row.astype(BF16)
    r1 = row - d0.astype(F32)
    d1 = r1.astype(BF16)
    d2 = (r1 - d1.astype(F32)).astype(BF16)
    sub = lax.broadcasted_iota(jnp.int32, (n_feat, n), 0)
    d_rows = jnp.where(
        sub == 0, d0.astype(F32), jnp.where(sub == 1, d1.astype(F32), jnp.where(sub == 2, d2.astype(F32), 0.0))
    ).astype(BF16)
    nil = jnp.zeros((n_feat, n), BF16)
    feat_low = jnp.concatenate([feat, nil], axis=0)
    d_high = jnp.concatenate([nil, d_rows], axis=0)
    ones = jnp.ones((8, n), BF16)

    def top(c, carry):
        logit_acc, d_inter = carry
        at = pl.ds(pl.multiple_of(c * step, step), step)
        w = wh_t[:, at]
        v = tn(w, feat)
        wo = jnp.broadcast_to(wo_row[:, at].astype(F32), (8, step))
        top_row = lax.broadcasted_iota(jnp.int32, (8, step), 0) == 0
        wo_cols = tn(jnp.where(top_row, wo, 0.0).astype(BF16), ones)
        s = jax.nn.sigmoid(v)
        hidden = (v * s).astype(BF16)
        logit_acc = logit_acc + jnp.dot(wo.astype(BF16), hidden, preferred_element_type=F32)
        d_hidden = (wo_cols * row * s * (1.0 + v * (1.0 - s))).astype(BF16)
        grad = nt(d_hidden, feat_low) + nt(hidden, d_high)
        grads[:, pl.ds(c, 1), :, :] = grad.astype(BF16).reshape(grads.shape[0], 1, grads.shape[2], 2 * n_feat)
        d_inter = d_inter + jnp.dot(w, d_hidden, preferred_element_type=F32)
        return logit_acc, d_inter

    logit_acc, d_inter = lax.fori_loop(
        0, hid // step, top, (jnp.zeros((8, n), F32), jnp.zeros((n_feat, n), F32)), unroll=2
    )
    logits[...] = logit_acc[0:1]
    inter[...] = d_inter

    def back(eb, carry):
        p = lax.div(eb, emb // SUB // 2)
        rows = pl.ds(pl.multiple_of(eb * SUB, SUB), SUB)
        low = pl.ds(pl.multiple_of(lax.rem(eb, emb // SUB // 2) * SUB, SUB), SUB)
        right = [fac[K1 + j, rows, :] for j in range(K2)]
        d_right = [jnp.zeros((SUB, n), F32) for _ in range(K2)]
        for i in range(K1):
            a = fac[i, rows, :]
            d_left = jnp.zeros((SUB, n), F32)
            for j in range(K2):
                g = inter[pl.ds(i * K2 + j, 1), :]
                d_left = d_left + g * right[j]
                d_right[j] = d_right[j] + g * a
            dfac[p, i, low, :] = d_left.astype(BF16)
        for j in range(K2):
            dfac[p, K1 + j, low, :] = d_right[j].astype(BF16)
        return carry

    lax.fori_loop(0, emb // SUB, back, 0, unroll=2)


def dense(fac, w_hidden, w_out, d_logit):
    hid, feat = w_hidden.shape
    n = d_logit.shape[0]
    return pl.pallas_call(
        dense_kernel,
        out_shape=(
            jax.ShapeDtypeStruct((1, n), F32),
            jax.ShapeDtypeStruct((16, 8, hid // 128, 2 * feat), BF16),
            jax.ShapeDtypeStruct((2, KK, fac.shape[1] // 2, n), BF16),
        ),
        scratch_shapes=[pltpu.VMEM((feat, n), F32)],
        compiler_params=pltpu.CompilerParams(vmem_limit_bytes=VMEM),
        cost_estimate=pl.CostEstimate(flops=10**9, bytes_accessed=10**7, transcendentals=10**6),
    )(fac, w_hidden.T, w_out[None, :], d_logit[None, :])


def bwd_kernel(
    dfac, words, pooled, proj, grads,
    tg_low, tg_high, hid_out, pg_out,
    kron_t, gbuf, acc, dpool, wbuf, pbuf, tbuf, t_half, t_full, t_z, t_share, pg,
    h_core, h_sum, h_half, h_full, h_z, hx_sum, hx_half, hx_full, hx_z, p_x, p_z, p_all,
    own_sem, w_sem, p_sem, core_s, core_r, ici_s, ici_r, half_s, half_r, rest_s, rest_r, ts_s, ts_r, gr_s, gr_r,
    th_s, th_r, tf_s, tf_r, tz_s, tz_r, gz_s, gz_r, gx_s, gx_r, gh_s, gh_r, h_s, h_r, q_s, q_r,
):
    me, core, y, z, other, right, left, across = peers()
    opposite = {"mp": z * 8 + lax.rem(y + 2, 4) * 2 + core}
    rep = lax.axis_index("replica")
    x = lax.rem(rep, 4)
    zl = lax.div(rep, 4)
    x_to = [None] + [{"replica": zl * 4 + lax.rem(x + d, 4)} for d in (1, 2, 3)]
    x_right, x_left = x_to[1], x_to[3]
    z_near = {"replica": (1 - zl) * 4 + x}
    n_f = tbuf.shape[1]
    width = dpool.shape[1]
    places = ((0, 0), (0, 3), (0, 1), (1, 0), (1, 3), (1, 1), (0, 2), (1, 2))
    order = [(p, n) for p in range(2) for n in (0, 1, 2, 3, 6, 4, 5, 7)]
    sends = []
    tg_out = (tg_low, tg_high)

    def go(copy):
        copy.start()
        sends.append(copy)

    def chip(n):
        dz, dy = places[n]
        return lax.rem(z + dz, 2) * 4 + lax.rem(y + dy, 4)

    def block(n):
        return chip(n) * 2 + core

    def to_core(p, n):
        ref = gbuf.at[p, block(n)]
        return remote(ref, ref, core_s.at[p, n], core_r.at[p, n], other)

    def from_core(p, n):
        ref = gbuf.at[p, chip(n) * 2 + 1 - core]
        remote(ref, ref, core_s.at[p, n], core_r.at[p, n], other).wait_recv()

    def whole(p, n, m, device):
        ref = gbuf.at[p, block(n), pl.ds(0, GATHER_LOW[p] if m in (4, 5) else KK)]
        return remote(ref, ref, ici_s.at[p, m], ici_r.at[p, m], device)

    def arrived(p, m):
        whole(p, m, m, right).wait_recv()

    def half(p, n, m, d):
        cut, top = (K1, KK) if m == 6 else ((GATHER_LOW[p] + 1) // 2, GATHER_LOW[p])
        ref = gbuf.at[p, block(n), pl.ds(cut, top - cut) if d else pl.ds(0, cut)]
        i = (p, m - 6, d)
        return remote(ref, ref, half_s.at[i], half_r.at[i], (right, left)[d])

    def rest(p, n):
        ref = gbuf.at[p, block(n), pl.ds(GATHER_LOW[p], KK - GATHER_LOW[p])]
        i = (1, 2, 6).index(n)
        return remote(ref, ref, rest_s.at[p, i], rest_r.at[p, i], across)

    def rest_arrived(p, m):
        ref = gbuf.at[p, block(m), pl.ds(GATHER_LOW[p], KK - GATHER_LOW[p])]
        i = (4, 5, 7).index(m)
        remote(ref, ref, rest_s.at[p, i], rest_r.at[p, i], across).wait_recv()

    def half_arrived(p, m):
        for d in range(2):
            half(p, m, m, d).wait_recv()
        if m == 6:
            go(rest(p, 6))
        else:
            rest_arrived(p, 7)
        go(to_core(p, m))

    def near(p):
        for d in range(2):
            arrived(p, 1 + d)
            go(half(p, 1 + d, 6, d))
            go(rest(p, 1 + d))
            go(to_core(p, 1 + d))
        arrived(p, 3)
        go(whole(p, 3, 4, right))
        go(whole(p, 3, 5, left))
        go(to_core(p, 3))

    def far(p):
        for d in range(2):
            arrived(p, 4 + d)
            go(half(p, 4 + d, 7, d))
        for d in range(2):
            rest_arrived(p, 4 + d)
            go(to_core(p, 4 + d))

    def w_copy(n):
        return pltpu.make_async_copy(words.at[chip(n)], wbuf.at[n], w_sem.at[n])

    def p_copy(i):
        p, n = order[i]
        return pltpu.make_async_copy(
            pooled.at[chip(n), :, pl.ds(p * width, width), :], pbuf.at[i % 2], p_sem.at[i % 2]
        )

    def work(p, n):
        i = order.index((p, n))
        p_copy(i).wait()
        if i + 1 < len(order):
            p_copy(i + 1).start()
        if p == 0:
            w_copy(n).wait()
        from_core(p, n)
        slot = i % 2
        base = chip(n) * 2

        def spread(eb, carry):
            rows = pl.ds(pl.multiple_of(eb * SUB, SUB), SUB)
            g = jnp.concatenate(
                [gbuf[p, base + c, :, rows, :].reshape(KK * SUB, 128) for c in range(2)], axis=1
            )
            d = jnp.dot(kron_t[...], g, preferred_element_type=F32).astype(BF16)
            dpool[:, rows, :] = d.reshape(n_f, SUB, 256)
            pg[...] += nt(pbuf[slot, :, rows, :].reshape(n_f * SUB, 256), g)
            return carry

        lax.fori_loop(0, width // SUB, spread, 0, unroll=8)

        def field(f, carry):
            part = nt(digits(wbuf[n, f]), dpool[f])
            if n == 0:
                acc[f] = part
            elif n == 7:
                tbuf[p, f] = (acc[f] + part).astype(BF16)
            else:
                acc[f] += part
            return carry

        lax.fori_loop(0, n_f, field, 0, unroll=8)

    def first(dx, zo):
        return (lax.rem(zl + 1 + zo, 2) * 4 + lax.rem(x + dx, 4)) * 2

    n_rows = tbuf.shape[2]

    def low(p, zo):
        return pl.ds(0, n_rows if zo else X_FIRST[p])

    def high(p):
        return pl.ds(X_FIRST[p], n_rows - X_FIRST[p])

    def split(p):
        return X_FIRST[p] < n_rows

    def t_half_copy(p, zo, d):
        i = (p, zo, d)
        src = tbuf.at[p, first(2, zo) + d, low(p, zo)]
        return remote(src, t_half.at[p, zo, d, low(p, zo)], th_s.at[i], th_r.at[i], (x_right, x_left)[d])

    def t_full_copy(p, zo, d):
        i = (p, zo, d)
        src = tbuf.at[p, pl.ds(first(1 + 2 * d, zo), 2), low(p, zo)]
        return remote(src, t_full.at[p, zo, d, :, low(p, zo)], tf_s.at[i], tf_r.at[i], (x_right, x_left)[d])

    def t_share_copy(p, i):
        src = tbuf.at[p, pl.ds(first((2, 1, 3)[i], 0), 2), high(p)]
        return remote(src, t_share.at[i], ts_s.at[i], ts_r.at[i], z_near)

    def t_z_copy(p):
        return remote(tbuf.at[p, pl.ds(first(0, 0), 2)], t_z.at[p], tz_s.at[p], tz_r.at[p], z_near)

    def g_x_copy(p, zb, d, dx=0):
        ref = tg_out[p].at[pl.ds(first(dx, 1 - zb), 2), low(p, 1 - zb)]
        i = (p, zb, d)
        return remote(ref, ref, gx_s.at[i], gx_r.at[i], (x_right, x_left)[d])

    def g_z_copy(p, zb):
        ref = tg_out[p].at[pl.ds(first(0, 1 - zb), 2)]
        return remote(ref, ref, gz_s.at[p], gz_r.at[p], z_near)

    def g_half_copy(p, zb, d, dx):
        ref = tg_out[p].at[first(dx, 1 - zb) + d, low(p, 1 - zb)]
        i = (p, zb, d)
        return remote(ref, ref, gh_s.at[i], gh_r.at[i], (x_right, x_left)[d])

    def g_rest_copy(p, zb, i):
        ref = tg_out[p].at[pl.ds(first((3, 1, 2)[i], 1 - zb), 2), high(p)]
        return remote(ref, ref, gr_s.at[i], gr_r.at[i], z_near)

    def t_start(p):
        for zo in range(1 if split(p) else 2):
            for d in range(2):
                go(t_half_copy(p, zo, d))
        if split(p):
            go(t_share_copy(p, 0))

    def take_share(p, i):
        t_share_copy(p, i).wait_recv()
        for k in range(2):
            at = first((2, 1, 3)[i], 1) + k
            tbuf[p, at, high(p)] = (tbuf[p, at, high(p)].astype(F32) + t_share[i, k].astype(F32)).astype(BF16)

    def t_open(p):
        go(t_share_copy(p, 1))
        go(t_share_copy(p, 2))
        take_share(p, 0)
        for d in range(2):
            go(t_half_copy(p, 1, d))

    def t_pass(p, zo):
        for d in range(2):
            t_half_copy(p, zo, d).wait_recv()
            at, rows = first(1 + 2 * d, zo) + d, low(p, zo)
            tbuf[p, at, rows] = (tbuf[p, at, rows].astype(F32) + t_half[p, zo, d, rows].astype(F32)).astype(BF16)
            if zo and split(p):
                take_share(p, 1 + d)
            go(t_full_copy(p, zo, d))

    def t_total(p, zo, k):
        rows = low(p, zo)
        total = tbuf[p, first(0, zo) + k, rows].astype(F32)
        return total + t_full[p, zo, 0, k, rows].astype(F32) + t_full[p, zo, 1, k, rows].astype(F32)

    def t_cross(p):
        for d in range(2):
            t_full_copy(p, 0, d).wait_recv()
        for k in range(2):
            tbuf[p, first(0, 0) + k, low(p, 0)] = t_total(p, 0, k).astype(BF16)
        go(t_z_copy(p))

    def t_finish(p):
        for d in range(2):
            t_full_copy(p, 1, d).wait_recv()
        t_z_copy(p).wait_recv()
        for k in range(2):
            tg_out[p][first(0, 1) + k] = (t_total(p, 1, k) + t_z[p, k].astype(F32)).astype(BF16)
        go(g_z_copy(p, 0))
        for d in range(2):
            go(g_x_copy(p, 0, d))

    def t_spread(p):
        g_z_copy(p, 1).wait_recv()
        for d in range(2):
            go(g_x_copy(p, 1, d))

    def t_relay(p, zb):
        for d in range(2):
            dx = 3 - 2 * d
            g_x_copy(p, zb, d, dx).wait_recv()
            go(g_half_copy(p, zb, d, dx))
            if not zb and split(p):
                go(g_rest_copy(p, 0, d))

    def t_last(p, zb):
        for d in range(2):
            g_half_copy(p, zb, d, 2).wait_recv()
        if split(p):
            if zb:
                for i in range(3):
                    g_rest_copy(p, 1, i).wait_recv()
            else:
                go(g_rest_copy(p, 0, 2))

    def h_copy(i):
        if i == 0:
            src, dst, to = grads.at[:, 1 - core], h_core, other
        elif i < 3:
            d = i - 1
            src, dst, to = h_sum.at[:, lax.rem(y + 2, 4), pl.ds(d * 128, 128)], h_half.at[d], (right, left)[d]
        elif i < 5:
            d = i - 3
            src, dst, to = h_sum.at[:, lax.rem(y + 1 + 2 * d, 4)], h_full.at[d], (right, left)[d]
        elif i == 5:
            src, dst, to = h_sum.at[1 - z, y], h_z, across
        elif i < 8:
            d = i - 6
            src, dst, to = hx_sum.at[:, lax.rem(x + 2, 4), pl.ds(d * 16, 16)], hx_half.at[d], (x_right, x_left)[d]
        elif i < 10:
            d = i - 8
            src, dst, to = hx_sum.at[:, lax.rem(x + 1 + 2 * d, 4)], hx_full.at[d], (x_right, x_left)[d]
        else:
            src, dst, to = hx_sum.at[1 - zl, x], hx_z, z_near
        return remote(src, dst, h_s.at[i], h_r.at[i], to)

    def wide(v):
        return v.astype(F32)

    def h1():
        h_copy(0).wait_recv()
        for q in range(8):
            total = wide(grads[q, core]) + wide(h_core[q])
            h_sum[q // 4, q % 4] = total.astype(BF16).reshape(h_sum.shape[2:])
        go(h_copy(1))
        go(h_copy(2))

    def h2():
        for d in range(2):
            h_copy(1 + d).wait_recv()
            at, rows = lax.rem(y + 1 + 2 * d, 4), pl.ds(d * 128, 128)
            for k in range(2):
                h_sum[k, at, rows] = (wide(h_sum[k, at, rows]) + wide(h_half[d, k])).astype(BF16)
            go(h_copy(3 + d))

    def h3():
        for d in range(2):
            h_copy(3 + d).wait_recv()
        for k in range(2):
            h_sum[k, y] = (wide(h_sum[k, y]) + wide(h_full[0, k]) + wide(h_full[1, k])).astype(BF16)
        go(h_copy(5))

    def h4():
        h_copy(5).wait_recv()
        total = (wide(h_sum[z, y]) + wide(h_z[...])).astype(BF16).reshape(8, 32, 128)
        for q in range(8):
            hx_sum[q // 4, q % 4] = total[q]
        go(h_copy(6))
        go(h_copy(7))

    def h5():
        for d in range(2):
            h_copy(6 + d).wait_recv()
            at, rows = lax.rem(x + 1 + 2 * d, 4), pl.ds(d * 16, 16)
            for k in range(2):
                hx_sum[k, at, rows] = (wide(hx_sum[k, at, rows]) + wide(hx_half[d, k])).astype(BF16)
            go(h_copy(8 + d))

    def h6():
        for d in range(2):
            h_copy(8 + d).wait_recv()
        for k in range(2):
            hx_sum[k, x] = (wide(hx_sum[k, x]) + wide(hx_full[0, k]) + wide(hx_full[1, k])).astype(BF16)
        go(h_copy(10))

    def h7():
        h_copy(10).wait_recv()
        hid_out[...] = wide(hx_sum[zl, x]) + wide(hx_z[...])

    def q_copy(i):
        if i < 3:
            src, dst, to = p_x.at[3], p_x.at[i], x_to[1 + i]
        elif i == 3:
            src, dst, to = p_z.at[0], p_z.at[1], z_near
        elif i == 4:
            ref = p_all.at[z, y, core]
            src, dst, to = ref, ref, other
        elif i < 8:
            ref = p_all.at[z, y]
            src, dst, to = ref, ref, (right, opposite, left)[i - 5]
        else:
            ref = p_all.at[z]
            src, dst, to = ref, ref, across
        return remote(src, dst, q_s.at[i], q_r.at[i], to)

    def q0():
        a = lax.rem(lax.broadcasted_iota(jnp.int32, pg.shape, 0), SUB)
        b = lax.rem(lax.broadcasted_iota(jnp.int32, pg.shape, 1), SUB)
        p_x[3] = jnp.sum(jnp.where(a == b, pg[...], 0.0).reshape(n_f, SUB, KK * SUB), axis=1)
        for i in range(3):
            go(q_copy(i))

    def q1():
        for i in range(3):
            q_copy(i).wait_recv()
        p_z[0] = p_x[0] + p_x[1] + p_x[2] + p_x[3]
        go(q_copy(3))

    def q2():
        q_copy(3).wait_recv()
        p_all[z, y, core] = p_z[0] + p_z[1]
        go(q_copy(4))

    def q3():
        ref = p_all.at[z, y, 1 - core]
        remote(ref, ref, q_s.at[4], q_r.at[4], other).wait_recv()
        for i in range(3):
            go(q_copy(5 + i))

    def q4():
        for i in range(3):
            ref = p_all.at[z, lax.rem(y + 3 - i, 4)]
            remote(ref, ref, q_s.at[5 + i], q_r.at[5 + i], right).wait_recv()
        go(q_copy(8))

    def q5():
        ref = p_all.at[1 - z]
        remote(ref, ref, q_s.at[8], q_r.at[8], across).wait_recv()
        j = 2 * rep + lax.div(me, 8)
        pg_out[...] = p_all[lax.div(j, 8), lax.rem(lax.div(j, 2), 4), lax.rem(j, 2)]

    own = [pltpu.make_async_copy(dfac.at[p], gbuf.at[p, me], own_sem.at[p]) for p in range(2)]
    for c in own:
        c.start()
    p_copy(0).start()
    for _, n in order[:8]:
        w_copy(n).start()
    pg[...] = jnp.zeros_like(pg)
    kron_t[...] = spread_out(proj[pl.ds(pl.multiple_of(me * n_f, n_f), n_f), :], False)
    barrier((other, right, left, opposite, across, x_to[1], x_to[2], x_to[3], z_near))
    own[0].wait()
    for i, to in enumerate((right, left, across)):
        go(whole(0, 0, 1 + i, to))
    go(to_core(0, 0))
    own[1].wait()
    go(to_core(1, 0))
    go(h_copy(0))
    work(0, 0)
    near(0)
    work(0, 1)
    work(0, 2)
    work(0, 3)
    half_arrived(0, 6)
    go(whole(1, 0, 1, right))
    go(whole(1, 0, 2, left))
    work(0, 6)
    far(0)
    go(whole(1, 0, 3, across))
    work(0, 4)
    work(0, 5)
    half_arrived(0, 7)
    work(0, 7)
    t_start(0)
    near(1)
    work(1, 0)
    t_pass(0, 0)
    work(1, 1)
    t_pass(0, 1)
    work(1, 2)
    t_cross(0)
    half_arrived(1, 6)
    work(1, 3)
    far(1)
    t_finish(0)
    work(1, 6)
    half_arrived(1, 7)
    work(1, 4)
    t_spread(0)
    work(1, 5)
    t_relay(0, 0)
    h1()
    work(1, 7)
    t_start(1)
    q0()
    t_open(1)
    t_relay(0, 1)
    h2()
    t_pass(1, 0)
    q1()
    t_pass(1, 1)
    h3()
    q2()
    t_cross(1)
    h4()
    q3()
    t_finish(1)
    h5()
    q4()
    t_spread(1)
    h6()
    t_relay(1, 0)
    t_last(1, 0)
    t_relay(1, 1)
    q5()
    h7()
    t_last(0, 0)
    t_last(0, 1)
    t_last(1, 1)
    for s in sends:
        s.wait_send()


def backward(dfac, words, pooled, proj, grads):
    _, n_f, emb, _ = pooled.shape
    rows = 8 * HI
    width = emb // 2
    n_grad = grads.shape[2]
    grads = grads.reshape(8, 2, 8, n_grad, 128)
    dma = pltpu.SemaphoreType.DMA
    vmem = pl.BlockSpec(memory_space=pltpu.VMEM)
    hbm = pl.BlockSpec(memory_space=pl.ANY)
    a222 = dma((2, 2, 2))
    return pl.pallas_call(
        bwd_kernel,
        out_shape=(
            jax.ShapeDtypeStruct((n_f, rows, width), BF16),
            jax.ShapeDtypeStruct((n_f, rows, width), BF16),
            jax.ShapeDtypeStruct((n_grad, 128), F32),
            jax.ShapeDtypeStruct((n_f, KK * SUB), F32),
        ),
        in_specs=[vmem, hbm, hbm, vmem, vmem],
        out_specs=(vmem, vmem, vmem, vmem),
        scratch_shapes=[
            pltpu.VMEM((n_f * SUB, KK * SUB), BF16),
            pltpu.VMEM((2, 16, KK, width, 128), BF16),
            pltpu.VMEM((n_f, rows, width), F32),
            pltpu.VMEM((n_f, width, 256), BF16),
            pltpu.VMEM((8, n_f, HI, 256), jnp.int32),
            pltpu.VMEM((2, n_f, width, 256), BF16),
            pltpu.VMEM((2, n_f, rows, width), BF16),
            pltpu.VMEM((2, 2, 2, rows, width), BF16),
            pltpu.VMEM((2, 2, 2, 2, rows, width), BF16),
            pltpu.VMEM((2, 2, rows, width), BF16),
            pltpu.VMEM((3, 2, rows - X_FIRST[1], width), BF16),
            pltpu.VMEM((n_f * SUB, KK * SUB), F32),
            pltpu.VMEM((8, 8, n_grad, 128), BF16),
            pltpu.VMEM((2, 4, 8 * n_grad, 128), BF16),
            pltpu.VMEM((2, 2, 4 * n_grad, 128), BF16),
            pltpu.VMEM((2, 2, 8 * n_grad, 128), BF16),
            pltpu.VMEM((8 * n_grad, 128), BF16),
            pltpu.VMEM((2, 4, n_grad, 128), BF16),
            pltpu.VMEM((2, 2, n_grad // 2, 128), BF16),
            pltpu.VMEM((2, 2, n_grad, 128), BF16),
            pltpu.VMEM((n_grad, 128), BF16),
            pltpu.VMEM((4, n_f, KK * SUB), F32),
            pltpu.VMEM((2, n_f, KK * SUB), F32),
            pltpu.VMEM((2, 4, 2, n_f, KK * SUB), F32),
            dma((2,)), dma((8,)), dma((2,)), dma((2, 8)), dma((2, 8)), dma((2, 6)), dma((2, 6)), a222, a222,
            dma((2, 3)), dma((2, 3)), dma((3,)), dma((3,)), dma((3,)), dma((3,)),
            a222, a222, a222, a222, dma((2,)), dma((2,)), dma((2,)), dma((2,)), a222, a222, a222, a222,
            dma((11,)), dma((11,)), dma((9,)), dma((9,)),
        ],
        compiler_params=pltpu.CompilerParams(collective_id=1, has_side_effects=True, vmem_limit_bytes=VMEM),
        cost_estimate=pl.CostEstimate(flops=20 * 10**9, bytes_accessed=40 * 10**6, transcendentals=0),
    )(dfac, words, pooled, proj, grads)


def local(indices, lengths, tables, proj, w_hidden, w_out, d_logit):
    n_f = indices.shape[0]
    me = lax.axis_index("mp")
    words, pooled, fac = forward(indices, lengths, tables, proj)
    logits, grads, dfac = dense(fac, w_hidden, w_out, d_logit)
    low, high, dense_sum, pg = backward(dfac, words, pooled, proj, grads)
    table_grad = jnp.concatenate([low, high], axis=2).astype(F32)
    feat = w_hidden.shape[1]
    mine = proj.shape[0] // 128
    pg = lax.dynamic_slice_in_dim(pg, lax.rem(me * mine, n_f), mine, 0)
    return (
        logits.reshape(-1),
        table_grad,
        dense_sum[:, :feat],
        dense_sum[:, feat : feat + 3].sum(1),
        pg.reshape(mine, KK, SUB).sum(2),
    )


def solution(mesh):
    in_specs = (
        P("mp", None, "replica"),
        P("mp", "replica"),
        P("mp", None, None),
        P(),
        P(),
        P(),
        P(("replica", "mp")),
    )
    out_specs = (
        P(("replica", "mp")),
        P("mp", None, None),
        P(("replica", "mp"), None),
        P(("replica", "mp")),
        P(("replica", "mp"), None),
    )
    return jax.shard_map(local, mesh=mesh, in_specs=in_specs, out_specs=out_specs, check_vma=False)
```

```python
import functools

import jax
import jax.numpy as jnp
from jax import lax
from jax.experimental import pallas as pl
from jax.experimental.pallas import tpu as pltpu
from jax.sharding import PartitionSpec as P

MESH = pl.DeviceIdType.MESH
K1 = 8
K2 = 8
KK = K1 + K2
SUB = 16
HI = 64
BITS = 4
VMEM = 60 * 1024 * 1024
LOW = 9
LOW_HALF = 5
HIGH_HALF = 13
GATHER_LOW = (9, 12)
X_FIRST = (512, 288)
F32 = jnp.float32
BF16 = jnp.bfloat16


def peers():
    me = lax.axis_index("mp")
    core = lax.rem(me, 2)
    y = lax.rem(lax.div(me, 2), 4)
    z = lax.div(me, 8)
    other = {"mp": me + 1 - 2 * core}
    right = {"mp": z * 8 + lax.rem(y + 1, 4) * 2 + core}
    left = {"mp": z * 8 + lax.rem(y + 3, 4) * 2 + core}
    across = {"mp": (1 - z) * 8 + y * 2 + core}
    return me, core, y, z, other, right, left, across


def barrier(devices):
    sem = pltpu.get_barrier_semaphore()
    for d in devices:
        pl.semaphore_signal(sem, inc=1, device_id=d, device_id_type=MESH)
    pl.semaphore_wait(sem, len(devices))


def remote(src, dst, send, recv, device):
    return pltpu.make_async_remote_copy(
        src_ref=src, dst_ref=dst, send_sem=send, recv_sem=recv, device_id=device, device_id_type=MESH
    )


def digits(words):
    return jnp.concatenate(
        [(lax.shift_right_logical(words, BITS * d) & 15).astype(F32).astype(BF16) for d in range(8)], axis=0
    )


def nt(a, b):
    return lax.dot_general(a, b, (((1,), (1,)), ((), ())), preferred_element_type=F32)


def tn(a, b):
    return lax.dot_general(a, b, (((0,), (0,)), ((), ())), preferred_element_type=F32)


def spread_out(here, flip):
    n = here.shape[0] * SUB
    owner = lax.div(lax.broadcasted_iota(jnp.int32, (n, KK), 0), SUB)
    pick = (owner == lax.broadcasted_iota(jnp.int32, (n, KK), 1)).astype(F32).astype(BF16)
    rows = (nt(pick, here) if flip else jnp.dot(pick, here, preferred_element_type=F32)).astype(BF16)
    full = nt(rows, pick)
    a = lax.rem(lax.broadcasted_iota(jnp.int32, (n, n), 0), SUB)
    b = lax.rem(lax.broadcasted_iota(jnp.int32, (n, n), 1), SUB)
    return jnp.where(a == b, full, 0.0).astype(BF16)


def fwd_kernel(
    idx, lens, tab, proj, words_out, pooled_out, fac_out,
    kron, tab_t, sbuf, rcore, rhalf, rfull, rz, rshare, wbuf, pbuf,
    core_s, core_r, half_s, half_r, full_s, full_r, z_s, z_r, share_s, share_r, w_sem, p_sem,
):
    me, core, y, z, other, right, left, across = peers()
    n_f = idx.shape[0]
    emb = tab.shape[2]

    def chunk_of(t):
        early, late = 1 - jnp.minimum(lax.div(t, 2), 1), lax.div(t, 6)
        mid = 1 - early - late
        dy = early * 2 + mid * (1 + 2 * lax.rem(t, 2))
        zo = early * t + mid * lax.div(t - 2 + 2 * early, 2) + late * (t - 6)
        return lax.rem(z + 1 + zo, 2) * 4 + lax.rem(y + dy, 4)

    def p_copy(t):
        slot = lax.rem(t, 2)
        return pltpu.make_async_copy(pbuf.at[slot], pooled_out.at[chunk_of(t)], p_sem.at[slot])

    def w_copy(t):
        return pltpu.make_async_copy(wbuf.at[t], words_out.at[chunk_of(t)], w_sem.at[t])

    def core_copy(t):
        return remote(sbuf.at[t, 1 - core], rcore.at[t], core_s.at[t], core_r.at[t], other)

    def half_range(part, d):
        return ((0, LOW_HALF), (LOW_HALF, LOW), (LOW, HIGH_HALF), (HIGH_HALF, KK))[2 * part + d]

    def half_copy(i, d):
        low, high = half_range(i // 2, d)
        zo, ks = min(i, 1), pl.ds(low, high - low)
        return remote(
            sbuf.at[zo, core, ks], rhalf.at[zo, ks], half_s.at[i, d], half_r.at[i, d], (right, left)[d]
        )

    def full_copy(zo, d):
        ks = pl.ds(0, KK if zo else LOW)
        return remote(
            sbuf.at[2 + 2 * zo + d, core, ks], rfull.at[zo, d, ks], full_s.at[zo, d], full_r.at[zo, d], (right, left)[d]
        )

    def share_copy(i):
        t = (0, 2, 3)[i]
        return remote(sbuf.at[t, core, pl.ds(LOW, KK - LOW)], rshare.at[i], share_s.at[i], share_r.at[i], across)

    def z_copy():
        return remote(sbuf.at[6, core], rz, z_s, z_r, across)

    def compute(t, start=False):
        q = chunk_of(t)
        slot = lax.rem(t, 2)
        where = pl.ds(pl.multiple_of(q * 256, 256), 256)
        if not start:

            @pl.when(t >= 2)
            def _():
                p_copy(t - 2).wait()

        else:
            eye = (
                lax.broadcasted_iota(jnp.int32, (emb, emb), 0) == lax.broadcasted_iota(jnp.int32, (emb, emb), 1)
            ).astype(F32).astype(BF16)

        def field(f, carry):
            ids = idx[f, :, where]
            live = lens[pl.ds(f, 1), where]
            lane_slot = lax.broadcasted_iota(jnp.int32, ids.shape, 0)
            hi = ids & (HI - 1)
            val = jnp.where(lane_slot < live, jnp.left_shift(1, BITS * lax.shift_right_logical(ids, 6)), 0)
            rows = lax.broadcasted_iota(jnp.int32, (HI, 256), 0)
            words = jnp.zeros((HI, 256), jnp.int32)
            for s in range(8):
                words = words + jnp.where(hi[s : s + 1, :] == rows, val[s : s + 1, :], 0)
            wbuf[t, f] = words
            if start:
                table = nt(eye, tab[f]).astype(BF16)
                tab_t[f] = table
            else:
                table = tab_t[f]
            pooled = jnp.dot(table, digits(words), preferred_element_type=F32)
            pbuf[slot, f] = pooled.astype(BF16)
            return carry

        lax.fori_loop(0, n_f, field, 0, unroll=4)
        p_copy(t).start()
        w_copy(t).start()

        def block(eb, carry):
            rows = pl.ds(pl.multiple_of(eb * SUB, SUB), SUB)
            x = pbuf[slot, :, rows, :].reshape(n_f * SUB, 256)
            part = jnp.dot(kron[...], x, preferred_element_type=F32).astype(BF16).reshape(KK, SUB, 256)
            sbuf[t, 0, :, rows, :] = part[:, :, :128]
            sbuf[t, 1, :, rows, :] = part[:, :, 128:]
            return carry

        lax.fori_loop(0, emb // SUB, block, 0, unroll=8)
        if not start:
            core_copy(t).start()

    def add(t, parts, out=None):
        edges = sorted({e for _, _, a, b in parts for e in (a, b)})
        for low, high in zip(edges, edges[1:]):
            refs = [(r, base) for r, base, a, b in parts if a <= low and high <= b]

            def one(k, carry, refs=refs):
                total = sbuf[t, core, k].astype(F32)
                for r, base in refs:
                    total = total + r[k - base].astype(F32)
                if out is None:
                    sbuf[t, core, k] = total.astype(BF16)
                else:
                    out[k] = total
                return carry

            lax.fori_loop(low, high, one, 0)

    def near(t):
        core_copy(t).wait_recv()
        return (rcore.at[t], 0, 0, KK)

    def share(i):
        share_copy(i).wait_recv()
        return (rshare.at[i], LOW, LOW, KK)

    def opposite(zo):
        add(zo, [near(zo)])
        for d in range(2):
            half_copy(zo, d).start()
        if not zo:
            share_copy(0).start()

    def opposite_rest():
        add(1, [share(0)])
        for d in range(2):
            half_copy(2, d).start()

    def side(zo, d):
        t = 2 + 2 * zo + d
        half_copy(zo, d).wait_recv()
        parts = [near(t), (rhalf.at[zo], 0, *half_range(0, d))]
        if zo:
            half_copy(2, d).wait_recv()
            parts += [(rhalf.at[zo], 0, *half_range(1, d)), share(1 + d)]
        add(t, parts)
        full_copy(zo, d).start()
        if not zo:
            share_copy(1 + d).start()

    def own(zo):
        for d in range(2):
            full_copy(zo, d).wait_recv()
        parts = [near(6 + zo)] + [(rfull.at[zo, d], 0, 0, KK if zo else LOW) for d in range(2)]
        if zo:
            z_copy().wait_recv()
            add(7, parts + [(rz, 0, 0, KK)], fac_out)
        else:
            add(6, parts)
            z_copy().start()

    def span(a, b):
        def step(t, carry):
            compute(t)
            return carry

        lax.fori_loop(a, b, step, 0)

    kron[...] = spread_out(proj[pl.ds(pl.multiple_of(me * n_f, n_f), n_f), :], True)
    compute(0, True)
    barrier((other, right, left, across))
    core_copy(0).start()
    opposite(0)
    span(1, 2)
    opposite(1)
    span(2, 3)
    side(0, 0)
    opposite_rest()
    span(3, 4)
    side(0, 1)
    span(4, 7)
    own(0)
    side(1, 0)
    side(1, 1)
    span(7, 8)
    own(1)

    for t in range(8):
        core_copy(t).wait_send()
        w_copy(t).wait()
    for zo in range(2):
        for d in range(2):
            full_copy(zo, d).wait_send()
    for i in range(3):
        for d in range(2):
            half_copy(i, d).wait_send()
    for t in range(3):
        share_copy(t).wait_send()
    z_copy().wait_send()
    p_copy(6).wait()
    p_copy(7).wait()


def forward(indices, lengths, tables, proj):
    n_f, _, emb = tables.shape
    dma = pltpu.SemaphoreType.DMA
    vmem = pl.BlockSpec(memory_space=pltpu.VMEM)
    hbm = pl.BlockSpec(memory_space=pl.ANY)
    return pl.pallas_call(
        fwd_kernel,
        out_shape=(
            jax.ShapeDtypeStruct((8, n_f, HI, 256), jnp.int32),
            jax.ShapeDtypeStruct((8, n_f, emb, 256), BF16),
            jax.ShapeDtypeStruct((KK, emb, 128), F32),
        ),
        in_specs=[vmem] * 4,
        out_specs=(hbm, hbm, vmem),
        scratch_shapes=[
            pltpu.VMEM((n_f * SUB, KK * SUB), BF16),
            pltpu.VMEM((n_f, emb, 8 * HI), BF16),
            pltpu.VMEM((8, 2, KK, emb, 128), BF16),
            pltpu.VMEM((8, KK, emb, 128), BF16),
            pltpu.VMEM((2, KK, emb, 128), BF16),
            pltpu.VMEM((2, 2, KK, emb, 128), BF16),
            pltpu.VMEM((KK, emb, 128), BF16),
            pltpu.VMEM((3, KK - LOW, emb, 128), BF16),
            pltpu.VMEM((8, n_f, HI, 256), jnp.int32),
            pltpu.VMEM((2, n_f, emb, 256), BF16),
            dma((8,)), dma((8,)), dma((3, 2)), dma((3, 2)), dma((2, 2)), dma((2, 2)), dma, dma, dma((3,)), dma((3,)),
            dma((8,)), dma((2,)),
        ],
        compiler_params=pltpu.CompilerParams(collective_id=0, has_side_effects=True, vmem_limit_bytes=VMEM),
        cost_estimate=pl.CostEstimate(flops=15 * 10**9, bytes_accessed=40 * 10**6, transcendentals=0),
    )(indices, lengths, tables, proj)


def dense_kernel(fac, wh_t, wo_row, dl, logits, grads, dfac, inter):
    n_feat, hid = wh_t.shape
    emb = fac.shape[1]
    step = grads.shape[0] * grads.shape[2]

    def left(i, carry):
        a = fac[i]
        for j in range(K2):
            inter[pl.ds(i * K2 + j, 1), :] = jnp.sum(a * fac[K1 + j], axis=0, keepdims=True)
        return carry

    lax.fori_loop(0, K1, left, 0, unroll=2)
    feat = inter[...].astype(BF16)
    row = dl[...]
    n = row.shape[1]
    d0 = row.astype(BF16)
    r1 = row - d0.astype(F32)
    d1 = r1.astype(BF16)
    d2 = (r1 - d1.astype(F32)).astype(BF16)
    sub = lax.broadcasted_iota(jnp.int32, (n_feat, n), 0)
    d_rows = jnp.where(
        sub == 0, d0.astype(F32), jnp.where(sub == 1, d1.astype(F32), jnp.where(sub == 2, d2.astype(F32), 0.0))
    ).astype(BF16)
    nil = jnp.zeros((n_feat, n), BF16)
    feat_low = jnp.concatenate([feat, nil], axis=0)
    d_high = jnp.concatenate([nil, d_rows], axis=0)
    ones = jnp.ones((8, n), BF16)

    def top(c, carry):
        logit_acc, d_inter = carry
        at = pl.ds(pl.multiple_of(c * step, step), step)
        w = wh_t[:, at]
        v = tn(w, feat)
        wo = jnp.broadcast_to(wo_row[:, at].astype(F32), (8, step))
        top_row = lax.broadcasted_iota(jnp.int32, (8, step), 0) == 0
        wo_cols = tn(jnp.where(top_row, wo, 0.0).astype(BF16), ones)
        s = jax.nn.sigmoid(v)
        hidden = (v * s).astype(BF16)
        logit_acc = logit_acc + jnp.dot(wo.astype(BF16), hidden, preferred_element_type=F32)
        d_hidden = (wo_cols * row * s * (1.0 + v * (1.0 - s))).astype(BF16)
        grad = nt(d_hidden, feat_low) + nt(hidden, d_high)
        grads[:, pl.ds(c, 1), :, :] = grad.astype(BF16).reshape(grads.shape[0], 1, grads.shape[2], 2 * n_feat)
        d_inter = d_inter + jnp.dot(w, d_hidden, preferred_element_type=F32)
        return logit_acc, d_inter

    logit_acc, d_inter = lax.fori_loop(
        0, hid // step, top, (jnp.zeros((8, n), F32), jnp.zeros((n_feat, n), F32)), unroll=2
    )
    logits[...] = logit_acc[0:1]
    inter[...] = d_inter

    def back(eb, carry):
        p = lax.div(eb, emb // SUB // 2)
        rows = pl.ds(pl.multiple_of(eb * SUB, SUB), SUB)
        low = pl.ds(pl.multiple_of(lax.rem(eb, emb // SUB // 2) * SUB, SUB), SUB)
        right = [fac[K1 + j, rows, :] for j in range(K2)]
        d_right = [jnp.zeros((SUB, n), F32) for _ in range(K2)]
        for i in range(K1):
            a = fac[i, rows, :]
            d_left = jnp.zeros((SUB, n), F32)
            for j in range(K2):
                g = inter[pl.ds(i * K2 + j, 1), :]
                d_left = d_left + g * right[j]
                d_right[j] = d_right[j] + g * a
            dfac[p, i, low, :] = d_left.astype(BF16)
        for j in range(K2):
            dfac[p, K1 + j, low, :] = d_right[j].astype(BF16)
        return carry

    lax.fori_loop(0, emb // SUB, back, 0, unroll=2)


def dense(fac, w_hidden, w_out, d_logit):
    hid, feat = w_hidden.shape
    n = d_logit.shape[0]
    return pl.pallas_call(
        dense_kernel,
        out_shape=(
            jax.ShapeDtypeStruct((1, n), F32),
            jax.ShapeDtypeStruct((16, 8, hid // 128, 2 * feat), BF16),
            jax.ShapeDtypeStruct((2, KK, fac.shape[1] // 2, n), BF16),
        ),
        scratch_shapes=[pltpu.VMEM((feat, n), F32)],
        compiler_params=pltpu.CompilerParams(vmem_limit_bytes=VMEM),
        cost_estimate=pl.CostEstimate(flops=10**9, bytes_accessed=10**7, transcendentals=10**6),
    )(fac, w_hidden.T, w_out[None, :], d_logit[None, :])


def bwd_kernel(
    dfac, words, pooled, proj, grads,
    tg_low, tg_high, hid_out, pg_out,
    kron_t, gbuf, acc, dpool, wbuf, pbuf, tbuf, t_half, t_full, t_z, t_share, pg,
    h_core, h_sum, h_half, h_full, h_z, hx_sum, hx_half, hx_full, hx_z, p_x, p_z, p_all,
    own_sem, w_sem, p_sem, core_s, core_r, ici_s, ici_r, half_s, half_r, rest_s, rest_r, ts_s, ts_r, gr_s, gr_r,
    th_s, th_r, tf_s, tf_r, tz_s, tz_r, gz_s, gz_r, gx_s, gx_r, gh_s, gh_r, h_s, h_r, q_s, q_r,
):
    me, core, y, z, other, right, left, across = peers()
    opposite = {"mp": z * 8 + lax.rem(y + 2, 4) * 2 + core}
    rep = lax.axis_index("replica")
    x = lax.rem(rep, 4)
    zl = lax.div(rep, 4)
    x_to = [None] + [{"replica": zl * 4 + lax.rem(x + d, 4)} for d in (1, 2, 3)]
    x_right, x_left = x_to[1], x_to[3]
    z_near = {"replica": (1 - zl) * 4 + x}
    n_f = tbuf.shape[1]
    width = dpool.shape[1]
    places = ((0, 0), (0, 3), (0, 1), (1, 0), (1, 3), (1, 1), (0, 2), (1, 2))
    order = [(p, n) for p in range(2) for n in (0, 1, 2, 3, 6, 4, 5, 7)]
    sends = []
    tg_out = (tg_low, tg_high)

    def go(copy):
        copy.start()
        sends.append(copy)

    def chip(n):
        dz, dy = places[n]
        return lax.rem(z + dz, 2) * 4 + lax.rem(y + dy, 4)

    def block(n):
        return chip(n) * 2 + core

    def to_core(p, n):
        ref = gbuf.at[p, block(n)]
        return remote(ref, ref, core_s.at[p, n], core_r.at[p, n], other)

    def from_core(p, n):
        ref = gbuf.at[p, chip(n) * 2 + 1 - core]
        remote(ref, ref, core_s.at[p, n], core_r.at[p, n], other).wait_recv()

    def whole(p, n, m, device):
        ref = gbuf.at[p, block(n), pl.ds(0, GATHER_LOW[p] if m in (4, 5) else KK)]
        return remote(ref, ref, ici_s.at[p, m], ici_r.at[p, m], device)

    def arrived(p, m):
        whole(p, m, m, right).wait_recv()

    def half(p, n, m, d):
        cut, top = (K1, KK) if m == 6 else ((GATHER_LOW[p] + 1) // 2, GATHER_LOW[p])
        ref = gbuf.at[p, block(n), pl.ds(cut, top - cut) if d else pl.ds(0, cut)]
        i = (p, m - 6, d)
        return remote(ref, ref, half_s.at[i], half_r.at[i], (right, left)[d])

    def rest(p, n):
        ref = gbuf.at[p, block(n), pl.ds(GATHER_LOW[p], KK - GATHER_LOW[p])]
        i = (1, 2, 6).index(n)
        return remote(ref, ref, rest_s.at[p, i], rest_r.at[p, i], across)

    def rest_arrived(p, m):
        ref = gbuf.at[p, block(m), pl.ds(GATHER_LOW[p], KK - GATHER_LOW[p])]
        i = (4, 5, 7).index(m)
        remote(ref, ref, rest_s.at[p, i], rest_r.at[p, i], across).wait_recv()

    def half_arrived(p, m):
        for d in range(2):
            half(p, m, m, d).wait_recv()
        if m == 6:
            go(rest(p, 6))
        else:
            rest_arrived(p, 7)
        go(to_core(p, m))

    def near(p):
        for d in range(2):
            arrived(p, 1 + d)
            go(half(p, 1 + d, 6, d))
            go(rest(p, 1 + d))
            go(to_core(p, 1 + d))
        arrived(p, 3)
        go(whole(p, 3, 4, right))
        go(whole(p, 3, 5, left))
        go(to_core(p, 3))

    def far(p):
        for d in range(2):
            arrived(p, 4 + d)
            go(half(p, 4 + d, 7, d))
        for d in range(2):
            rest_arrived(p, 4 + d)
            go(to_core(p, 4 + d))

    def w_copy(n):
        return pltpu.make_async_copy(words.at[chip(n)], wbuf.at[n], w_sem.at[n])

    def p_copy(i):
        p, n = order[i]
        return pltpu.make_async_copy(
            pooled.at[chip(n), :, pl.ds(p * width, width), :], pbuf.at[i % 2], p_sem.at[i % 2]
        )

    def work(p, n):
        i = order.index((p, n))
        p_copy(i).wait()
        if i + 1 < len(order):
            p_copy(i + 1).start()
        if p == 0:
            w_copy(n).wait()
        from_core(p, n)
        slot = i % 2
        base = chip(n) * 2

        def spread(eb, carry):
            rows = pl.ds(pl.multiple_of(eb * SUB, SUB), SUB)
            g = jnp.concatenate(
                [gbuf[p, base + c, :, rows, :].reshape(KK * SUB, 128) for c in range(2)], axis=1
            )
            d = jnp.dot(kron_t[...], g, preferred_element_type=F32).astype(BF16)
            dpool[:, rows, :] = d.reshape(n_f, SUB, 256)
            pg[...] += nt(pbuf[slot, :, rows, :].reshape(n_f * SUB, 256), g)
            return carry

        lax.fori_loop(0, width // SUB, spread, 0, unroll=8)

        def field(f, carry):
            part = nt(digits(wbuf[n, f]), dpool[f])
            if n == 0:
                acc[f] = part
            elif n == 7:
                tbuf[p, f] = (acc[f] + part).astype(BF16)
            else:
                acc[f] += part
            return carry

        lax.fori_loop(0, n_f, field, 0, unroll=4)

    def first(dx, zo):
        return (lax.rem(zl + 1 + zo, 2) * 4 + lax.rem(x + dx, 4)) * 2

    n_rows = tbuf.shape[2]

    def low(p, zo):
        return pl.ds(0, n_rows if zo else X_FIRST[p])

    def high(p):
        return pl.ds(X_FIRST[p], n_rows - X_FIRST[p])

    def split(p):
        return X_FIRST[p] < n_rows

    def t_half_copy(p, zo, d):
        i = (p, zo, d)
        src = tbuf.at[p, first(2, zo) + d, low(p, zo)]
        return remote(src, t_half.at[p, zo, d, low(p, zo)], th_s.at[i], th_r.at[i], (x_right, x_left)[d])

    def t_full_copy(p, zo, d):
        i = (p, zo, d)
        src = tbuf.at[p, pl.ds(first(1 + 2 * d, zo), 2), low(p, zo)]
        return remote(src, t_full.at[p, zo, d, :, low(p, zo)], tf_s.at[i], tf_r.at[i], (x_right, x_left)[d])

    def t_share_copy(p, i):
        src = tbuf.at[p, pl.ds(first((2, 1, 3)[i], 0), 2), high(p)]
        return remote(src, t_share.at[i], ts_s.at[i], ts_r.at[i], z_near)

    def t_z_copy(p):
        return remote(tbuf.at[p, pl.ds(first(0, 0), 2)], t_z.at[p], tz_s.at[p], tz_r.at[p], z_near)

    def g_x_copy(p, zb, d, dx=0):
        ref = tg_out[p].at[pl.ds(first(dx, 1 - zb), 2), low(p, 1 - zb)]
        i = (p, zb, d)
        return remote(ref, ref, gx_s.at[i], gx_r.at[i], (x_right, x_left)[d])

    def g_z_copy(p, zb):
        ref = tg_out[p].at[pl.ds(first(0, 1 - zb), 2)]
        return remote(ref, ref, gz_s.at[p], gz_r.at[p], z_near)

    def g_half_copy(p, zb, d, dx):
        ref = tg_out[p].at[first(dx, 1 - zb) + d, low(p, 1 - zb)]
        i = (p, zb, d)
        return remote(ref, ref, gh_s.at[i], gh_r.at[i], (x_right, x_left)[d])

    def g_rest_copy(p, zb, i):
        ref = tg_out[p].at[pl.ds(first((3, 1, 2)[i], 1 - zb), 2), high(p)]
        return remote(ref, ref, gr_s.at[i], gr_r.at[i], z_near)

    def t_start(p):
        for zo in range(1 if split(p) else 2):
            for d in range(2):
                go(t_half_copy(p, zo, d))
        if split(p):
            go(t_share_copy(p, 0))

    def take_share(p, i):
        t_share_copy(p, i).wait_recv()
        for k in range(2):
            at = first((2, 1, 3)[i], 1) + k
            tbuf[p, at, high(p)] = (tbuf[p, at, high(p)].astype(F32) + t_share[i, k].astype(F32)).astype(BF16)

    def t_open(p):
        go(t_share_copy(p, 1))
        go(t_share_copy(p, 2))
        take_share(p, 0)
        for d in range(2):
            go(t_half_copy(p, 1, d))

    def t_pass(p, zo):
        for d in range(2):
            t_half_copy(p, zo, d).wait_recv()
            at, rows = first(1 + 2 * d, zo) + d, low(p, zo)
            tbuf[p, at, rows] = (tbuf[p, at, rows].astype(F32) + t_half[p, zo, d, rows].astype(F32)).astype(BF16)
            if zo and split(p):
                take_share(p, 1 + d)
            go(t_full_copy(p, zo, d))

    def t_total(p, zo, k):
        rows = low(p, zo)
        total = tbuf[p, first(0, zo) + k, rows].astype(F32)
        return total + t_full[p, zo, 0, k, rows].astype(F32) + t_full[p, zo, 1, k, rows].astype(F32)

    def t_cross(p):
        for d in range(2):
            t_full_copy(p, 0, d).wait_recv()
        for k in range(2):
            tbuf[p, first(0, 0) + k, low(p, 0)] = t_total(p, 0, k).astype(BF16)
        go(t_z_copy(p))

    def t_finish(p):
        for d in range(2):
            t_full_copy(p, 1, d).wait_recv()
        t_z_copy(p).wait_recv()
        for k in range(2):
            tg_out[p][first(0, 1) + k] = (t_total(p, 1, k) + t_z[p, k].astype(F32)).astype(BF16)
        go(g_z_copy(p, 0))
        for d in range(2):
            go(g_x_copy(p, 0, d))

    def t_spread(p):
        g_z_copy(p, 1).wait_recv()
        for d in range(2):
            go(g_x_copy(p, 1, d))

    def t_relay(p, zb):
        for d in range(2):
            dx = 3 - 2 * d
            g_x_copy(p, zb, d, dx).wait_recv()
            go(g_half_copy(p, zb, d, dx))
            if not zb and split(p):
                go(g_rest_copy(p, 0, d))

    def t_last(p, zb):
        for d in range(2):
            g_half_copy(p, zb, d, 2).wait_recv()
        if split(p):
            if zb:
                for i in range(3):
                    g_rest_copy(p, 1, i).wait_recv()
            else:
                go(g_rest_copy(p, 0, 2))

    def h_copy(i):
        if i == 0:
            src, dst, to = grads.at[:, 1 - core], h_core, other
        elif i < 3:
            d = i - 1
            src, dst, to = h_sum.at[:, lax.rem(y + 2, 4), pl.ds(d * 128, 128)], h_half.at[d], (right, left)[d]
        elif i < 5:
            d = i - 3
            src, dst, to = h_sum.at[:, lax.rem(y + 1 + 2 * d, 4)], h_full.at[d], (right, left)[d]
        elif i == 5:
            src, dst, to = h_sum.at[1 - z, y], h_z, across
        elif i < 8:
            d = i - 6
            src, dst, to = hx_sum.at[:, lax.rem(x + 2, 4), pl.ds(d * 16, 16)], hx_half.at[d], (x_right, x_left)[d]
        elif i < 10:
            d = i - 8
            src, dst, to = hx_sum.at[:, lax.rem(x + 1 + 2 * d, 4)], hx_full.at[d], (x_right, x_left)[d]
        else:
            src, dst, to = hx_sum.at[1 - zl, x], hx_z, z_near
        return remote(src, dst, h_s.at[i], h_r.at[i], to)

    def wide(v):
        return v.astype(F32)

    def h1():
        h_copy(0).wait_recv()
        for q in range(8):
            total = wide(grads[q, core]) + wide(h_core[q])
            h_sum[q // 4, q % 4] = total.astype(BF16).reshape(h_sum.shape[2:])
        go(h_copy(1))
        go(h_copy(2))

    def h2():
        for d in range(2):
            h_copy(1 + d).wait_recv()
            at, rows = lax.rem(y + 1 + 2 * d, 4), pl.ds(d * 128, 128)
            for k in range(2):
                h_sum[k, at, rows] = (wide(h_sum[k, at, rows]) + wide(h_half[d, k])).astype(BF16)
            go(h_copy(3 + d))

    def h3():
        for d in range(2):
            h_copy(3 + d).wait_recv()
        for k in range(2):
            h_sum[k, y] = (wide(h_sum[k, y]) + wide(h_full[0, k]) + wide(h_full[1, k])).astype(BF16)
        go(h_copy(5))

    def h4():
        h_copy(5).wait_recv()
        total = (wide(h_sum[z, y]) + wide(h_z[...])).astype(BF16).reshape(8, 32, 128)
        for q in range(8):
            hx_sum[q // 4, q % 4] = total[q]
        go(h_copy(6))
        go(h_copy(7))

    def h5():
        for d in range(2):
            h_copy(6 + d).wait_recv()
            at, rows = lax.rem(x + 1 + 2 * d, 4), pl.ds(d * 16, 16)
            for k in range(2):
                hx_sum[k, at, rows] = (wide(hx_sum[k, at, rows]) + wide(hx_half[d, k])).astype(BF16)
            go(h_copy(8 + d))

    def h6():
        for d in range(2):
            h_copy(8 + d).wait_recv()
        for k in range(2):
            hx_sum[k, x] = (wide(hx_sum[k, x]) + wide(hx_full[0, k]) + wide(hx_full[1, k])).astype(BF16)
        go(h_copy(10))

    def h7():
        h_copy(10).wait_recv()
        hid_out[...] = wide(hx_sum[zl, x]) + wide(hx_z[...])

    def q_copy(i):
        if i < 3:
            src, dst, to = p_x.at[3], p_x.at[i], x_to[1 + i]
        elif i == 3:
            src, dst, to = p_z.at[0], p_z.at[1], z_near
        elif i == 4:
            ref = p_all.at[z, y, core]
            src, dst, to = ref, ref, other
        elif i < 8:
            ref = p_all.at[z, y]
            src, dst, to = ref, ref, (right, opposite, left)[i - 5]
        else:
            ref = p_all.at[z]
            src, dst, to = ref, ref, across
        return remote(src, dst, q_s.at[i], q_r.at[i], to)

    def q0():
        a = lax.rem(lax.broadcasted_iota(jnp.int32, pg.shape, 0), SUB)
        b = lax.rem(lax.broadcasted_iota(jnp.int32, pg.shape, 1), SUB)
        p_x[3] = jnp.sum(jnp.where(a == b, pg[...], 0.0).reshape(n_f, SUB, KK * SUB), axis=1)
        for i in range(3):
            go(q_copy(i))

    def q1():
        for i in range(3):
            q_copy(i).wait_recv()
        p_z[0] = p_x[0] + p_x[1] + p_x[2] + p_x[3]
        go(q_copy(3))

    def q2():
        q_copy(3).wait_recv()
        p_all[z, y, core] = p_z[0] + p_z[1]
        go(q_copy(4))

    def q3():
        ref = p_all.at[z, y, 1 - core]
        remote(ref, ref, q_s.at[4], q_r.at[4], other).wait_recv()
        for i in range(3):
            go(q_copy(5 + i))

    def q4():
        for i in range(3):
            ref = p_all.at[z, lax.rem(y + 3 - i, 4)]
            remote(ref, ref, q_s.at[5 + i], q_r.at[5 + i], right).wait_recv()
        go(q_copy(8))

    def q5():
        ref = p_all.at[1 - z]
        remote(ref, ref, q_s.at[8], q_r.at[8], across).wait_recv()
        j = 2 * rep + lax.div(me, 8)
        pg_out[...] = p_all[lax.div(j, 8), lax.rem(lax.div(j, 2), 4), lax.rem(j, 2)]

    own = [pltpu.make_async_copy(dfac.at[p], gbuf.at[p, me], own_sem.at[p]) for p in range(2)]
    for c in own:
        c.start()
    p_copy(0).start()
    for _, n in order[:8]:
        w_copy(n).start()
    pg[...] = jnp.zeros_like(pg)
    kron_t[...] = spread_out(proj[pl.ds(pl.multiple_of(me * n_f, n_f), n_f), :], False)
    barrier((other, right, left, opposite, across, x_to[1], x_to[2], x_to[3], z_near))
    own[0].wait()
    for i, to in enumerate((right, left, across)):
        go(whole(0, 0, 1 + i, to))
    go(to_core(0, 0))
    own[1].wait()
    go(to_core(1, 0))
    go(h_copy(0))
    work(0, 0)
    near(0)
    work(0, 1)
    work(0, 2)
    work(0, 3)
    half_arrived(0, 6)
    work(0, 6)
    far(0)
    for i, to in enumerate((right, left, across)):
        go(whole(1, 0, 1 + i, to))
    work(0, 4)
    work(0, 5)
    half_arrived(0, 7)
    work(0, 7)
    t_start(0)
    near(1)
    work(1, 0)
    t_pass(0, 0)
    work(1, 1)
    t_pass(0, 1)
    work(1, 2)
    t_cross(0)
    half_arrived(1, 6)
    work(1, 3)
    far(1)
    t_finish(0)
    work(1, 6)
    half_arrived(1, 7)
    work(1, 4)
    t_spread(0)
    work(1, 5)
    t_relay(0, 0)
    h1()
    work(1, 7)
    t_start(1)
    q0()
    t_open(1)
    t_relay(0, 1)
    h2()
    t_pass(1, 0)
    q1()
    t_pass(1, 1)
    h3()
    q2()
    t_cross(1)
    h4()
    q3()
    t_finish(1)
    h5()
    q4()
    t_spread(1)
    h6()
    t_relay(1, 0)
    t_last(1, 0)
    t_relay(1, 1)
    q5()
    h7()
    t_last(0, 0)
    t_last(0, 1)
    t_last(1, 1)
    for s in sends:
        s.wait_send()


def backward(dfac, words, pooled, proj, grads):
    _, n_f, emb, _ = pooled.shape
    rows = 8 * HI
    width = emb // 2
    n_grad = grads.shape[2]
    grads = grads.reshape(8, 2, 8, n_grad, 128)
    dma = pltpu.SemaphoreType.DMA
    vmem = pl.BlockSpec(memory_space=pltpu.VMEM)
    hbm = pl.BlockSpec(memory_space=pl.ANY)
    a222 = dma((2, 2, 2))
    return pl.pallas_call(
        bwd_kernel,
        out_shape=(
            jax.ShapeDtypeStruct((n_f, rows, width), BF16),
            jax.ShapeDtypeStruct((n_f, rows, width), BF16),
            jax.ShapeDtypeStruct((n_grad, 128), F32),
            jax.ShapeDtypeStruct((n_f, KK * SUB), F32),
        ),
        in_specs=[vmem, hbm, hbm, vmem, vmem],
        out_specs=(vmem, vmem, vmem, vmem),
        scratch_shapes=[
            pltpu.VMEM((n_f * SUB, KK * SUB), BF16),
            pltpu.VMEM((2, 16, KK, width, 128), BF16),
            pltpu.VMEM((n_f, rows, width), F32),
            pltpu.VMEM((n_f, width, 256), BF16),
            pltpu.VMEM((8, n_f, HI, 256), jnp.int32),
            pltpu.VMEM((2, n_f, width, 256), BF16),
            pltpu.VMEM((2, n_f, rows, width), BF16),
            pltpu.VMEM((2, 2, 2, rows, width), BF16),
            pltpu.VMEM((2, 2, 2, 2, rows, width), BF16),
            pltpu.VMEM((2, 2, rows, width), BF16),
            pltpu.VMEM((3, 2, rows - X_FIRST[1], width), BF16),
            pltpu.VMEM((n_f * SUB, KK * SUB), F32),
            pltpu.VMEM((8, 8, n_grad, 128), BF16),
            pltpu.VMEM((2, 4, 8 * n_grad, 128), BF16),
            pltpu.VMEM((2, 2, 4 * n_grad, 128), BF16),
            pltpu.VMEM((2, 2, 8 * n_grad, 128), BF16),
            pltpu.VMEM((8 * n_grad, 128), BF16),
            pltpu.VMEM((2, 4, n_grad, 128), BF16),
            pltpu.VMEM((2, 2, n_grad // 2, 128), BF16),
            pltpu.VMEM((2, 2, n_grad, 128), BF16),
            pltpu.VMEM((n_grad, 128), BF16),
            pltpu.VMEM((4, n_f, KK * SUB), F32),
            pltpu.VMEM((2, n_f, KK * SUB), F32),
            pltpu.VMEM((2, 4, 2, n_f, KK * SUB), F32),
            dma((2,)), dma((8,)), dma((2,)), dma((2, 8)), dma((2, 8)), dma((2, 6)), dma((2, 6)), a222, a222,
            dma((2, 3)), dma((2, 3)), dma((3,)), dma((3,)), dma((3,)), dma((3,)),
            a222, a222, a222, a222, dma((2,)), dma((2,)), dma((2,)), dma((2,)), a222, a222, a222, a222,
            dma((11,)), dma((11,)), dma((9,)), dma((9,)),
        ],
        compiler_params=pltpu.CompilerParams(collective_id=1, has_side_effects=True, vmem_limit_bytes=VMEM),
        cost_estimate=pl.CostEstimate(flops=20 * 10**9, bytes_accessed=40 * 10**6, transcendentals=0),
    )(dfac, words, pooled, proj, grads)


def local(indices, lengths, tables, proj, w_hidden, w_out, d_logit):
    n_f = indices.shape[0]
    me = lax.axis_index("mp")
    words, pooled, fac = forward(indices, lengths, tables, proj)
    logits, grads, dfac = dense(fac, w_hidden, w_out, d_logit)
    low, high, dense_sum, pg = backward(dfac, words, pooled, proj, grads)
    table_grad = jnp.concatenate([low, high], axis=2).astype(F32)
    feat = w_hidden.shape[1]
    mine = proj.shape[0] // 128
    pg = lax.dynamic_slice_in_dim(pg, lax.rem(me * mine, n_f), mine, 0)
    return (
        logits.reshape(-1),
        table_grad,
        dense_sum[:, :feat],
        dense_sum[:, feat : feat + 3].sum(1),
        pg.reshape(mine, KK, SUB).sum(2),
    )


def solution(mesh):
    in_specs = (
        P("mp", None, "replica"),
        P("mp", "replica"),
        P("mp", None, None),
        P(),
        P(),
        P(),
        P(("replica", "mp")),
    )
    out_specs = (
        P(("replica", "mp")),
        P("mp", None, None),
        P(("replica", "mp"), None),
        P(("replica", "mp")),
        P(("replica", "mp"), None),
    )
    return jax.shard_map(local, mesh=mesh, in_specs=in_specs, out_specs=out_specs, check_vma=False)
```
